32 devices in a mesh: seq: 16 (over z, y, x), tp: 2 (over core).
Axes of the slice: x: 2, y: 2, z: 4, core: 2. Of those that a mesh axis runs over, the one named last changes fastest.
Arguments:
- prev_hidden: bfloat16 [256, 7168], P('seq', 'tp'), may hold values from -12 to 12
- token_embed: bfloat16 [256, 7168], P('seq', 'tp'), may hold values from -6 to 6
- gain_hidden: float32 [7168], P('tp'), may hold values from 0.25 to 1.75
- gain_embed: float32 [7168], P('tp'), may hold values from 0.25 to 1.75
- gain_final: float32 [7168], P('seq'), may hold values from 0.25 to 1.75
- proj_hidden: bfloat16 [7168, 7168], P('tp', 'seq'), as said below
- proj_embed: bfloat16 [7168, 7168], P('tp', 'seq'), may hold values from -0.046875 to 0.046875
- head: bfloat16 [65536, 7168], P(('seq', 'tp')), as said below
- target_ids: int32 [256], P('seq'), may hold values from 0 to 65535
- valid: int32 [256], P('seq'), may hold values 0 or 1
- rest_count: int32 [1], replicated, may hold values from 1024 to 3839
Outputs:
- grad_prev_hidden: bfloat16 [256, 7168], P('seq', 'tp')
- grad_token_embed: bfloat16 [256, 7168], P('seq', 'tp')
- grad_proj_hidden: bfloat16 [7168, 7168], P('tp', 'seq')
- grad_proj_embed: bfloat16 [7168, 7168], P('tp', 'seq')
- grad_head: bfloat16 [65536, 7168], P(('seq', 'tp'))
The draws below stay inside these ranges and needn't reach their ends.
Inputs may be any that keep to these rules, and one draw needn't show every extreme that they name: `proj_hidden`: weights of the order of one over the square root of 14336. `head`: weights of the order of one over the square root of 796.
All inputs are finite; a program needn't handle non-finite values. No bound on the sum of `valid` on one device may be relied on, other than what follows from the above.
Results may differ from the reference program's by a relative error of at most 0.0071.
Values may be sent and summed in bfloat16 or wider, within the bound.
No kernel may reach another device: no remote copies, remote signals or barrier semaphores. Data moves between devices by JAX's collectives and lax.ppermute only.
A program may use at most 192 MiB of HBM per device.

```python
import math
import jax
import jax.numpy as jnp
import numpy as np
from jax import lax

D = 7168
VOCAB = 65536
TOKENS = 256


def shared_dirs(key):
    inner_key = jax.random.fold_in(key, 7)
    key_in, key_out = jax.random.split(inner_key)
    along_in = jax.random.truncated_normal(key_in, -3.0, 3.0, (D,), jnp.float32)
    along_out = jax.random.truncated_normal(key_out, -3.0, 3.0, (D,), jnp.float32)
    return (along_in, along_out)


def draw_prev_hidden(key, part):
    along_in, along_out = shared_dirs(key)
    key = jax.random.fold_in(key, 11)
    noise_key, row_key = jax.random.split(key)
    noise_part = jax.random.truncated_normal(noise_key, -6.0, 6.0, (TOKENS, D), jnp.float32)
    chosen = jax.random.permutation(row_key, TOKENS)[:8]
    strength = 0.3 * (40.0 / 3.0) ** (jnp.arange(8, dtype=jnp.float32) / 7.0)
    raised = jnp.zeros((TOKENS,), jnp.float32).at[chosen].set(strength)
    values = jnp.clip(noise_part + raised[:, None] * along_in[None, :], -12.0, 12.0)
    return values.astype(jnp.bfloat16)


def draw_proj_hidden(key, part):
    along_in, along_out = shared_dirs(key)
    key = jax.random.fold_in(key, 13)
    spread = (2.0 * D) ** (-0.5)
    noise_part = jax.random.truncated_normal(key, -6.0, 6.0, (D, D), jnp.float32) * spread
    values = noise_part + 2.0 / D * along_in[:, None] * along_out[None, :]
    return values.astype(jnp.bfloat16)


def draw_head(key, part):
    along_in, along_out = shared_dirs(key)
    key = jax.random.fold_in(key, 17)
    noise_key, pick_key, own_key = jax.random.split(key, 3)
    spread = float(D // 9) ** (-0.5)
    noise_part = jax.random.truncated_normal(noise_key, -6.0, 6.0, (VOCAB, D), jnp.float32) * spread
    picked = jax.random.permutation(pick_key, VOCAB)[:6]
    levels = jnp.array([403.3, 400.0, 263.3, 260.0, 163.3, 160.0], jnp.float32) / float(D)
    planted = levels[:, None] * along_out[None, :] + 0.003 * jax.random.normal(own_key, (6, D), jnp.float32)
    values = noise_part.at[picked].set(planted)
    return values.astype(jnp.bfloat16)


def plant(entries, key, low, high):
    longest = entries.shape.index(max(entries.shape))
    spots = []
    for shift in (0, 1):
        where = [jax.random.randint(jax.random.fold_in(key, axis), (), 0, length) for axis, length in enumerate(entries.shape)]
        where[longest] = (where[longest] + shift) % entries.shape[longest]
        spots.append(tuple(where))
    return entries.at[spots[0]].set(low).at[spots[1]].set(high)


def level_of(rng, shape, cuts, least, high):
    level, own = 1.0, jax.random.fold_in(rng, 6)
    for position, shards_of in cuts:
        steps = jnp.exp(jax.random.uniform(jax.random.fold_in(own, position), (shards_of,), jnp.float32, least / len(cuts), high / len(cuts)))
        level = level * jnp.repeat(steps, shape[position] // shards_of).reshape([-1 if axis == position else 1 for axis in range(len(shape))])
    return level


def rank_table(number_of, skew):
    portions = [(1 << 20) // math.isqrt(rank ** skew) + 1 for rank in range(1, number_of + 1)]
    deviation = 1 + sum(portions) // (1 << 30)
    return np.cumsum(np.array([max(1, weight // deviation) for weight in portions]))


def skewed_ids(stream_key, shape, amount, skew):
    table = rank_table(amount, skew)
    pick = jax.random.randint(jax.random.fold_in(stream_key, 1), shape, 0, int(table[amount - 1]))
    grade = jnp.searchsorted(jnp.asarray(table, jnp.int32), pick, side="right")
    return jax.random.permutation(jax.random.fold_in(stream_key, 2), amount)[grade].astype(jnp.int32)


def normal_values(rng, dims, deviation, bound, cuts=(), held_as=jnp.bfloat16):
    loudness = level_of(rng, dims, cuts, -0.22, 0.18) if cuts else 1.0
    result = jax.random.normal(rng, dims, jnp.float32) * deviation * loudness
    return jnp.minimum(jnp.maximum(result, -bound), bound).astype(held_as)


def setup_inputs(seed: int = 0) -> dict:
    keys = jax.random.split(jax.random.key(seed), 12)
    return {
        "prev_hidden": draw_prev_hidden(jax.random.fold_in(keys[11], 71), 0),
        "token_embed": normal_values(keys[1], (TOKENS, D), 1.0, 6.0, ((0, 16), (1, 2))),
        "gain_hidden": jnp.clip(1.0 + 0.15 * jax.random.normal(keys[2], (D,), jnp.float32), 0.25, 1.75),
        "gain_embed": jnp.clip(1.0 + 0.15 * jax.random.normal(keys[3], (D,), jnp.float32), 0.25, 1.75),
        "gain_final": jnp.clip(1.0 + 0.15 * jax.random.normal(keys[4], (D,), jnp.float32), 0.25, 1.75),
        "proj_hidden": draw_proj_hidden(jax.random.fold_in(keys[11], 71), 0),
        "proj_embed": normal_values(keys[6], (D, D), (2 * D) ** -0.5, 0.046875, ((0, 2), (1, 16))),
        "head": draw_head(jax.random.fold_in(keys[11], 71), 0),
        "target_ids": plant(skewed_ids(keys[8], (TOKENS,), VOCAB, 2), jax.random.fold_in(keys[8], 3), 0, VOCAB - 1).astype(jnp.int32),
        "valid": plant((jax.random.randint(keys[9], (TOKENS,), 0, 8) < 7).astype(jnp.int32), jax.random.fold_in(keys[9], 1), 0, 1),
        "rest_count": jax.random.randint(keys[10], (1,), 4 * TOKENS, 15 * TOKENS).astype(jnp.int32),
    }


loss_scale = 4096.0
epsilon = 1e-06

def row_scale(values):
    return lax.rsqrt(lax.optimization_barrier(jnp.mean(values * values, axis=-1, keepdims=True)) + epsilon)

def norm_back(grad_out, values, scale):
    return scale * grad_out - values * scale ** 3 * lax.optimization_barrier(jnp.mean(grad_out * values, axis=-1, keepdims=True))

def reference(prev_hidden, token_embed, gain_hidden, gain_embed, gain_final, proj_hidden, proj_embed, head, target_ids, valid, rest_count):
    prev_f = prev_hidden.astype(jnp.float32)
    embed_f = token_embed.astype(jnp.float32)
    shifted = jnp.concatenate([embed_f[1:], jnp.zeros((1, D), jnp.float32)], axis=0)
    scale_prev = row_scale(prev_f)
    scale_embed = row_scale(shifted)
    normed_prev = (prev_f * scale_prev * gain_hidden).astype(jnp.bfloat16)
    normed_embed = (shifted * scale_embed * gain_embed).astype(jnp.bfloat16)
    mixed = (jnp.dot(normed_prev, proj_hidden, preferred_element_type=jnp.float32) + jnp.dot(normed_embed, proj_embed, preferred_element_type=jnp.float32)).astype(jnp.bfloat16)
    mixed_f = mixed.astype(jnp.float32)
    scale_final = row_scale(mixed_f)
    final = (mixed_f * scale_final * gain_final).astype(jnp.bfloat16)
    logits = jnp.dot(final, head.T, preferred_element_type=jnp.float32)
    row_top = lax.optimization_barrier(jnp.max(logits, axis=-1, keepdims=True))
    expd = jnp.exp(logits - row_top)
    probs = expd / lax.optimization_barrier(jnp.sum(expd, axis=-1, keepdims=True))
    onehot = (jnp.arange(VOCAB, dtype=jnp.int32)[None, :] == target_ids[:, None]).astype(jnp.float32)
    count = jnp.sum(valid).astype(jnp.float32) + rest_count[0].astype(jnp.float32)
    coef = loss_scale * valid.astype(jnp.float32) / count
    dlogits = (coef[:, None] * (probs - onehot)).astype(jnp.bfloat16)
    grad_head = jnp.dot(dlogits.T, final, preferred_element_type=jnp.float32).astype(jnp.bfloat16)
    dfinal = jnp.dot(dlogits, head, preferred_element_type=jnp.float32)
    dmixed = norm_back(dfinal * gain_final, mixed_f, scale_final).astype(jnp.bfloat16)
    grad_proj_hidden = jnp.dot(normed_prev.T, dmixed, preferred_element_type=jnp.float32).astype(jnp.bfloat16)
    grad_proj_embed = jnp.dot(normed_embed.T, dmixed, preferred_element_type=jnp.float32).astype(jnp.bfloat16)
    dnormed_prev = jnp.dot(dmixed, proj_hidden.T, preferred_element_type=jnp.float32)
    dnormed_embed = jnp.dot(dmixed, proj_embed.T, preferred_element_type=jnp.float32)
    grad_prev_hidden = norm_back(dnormed_prev * gain_hidden, prev_f, scale_prev).astype(jnp.bfloat16)
    dshifted = norm_back(dnormed_embed * gain_embed, shifted, scale_embed)
    grad_token_embed = jnp.concatenate([jnp.zeros((1, D), jnp.float32), dshifted[:-1]], axis=0).astype(jnp.bfloat16)
    return (grad_prev_hidden, grad_token_embed, grad_proj_hidden, grad_proj_embed, grad_head)
```

```python
import jax
import jax.numpy as jnp
from jax import lax
from jax.sharding import PartitionSpec as P

D = 7168


loss_scale = 4096.0
epsilon = 1e-06

f32 = jnp.float32
bf16 = jnp.bfloat16


def swap(array, axis, bit):
    count = lax.axis_size(axis)
    return lax.ppermute(array, axis, [(i, i ^ (1 << bit)) for i in range(count)])


def bits_of(axis):
    return lax.axis_size(axis).bit_length() - 1


def place_of(axis, bit):
    return (lax.axis_index(axis) >> bit) & 1


def gather(array, axis, order):
    count = bits_of(axis)
    array = array.reshape((1,) * count + array.shape)
    for bit in order:
        dim = count - 1 - bit
        other = swap(array, axis, bit)
        array = jnp.where(
            place_of(axis, bit) == 0,
            jnp.concatenate([array, other], axis=dim),
            jnp.concatenate([other, array], axis=dim),
        )
    return array.reshape((1 << count,) + array.shape[count:])


def scatter(array, axis, order):
    count = bits_of(axis)
    array = array.reshape((2,) * count + array.shape[1:])
    for bit in order:
        dim = count - 1 - bit
        mine = place_of(axis, bit)
        sent = lax.dynamic_index_in_dim(array, 1 - mine, dim).astype(bf16)
        kept = lax.dynamic_index_in_dim(array, mine, dim).astype(f32)
        array = kept + swap(sent, axis, bit).astype(f32)
    return array.reshape(array.shape[count:])


def gather_lanes(array, axis):
    for bit in range(bits_of(axis)):
        other = swap(array, axis, bit)
        array = jnp.where(
            place_of(axis, bit) == 0,
            jnp.concatenate([array, other], axis=-1),
            jnp.concatenate([other, array], axis=-1),
        )
    return array


def scatter_lanes(array, axis, sent_as):
    for bit in reversed(range(bits_of(axis))):
        half = array.shape[-1] // 2
        mine = place_of(axis, bit)
        sent = lax.dynamic_slice_in_dim(array, (1 - mine) * half, half, -1).astype(sent_as)
        kept = lax.dynamic_slice_in_dim(array, mine * half, half, -1)
        array = kept + swap(sent, axis, bit).astype(f32)
    return array


def in_parts(values):
    high = lax.reduce_precision(values, 8, 7)
    middle = lax.reduce_precision(values - high, 8, 7)
    return high, middle, values - high - middle


def dot(left, right, on_left, on_right):
    return lax.dot_general(
        left, right, (((on_left,), (on_right,)), ((), ())), preferred_element_type=f32
    )


def shards(
    prev_hidden,
    token_embed,
    gain_hidden,
    gain_embed,
    gain_final,
    proj_hidden,
    proj_embed,
    head,
    target_ids,
    valid,
    rest_count,
):
    seq_bits = bits_of("seq")
    down = list(reversed(range(seq_bits)))
    down_crossed = down[:-2] + [0, 1]
    up, up_crossed = down[::-1], down_crossed[::-1]
    width = prev_hidden.shape[1]
    features = proj_hidden.shape[1]

    prev_f = prev_hidden.astype(f32)
    embed_f = token_embed.astype(f32)
    sums = lax.psum(
        jnp.stack([jnp.sum(prev_f * prev_f, axis=-1), jnp.sum(embed_f * embed_f, axis=-1)]), "tp"
    )
    scales = lax.rsqrt(sums / D + epsilon)
    scale_prev, scale_embed = scales[0][:, None], scales[1][:, None]
    normed_prev = (prev_f * scale_prev * gain_hidden).astype(bf16)
    normed_embed = (embed_f * scale_embed * gain_embed).astype(bf16)
    facts = jnp.stack([target_ids // 256, target_ids % 256, valid], axis=1).astype(bf16)
    facts = jnp.pad(facts, ((0, 0), (0, 125)))

    prev_all = gather(jnp.concatenate([normed_prev, facts], axis=1), "seq", down)
    embed_all = gather(normed_embed, "seq", down_crossed)
    prev_all = prev_all.reshape(-1, width + 128)
    embed_all = embed_all.reshape(-1, width)
    facts_all = prev_all[:, width:].astype(f32)
    prev_all = prev_all[:, :width]
    tokens = prev_all.shape[0]
    ids_all = (facts_all[:, 0] * 256 + facts_all[:, 1]).astype(jnp.int32)
    valid_all = facts_all[:, 2]

    from_prev = dot(proj_hidden, prev_all, 0, 1)
    from_embed = dot(proj_embed, embed_all, 0, 1)
    partial_value = from_prev + jnp.pad(from_embed[:, 1:], ((0, 0), (0, 1)))
    mixed_f = scatter_lanes(partial_value, "tp", f32).astype(bf16).astype(f32)
    scaled = (mixed_f * gain_final[:, None]).astype(bf16)
    square_parts = jnp.stack(in_parts(jnp.sum(mixed_f * mixed_f, axis=0))).astype(bf16)
    square_parts = jnp.pad(square_parts, ((0, 13), (0, 0)))
    cut = features // 2
    first = gather(jnp.concatenate([scaled[:cut], square_parts], axis=0), "seq", down)
    second = gather(scaled[cut:], "seq", down_crossed)
    scaled_all = jnp.concatenate([first[:, :cut], second], axis=1)
    squares = jnp.sum(first[:, cut : cut + 3].astype(f32), axis=(0, 1))
    scaled_all = gather_lanes(scaled_all.reshape(D, -1), "tp")
    scale_own = lax.rsqrt(squares / D + epsilon)
    scale_final = gather_lanes(scale_own, "tp")

    logits = dot(head, scaled_all, 1, 0) * scale_final
    vocab_rows = head.shape[0]
    vocab_start = lax.axis_index(("seq", "tp")) * vocab_rows
    entries = lax.broadcasted_iota(jnp.int32, (vocab_rows, 1), 0) + vocab_start
    onehot = entries == ids_all
    top = jnp.max(logits, axis=0)
    expd = jnp.exp(logits - top)
    stats = jnp.stack(
        [
            top,
            jnp.sum(expd, axis=0),
            jnp.sum(expd * logits, axis=0),
            jnp.sum(jnp.where(onehot, logits, 0.0), axis=0),
        ]
    )
    stats_all = lax.all_gather(stats, ("seq", "tp"), axis=0)
    tops = stats_all[:, 0]
    row_top = jnp.max(tops, axis=0)
    shares = jnp.exp(tops - row_top)
    row_total = jnp.sum(shares * stats_all[:, 1], axis=0)
    mean_logit = jnp.sum(shares * stats_all[:, 2], axis=0) / row_total
    target_logit = jnp.sum(stats_all[:, 3], axis=0)
    count = jnp.sum(valid_all) + rest_count[0].astype(f32)
    coef = loss_scale * valid_all / count
    share = jnp.exp(top - row_top) / row_total
    dlogits_f = coef * (expd * share - onehot.astype(f32))
    dlogits = dlogits_f.astype(bf16)
    total_dot = coef * (mean_logit - target_logit) / scale_final

    dfinal_part = dot(head, dlogits, 0, 0)
    dfinal_part = scatter_lanes(dfinal_part, "tp", bf16)
    dfinal_part = dfinal_part.reshape((-1, features) + dfinal_part.shape[1:])
    dfinal = jnp.concatenate(
        [
            scatter(dfinal_part[:, :cut], "seq", up),
            scatter(dfinal_part[:, cut:], "seq", up_crossed),
        ],
        axis=0,
    )
    grad_head = dot((dlogits_f * scale_final).astype(bf16), scaled_all, 1, 1).astype(bf16)

    own = dfinal.shape[1]
    dot_own = lax.dynamic_slice_in_dim(total_dot, lax.axis_index("tp") * own, own)
    dmixed = (
        scale_own * (dfinal * gain_final[:, None]) - mixed_f * (scale_own**3 * (dot_own / D))
    ).astype(bf16)
    dmixed = gather_lanes(dmixed, "tp")
    dmixed_late = jnp.pad(dmixed[:, :-1], ((0, 0), (1, 0)))
    blocks = (-1, prev_hidden.shape[0], width)
    grad_prev = scatter(dot(dmixed, proj_hidden, 0, 1).reshape(blocks), "seq", up)
    grad_embed = scatter(dot(dmixed_late, proj_embed, 0, 1).reshape(blocks), "seq", up_crossed)
    grad_proj_hidden = dot(prev_all, dmixed, 0, 1).astype(bf16)
    grad_proj_embed = dot(embed_all, dmixed_late, 0, 1).astype(bf16)
    grad_prev = grad_prev * gain_hidden
    grad_embed = grad_embed * gain_embed
    dots = lax.psum(
        jnp.stack([jnp.sum(grad_prev * prev_f, axis=-1), jnp.sum(grad_embed * embed_f, axis=-1)]),
        "tp",
    )
    grad_prev_hidden = (
        scale_prev * grad_prev - prev_f * (scale_prev**3 * (dots[0] / D)[:, None])
    ).astype(bf16)
    grad_token_embed = (
        scale_embed * grad_embed - embed_f * (scale_embed**3 * (dots[1] / D)[:, None])
    ).astype(bf16)
    return (grad_prev_hidden, grad_token_embed, grad_proj_hidden, grad_proj_embed, grad_head)


def solution(mesh):
    return jax.shard_map(
        shards,
        mesh=mesh,
        in_specs=(
            P("seq", "tp"),
            P("seq", "tp"),
            P("tp"),
            P("tp"),
            P("seq"),
            P("tp", "seq"),
            P("tp", "seq"),
            P(("seq", "tp"), None),
            P("seq"),
            P("seq"),
            P(),
        ),
        out_specs=(
            P("seq", "tp"),
            P("seq", "tp"),
            P("tp", "seq"),
            P("tp", "seq"),
            P(("seq", "tp"), None),
        ),
        check_vma=False,
    )
```

```python
import jax
import jax.numpy as jnp
from jax import lax
from jax.sharding import PartitionSpec as P

D = 7168


loss_scale = 4096.0
epsilon = 1e-06

f32 = jnp.float32
bf16 = jnp.bfloat16


def swap(array, axis, bit):
    count = lax.axis_size(axis)
    return lax.ppermute(array, axis, [(i, i ^ (1 << bit)) for i in range(count)])


def bits_of(axis):
    return lax.axis_size(axis).bit_length() - 1


def place_of(axis, bit):
    return (lax.axis_index(axis) >> bit) & 1


def gather(array, axis, order):
    count = bits_of(axis)
    array = array.reshape((1,) * count + array.shape)
    for bit in order:
        dim = count - 1 - bit
        other = swap(array, axis, bit)
        array = jnp.where(
            place_of(axis, bit) == 0,
            jnp.concatenate([array, other], axis=dim),
            jnp.concatenate([other, array], axis=dim),
        )
    return array.reshape((1 << count,) + array.shape[count:])


def scatter(arrays, axis, orders, beside=None):
    count = bits_of(axis)
    arrays = [array.reshape((2,) * count + array.shape[1:]) for array in arrays]
    done = None
    for step in range(count):
        places = [(count - 1 - order[step], place_of(axis, order[step])) for order in orders]
        sent = [
            lax.dynamic_index_in_dim(array, 1 - mine, dim).astype(bf16)
            for array, (dim, mine) in zip(arrays, places)
        ]
        if step == 0 and beside is not None:
            work, argument = beside
            argument, *sent = lax.optimization_barrier((argument, *sent))
        came = [swap(array, axis, order[step]) for array, order in zip(sent, orders)]
        if step == 0 and beside is not None:
            done, *came = lax.optimization_barrier((work(argument), *came))
        arrays = [
            lax.dynamic_index_in_dim(array, mine, dim).astype(f32) + other.astype(f32)
            for array, other, (dim, mine) in zip(arrays, came, places)
        ]
    return [array.reshape(array.shape[count:]) for array in arrays], done


def orders_of(axis):
    down = list(reversed(range(bits_of(axis))))
    return [down, down[:-2] + [0, 1], [0, 1] + down[:-2]]


def cut_in_three(size, unit):
    third = round(0.25 * size / unit) * unit
    first = (size - third + unit) // (2 * unit) * unit
    return first, size - third


def merged(group):
    tops, totals, weighted, targets = (jnp.stack([one[i] for one in group]) for i in range(4))
    top = jnp.max(tops, axis=0)
    shares = jnp.exp(tops - top)
    return jnp.stack(
        [
            top,
            jnp.sum(shares * totals, axis=0),
            jnp.sum(shares * weighted, axis=0),
            jnp.sum(targets, axis=0),
        ]
    )


def over_all(stats, axis):
    size = lax.axis_size(axis)
    step = 1
    while step < size:
        masks = [step * k for k in range(1, min(4, size // step))]
        group = [stats] + [
            lax.ppermute(stats, axis, [(i, i ^ mask) for i in range(size)]) for mask in masks
        ]
        stats = merged(group)
        step *= len(group)
    return stats


def gather_lanes(array, axis):
    for bit in range(bits_of(axis)):
        other = swap(array, axis, bit)
        array = jnp.where(
            place_of(axis, bit) == 0,
            jnp.concatenate([array, other], axis=-1),
            jnp.concatenate([other, array], axis=-1),
        )
    return array


def scatter_lanes(array, axis, sent_as):
    for bit in reversed(range(bits_of(axis))):
        half = array.shape[-1] // 2
        mine = place_of(axis, bit)
        sent = lax.dynamic_slice_in_dim(array, (1 - mine) * half, half, -1).astype(sent_as)
        kept = lax.dynamic_slice_in_dim(array, mine * half, half, -1)
        array = kept + swap(sent, axis, bit).astype(f32)
    return array


def in_parts(values):
    high = lax.reduce_precision(values, 8, 7)
    middle = lax.reduce_precision(values - high, 8, 7)
    return high, middle, values - high - middle


def dot(left, right, on_left, on_right):
    return lax.dot_general(
        left, right, (((on_left,), (on_right,)), ((), ())), preferred_element_type=f32
    )


def shards(
    prev_hidden,
    token_embed,
    gain_hidden,
    gain_embed,
    gain_final,
    proj_hidden,
    proj_embed,
    head,
    target_ids,
    valid,
    rest_count,
):
    down = orders_of("seq")
    up = [order[::-1] for order in down]
    width = prev_hidden.shape[1]
    features = proj_hidden.shape[1]

    prev_f = prev_hidden.astype(f32)
    embed_f = token_embed.astype(f32)
    sums = lax.psum(
        jnp.stack([jnp.sum(prev_f * prev_f, axis=-1), jnp.sum(embed_f * embed_f, axis=-1)]), "tp"
    )
    scales = lax.rsqrt(sums / D + epsilon)
    scale_prev, scale_embed = scales[0][:, None], scales[1][:, None]
    normed_prev = (prev_f * scale_prev * gain_hidden).astype(bf16)
    normed_embed = (embed_f * scale_embed * gain_embed).astype(bf16)
    facts = jnp.stack([target_ids // 256, target_ids % 256, valid], axis=1).astype(bf16)
    facts = jnp.pad(facts, ((0, 0), (0, 125)))

    main = round(0.75 * width / 128) * 128
    rest = width - main
    first, second, third = (
        gather(part, "seq", order)
        for part, order in zip(
            (
                normed_prev[:, :main],
                normed_embed[:, :main],
                jnp.concatenate([normed_prev[:, main:], normed_embed[:, main:], facts], axis=1),
            ),
            down,
        )
    )
    first, second = first.reshape(-1, main), second.reshape(-1, main)
    third = third.reshape(-1, 2 * rest + 128)
    prev_all = jnp.concatenate([first, third[:, :rest]], axis=1)
    embed_all = jnp.concatenate([second, third[:, rest : 2 * rest]], axis=1)
    facts_all = third[:, 2 * rest :].astype(f32)
    ids_all = (facts_all[:, 0] * 256 + facts_all[:, 1]).astype(jnp.int32)
    valid_all = facts_all[:, 2]

    from_prev = dot(proj_hidden, prev_all, 0, 1)
    from_embed = dot(proj_embed, embed_all, 0, 1)
    partial_value = from_prev + jnp.pad(from_embed[:, 1:], ((0, 0), (0, 1)))
    mixed_f = scatter_lanes(partial_value, "tp", f32).astype(bf16).astype(f32)
    scaled = (mixed_f * gain_final[:, None]).astype(bf16)
    square_parts = jnp.stack(in_parts(jnp.sum(mixed_f * mixed_f, axis=0))).astype(bf16)
    square_parts = jnp.pad(square_parts, ((0, 13), (0, 0)))
    one, two = cut_in_three(features, 16)
    first, second, third = (
        gather(part, "seq", order)
        for part, order in zip(
            (scaled[:one], scaled[one:two], jnp.concatenate([scaled[two:], square_parts], axis=0)),
            down,
        )
    )
    scaled_all = jnp.concatenate([first, second, third[:, : features - two]], axis=1)
    squares = jnp.sum(third[:, features - two :][:, :3].astype(f32), axis=(0, 1))
    scaled_all = gather_lanes(scaled_all.reshape(D, -1), "tp")
    scale_own = lax.rsqrt(squares / D + epsilon)
    scale_final = gather_lanes(scale_own, "tp")

    logits = dot(head, scaled_all, 1, 0) * scale_final
    vocab_rows = head.shape[0]
    vocab_start = lax.axis_index(("seq", "tp")) * vocab_rows
    entries = lax.broadcasted_iota(jnp.int32, (vocab_rows, 1), 0) + vocab_start
    onehot = entries == ids_all
    top = jnp.max(logits, axis=0)
    expd = jnp.exp(logits - top)
    stats = jnp.stack(
        [
            top,
            jnp.sum(expd, axis=0),
            jnp.sum(expd * logits, axis=0),
            jnp.sum(jnp.where(onehot, logits, 0.0), axis=0),
        ]
    )
    row_top, row_total, row_weighted, target_logit = over_all(over_all(stats, "seq"), "tp")
    mean_logit = row_weighted / row_total
    count = jnp.sum(valid_all) + rest_count[0].astype(f32)
    coef = loss_scale * valid_all / count
    share = jnp.exp(top - row_top) / row_total
    dlogits_f = coef * (expd * share - onehot.astype(f32))
    dlogits = dlogits_f.astype(bf16)
    total_dot = coef * (mean_logit - target_logit) / scale_final

    dfinal_part = dot(head, dlogits, 0, 0)
    dfinal_part = scatter_lanes(dfinal_part, "tp", bf16)
    dfinal_part = dfinal_part.reshape((-1, features) + dfinal_part.shape[1:])
    pieces, _ = scatter(
        [dfinal_part[:, :one], dfinal_part[:, one:two], dfinal_part[:, two:]], "seq", up
    )
    dfinal = jnp.concatenate(pieces, axis=0)

    own = dfinal.shape[1]
    dot_own = lax.dynamic_slice_in_dim(total_dot, lax.axis_index("tp") * own, own)
    dmixed = (
        scale_own * (dfinal * gain_final[:, None]) - mixed_f * (scale_own**3 * (dot_own / D))
    ).astype(bf16)
    dmixed = gather_lanes(dmixed, "tp")
    dmixed_late = jnp.pad(dmixed[:, :-1], ((0, 0), (1, 0)))
    rows = prev_hidden.shape[0]
    back_prev = dot(dmixed, proj_hidden, 0, 1).reshape(-1, rows, width)
    back_embed = dot(dmixed_late, proj_embed, 0, 1).reshape(-1, rows, width)
    (first, second, third), grad_head = scatter(
        [
            back_prev[..., :main],
            back_embed[..., :main],
            jnp.concatenate([back_prev[..., main:], back_embed[..., main:]], axis=-1),
        ],
        "seq",
        up,
        (
            lambda left: dot(left, scaled_all, 1, 1).astype(bf16),
            (dlogits_f * scale_final).astype(bf16),
        ),
    )
    grad_prev = jnp.concatenate([first, third[:, :rest]], axis=1)
    grad_embed = jnp.concatenate([second, third[:, rest:]], axis=1)
    grad_proj_hidden = dot(prev_all, dmixed, 0, 1).astype(bf16)
    grad_proj_embed = dot(embed_all, dmixed_late, 0, 1).astype(bf16)
    grad_prev = grad_prev * gain_hidden
    grad_embed = grad_embed * gain_embed
    dots = lax.psum(
        jnp.stack([jnp.sum(grad_prev * prev_f, axis=-1), jnp.sum(grad_embed * embed_f, axis=-1)]),
        "tp",
    )
    grad_prev_hidden = (
        scale_prev * grad_prev - prev_f * (scale_prev**3 * (dots[0] / D)[:, None])
    ).astype(bf16)
    grad_token_embed = (
        scale_embed * grad_embed - embed_f * (scale_embed**3 * (dots[1] / D)[:, None])
    ).astype(bf16)
    return (grad_prev_hidden, grad_token_embed, grad_proj_hidden, grad_proj_embed, grad_head)


def solution(mesh):
    return jax.shard_map(
        shards,
        mesh=mesh,
        in_specs=(
            P("seq", "tp"),
            P("seq", "tp"),
            P("tp"),
            P("tp"),
            P("seq"),
            P("tp", "seq"),
            P("tp", "seq"),
            P(("seq", "tp"), None),
            P("seq"),
            P("seq"),
            P(),
        ),
        out_specs=(
            P("seq", "tp"),
            P("seq", "tp"),
            P("tp", "seq"),
            P("tp", "seq"),
            P(("seq", "tp"), None),
        ),
        check_vma=False,
    )
```

```python
import functools

import jax
import jax.numpy as jnp
from jax import lax
from jax.experimental import pallas as pl
from jax.experimental.pallas import tpu as pltpu
from jax.sharding import PartitionSpec as P

D = 7168


loss_scale = 4096.0
epsilon = 1e-06

f32 = jnp.float32
bf16 = jnp.bfloat16
i32 = jnp.int32


def from_partner(array, axis, mask):
    size = lax.axis_size(axis)
    return lax.ppermute(array, axis, [(i, i ^ mask) for i in range(size)])


def plane_and_line():
    size = lax.axis_size("seq")
    plane = min(4, size)
    return list(range(plane)), list(range(0, size, plane))


def fetch(array, masks):
    return jnp.stack([array if mask == 0 else from_partner(array, "seq", mask) for mask in masks])


def gather_line_first(array):
    plane, line = plane_and_line()
    return fetch(fetch(array, line), plane)


def gather_plane_first(array):
    plane, line = plane_and_line()
    return fetch(fetch(array, plane), line)


def scatter_two(first, second, beside=None):
    plane, line = plane_and_line()
    done = None
    sent_one = [first[i].astype(bf16) for i in range(1, len(plane))]
    sent_two = [second[i].astype(bf16) for i in range(1, len(line))]
    if beside is not None:
        work, argument = beside
        argument, sent_one, sent_two = lax.optimization_barrier((argument, sent_one, sent_two))
    came_one = [from_partner(block, "seq", mask) for block, mask in zip(sent_one, plane[1:])]
    came_two = [from_partner(block, "seq", mask) for block, mask in zip(sent_two, line[1:])]
    if beside is not None:
        done, came_one, came_two = lax.optimization_barrier((work(argument), came_one, came_two))
    half_one, half_two = first[0].astype(f32), second[0].astype(f32)
    for block in came_one:
        half_one = half_one + block.astype(f32)
    for block in came_two:
        half_two = half_two + block.astype(f32)
    sent_one = [half_one[i].astype(bf16) for i in range(1, len(line))]
    sent_two = [half_two[i].astype(bf16) for i in range(1, len(plane))]
    came_one = [from_partner(block, "seq", mask) for block, mask in zip(sent_one, line[1:])]
    came_two = [from_partner(block, "seq", mask) for block, mask in zip(sent_two, plane[1:])]
    one, two = half_one[0], half_two[0]
    for block in came_one:
        one = one + block.astype(f32)
    for block in came_two:
        two = two + block.astype(f32)
    return one, two, done


def tp_masks():
    return range(1, lax.axis_size("tp"))


def over_cores(array):
    return jnp.concatenate([array] + [from_partner(array, "tp", mask) for mask in tp_masks()], axis=-1)


def lanes_by_index(array):
    count = lax.axis_size("tp")
    pieces = jnp.split(array, count, axis=-1)
    me = lax.axis_index("tp")
    step = 1
    while step < count:
        flipped = [pieces[i ^ step] for i in range(count)]
        pieces = [jnp.where(me & step == 0, a, b) for a, b in zip(pieces, flipped)]
        step *= 2
    return jnp.concatenate(pieces, axis=-1)


def merged(group):
    tops, totals, weighted, targets = (jnp.stack([one[i] for one in group]) for i in range(4))
    top = jnp.max(tops, axis=0)
    shares = jnp.exp(tops - top)
    return jnp.stack(
        [
            top,
            jnp.sum(shares * totals, axis=0),
            jnp.sum(shares * weighted, axis=0),
            jnp.sum(targets, axis=0),
        ]
    )


def in_parts(values):
    high = lax.reduce_precision(values, 8, 7)
    middle = lax.reduce_precision(values - high, 8, 7)
    return high, middle, values - high - middle


def dot(left, right, on_left, on_right, precision=None):
    return lax.dot_general(
        left,
        right,
        (((on_left,), (on_right,)), ((), ())),
        precision=precision,
        preferred_element_type=f32,
    )


def logits_kernel(
    where, ids, scale, own_a, own_b, other_a, other_b, head, out, stats, all_features, *, line
):
    step = pl.program_id(0)
    tile = head.shape[0]
    blocks, rows_a, lanes = own_a.shape
    features = all_features.shape[0] // blocks
    rows_b = features - rows_a

    @pl.when(step == 0)
    def _():
        plane = blocks // line
        for device in range(blocks):
            relative = where[0] ^ device
            low, high = relative % plane, relative // plane
            at_a, at_b = low * line + high, high * plane + low
            start = device * features
            for side, (a, b) in enumerate(((own_a, own_b), (other_a, other_b))):
                columns = slice(side * lanes, (side + 1) * lanes)
                all_features[start : start + rows_a, columns] = a[at_a]
                all_features[start + rows_a : start + features, columns] = b[at_b][:rows_b]
        stats[...] = jnp.zeros_like(stats)
        stats[0:1, :] = jnp.full((1, stats.shape[1]), -jnp.inf, f32)

    logits = jnp.dot(head[...], all_features[...], preferred_element_type=f32) * scale[...]
    out[...] = logits
    entries = lax.broadcasted_iota(i32, logits.shape, 0) + (where[1] + step * tile)
    before = stats[0:1, :]
    top = jnp.maximum(before, jnp.max(logits, axis=0, keepdims=True))
    shrink = jnp.exp(before - top)
    expd = jnp.exp(logits - top)
    stats[0:1, :] = top
    stats[1:2, :] = stats[1:2, :] * shrink + jnp.sum(expd, axis=0, keepdims=True)
    stats[2:3, :] = stats[2:3, :] * shrink + jnp.sum(expd * logits, axis=0, keepdims=True)
    stats[3:4, :] = stats[3:4, :] + jnp.sum(
        jnp.where(entries == ids[...], logits, 0.0), axis=0, keepdims=True
    )


def head_logits(where, ids, scale, own_a, own_b, other_a, other_b, head, line):
    vocab, tokens = head.shape[0], ids.shape[1]
    tile = 512
    whole = lambda array: pl.BlockSpec(array.shape, lambda i, w: (0,) * array.ndim)
    return pl.pallas_call(
        functools.partial(logits_kernel, line=line),
        grid_spec=pltpu.PrefetchScalarGridSpec(
            num_scalar_prefetch=1,
            grid=(vocab // tile,),
            in_specs=[
                whole(ids),
                whole(scale),
                whole(own_a),
                whole(own_b),
                whole(other_a),
                whole(other_b),
                pl.BlockSpec((tile, D), lambda i, w: (i, 0)),
            ],
            out_specs=[
                pl.BlockSpec((tile, tokens), lambda i, w: (i, 0)),
                pl.BlockSpec((8, tokens), lambda i, w: (0, 0)),
                pl.BlockSpec((D, tokens), lambda i, w: (0, 0)),
            ],
        ),
        out_shape=[
            jax.ShapeDtypeStruct((vocab, tokens), f32),
            jax.ShapeDtypeStruct((8, tokens), f32),
            jax.ShapeDtypeStruct((D, tokens), bf16),
        ],
        compiler_params=pltpu.CompilerParams(vmem_limit_bytes=44 << 20),
        cost_estimate=pl.CostEstimate(
            flops=2 * vocab * D * tokens,
            bytes_accessed=2 * vocab * D + 4 * D * tokens,
            transcendentals=vocab * tokens,
        ),
    )(where, ids, scale, own_a, own_b, other_a, other_b, head)


def dfinal_kernel(where, ids, rows, logits, head, kept, sent, scaled, turned):
    step = pl.program_id(0)
    vocab, tokens = logits.shape
    lanes = kept.shape[3]

    @pl.when(step == 0)
    def _():
        top, share, coef, scale = (rows[i : i + 1, :] for i in range(4))
        tile = 256
        for start in range(0, vocab, tile):
            probs = jnp.exp(logits[start : start + tile, :] - top) * share
            entries = lax.broadcasted_iota(i32, probs.shape, 0) + (where[1] + start)
            dlogits = coef * (probs - (entries == ids[...]).astype(f32))
            scaled[start : start + tile, :] = (dlogits * scale).astype(bf16)
            turned[:, start : start + tile] = dlogits.T.astype(bf16)

    product = jnp.dot(turned[...], head[...], preferred_element_type=f32).T
    half = product.shape[0] // 2
    flip = where[0] & 1
    for piece in range(2):
        block = product[piece * half : (piece + 1) * half]
        kept[0, piece ^ flip] = block[:, :lanes]
        sent[0, piece ^ flip] = block[:, lanes:].astype(bf16)


def head_back(where, ids, rows, logits, head, blocks):
    vocab, tokens = logits.shape
    features = D // blocks
    lanes = tokens // 2
    pairs = blocks // 2
    whole = lambda array: pl.BlockSpec(array.shape, lambda i, w: (0,) * array.ndim)
    place = lambda i, w: (i ^ (w[0] >> 1), 0, 0, 0)
    return pl.pallas_call(
        dfinal_kernel,
        grid_spec=pltpu.PrefetchScalarGridSpec(
            num_scalar_prefetch=1,
            grid=(pairs,),
            in_specs=[
                whole(ids),
                whole(rows),
                whole(logits),
                pl.BlockSpec((vocab, 2 * features), lambda i, w: (0, i)),
            ],
            out_specs=[
                pl.BlockSpec((1, 2, features, lanes), place),
                pl.BlockSpec((1, 2, features, lanes), place),
                pl.BlockSpec((vocab, tokens), lambda i, w: (0, 0)),
            ],
            scratch_shapes=[pltpu.VMEM((tokens, vocab), bf16)],
        ),
        out_shape=[
            jax.ShapeDtypeStruct((pairs, 2, features, lanes), f32),
            jax.ShapeDtypeStruct((pairs, 2, features, lanes), bf16),
            jax.ShapeDtypeStruct((vocab, tokens), bf16),
        ],
        compiler_params=pltpu.CompilerParams(vmem_limit_bytes=32 << 20),
        cost_estimate=pl.CostEstimate(
            flops=2 * vocab * D * tokens,
            bytes_accessed=2 * vocab * D + 4 * D * tokens,
            transcendentals=vocab * tokens,
        ),
    )(where, ids, rows, logits, head)


def plain_logits(where, ids, scale, pieces_a, pieces_b, head, line):
    rows_a = pieces_a[0].shape[1]
    blocks, _, lanes = pieces_a[0].shape
    features = D // blocks
    plane = blocks // line
    sides = []
    for a, b in zip(pieces_a, pieces_b):
        a = a.reshape(plane, line, rows_a, lanes).swapaxes(0, 1).reshape(blocks, rows_a, lanes)
        both = jnp.concatenate([a, b[:, : features - rows_a]], axis=1)
        sides.append(both[where[0] ^ jnp.arange(blocks)].reshape(D, lanes))
    all_features = jnp.concatenate(sides, axis=1)
    logits = dot(head, all_features, 1, 0) * scale
    top = jnp.max(logits, axis=0)
    expd = jnp.exp(logits - top)
    onehot = (jnp.arange(head.shape[0])[:, None] + where[1]) == ids
    stats = [
        top,
        jnp.sum(expd, axis=0),
        jnp.sum(expd * logits, axis=0),
        jnp.sum(jnp.where(onehot, logits, 0.0), axis=0),
    ]
    return logits, jnp.stack(stats), all_features


def plain_back(where, ids, rows, logits, head, blocks):
    top, share, coef, scale = rows[0], rows[1], rows[2], rows[3]
    lanes = logits.shape[1] // lax.axis_size("tp")
    onehot = (jnp.arange(head.shape[0])[:, None] + where[1]) == ids
    dlogits = coef * (jnp.exp(logits - top) * share - onehot.astype(f32))
    product = dot(head, dlogits.astype(bf16), 0, 0).reshape(blocks, D // blocks, -1)
    product = product[where[0] ^ jnp.arange(blocks)]
    return product[..., :lanes], product[..., lanes:].astype(bf16), (dlogits * scale).astype(bf16)


def shards(
    prev_hidden,
    token_embed,
    gain_hidden,
    gain_embed,
    gain_final,
    proj_hidden,
    proj_embed,
    head,
    target_ids,
    valid,
    rest_count,
):
    blocks, cores = lax.axis_size("seq"), lax.axis_size("tp")
    plane, line = (len(masks) for masks in plane_and_line())
    me = lax.axis_index("seq")
    rows, width = prev_hidden.shape
    features = proj_hidden.shape[1]
    tokens = rows * blocks
    lanes = tokens // cores

    prev_f = prev_hidden.astype(f32)
    embed_f = token_embed.astype(f32)
    sums = lax.psum(
        jnp.stack([jnp.sum(prev_f * prev_f, axis=-1), jnp.sum(embed_f * embed_f, axis=-1)]), "tp"
    )
    scales = lax.rsqrt(sums / D + epsilon)
    scale_prev, scale_embed = scales[0][:, None], scales[1][:, None]
    normed_prev = (prev_f * scale_prev * gain_hidden).astype(bf16)
    normed_embed = (embed_f * scale_embed * gain_embed).astype(bf16)
    facts = jnp.stack([target_ids // 256, target_ids % 256, valid], axis=1).astype(bf16)
    facts = jnp.pad(facts, ((0, 0), (0, 125)))

    cut = round((2 * width + 128) / 192) * 128 - width
    rest = width - cut
    first = gather_line_first(jnp.concatenate([normed_prev, normed_embed[:, :cut]], axis=1))
    second = gather_plane_first(jnp.concatenate([normed_embed[:, cut:], facts], axis=1))
    first = first.reshape(tokens, width + cut)
    second = second.swapaxes(0, 1).reshape(tokens, rest + 128)

    row = lax.broadcasted_iota(i32, (tokens, 1), 0)
    place = row // rows
    partner = (place % line) * plane + place // line
    position = (me ^ partner) * rows + row % rows
    column = lax.broadcasted_iota(i32, (1, tokens), 1)
    order_prev = (position == column).astype(f32)
    order_embed = (position - 1 == column).astype(f32)

    from_prev = dot(proj_hidden, first[:, :width], 0, 1)
    from_embed = dot(proj_embed[:cut], first[:, width:], 0, 1) + dot(
        proj_embed[cut:], second[:, :rest], 0, 1
    )
    partial_value = dot(
        jnp.concatenate([from_prev, from_embed], axis=1),
        jnp.concatenate([order_prev, order_embed], axis=0),
        1,
        0,
        lax.Precision.HIGHEST,
    )
    facts_all = dot(second[:, rest:], order_prev.astype(bf16), 0, 0)
    ids_all = (facts_all[0:1] * 256 + facts_all[1:2]).astype(i32)
    valid_all = facts_all[2]
    core = lax.axis_index("tp")
    cut_of = lambda mask: lax.dynamic_slice_in_dim(partial_value, (core ^ mask) * lanes, lanes, 1)
    mixed_f = cut_of(0)
    for mask in tp_masks():
        mixed_f = mixed_f + from_partner(cut_of(mask), "tp", mask)
    mixed_f = mixed_f.astype(bf16).astype(f32)
    scaled = (mixed_f * gain_final[:, None]).astype(bf16)
    square_parts = jnp.stack(in_parts(jnp.sum(mixed_f * mixed_f, axis=0))).astype(bf16)
    square_parts = jnp.pad(square_parts, ((0, 13), (0, 0)))
    rows_a = features - round(0.32 * features / 16) * 16
    own_a = gather_line_first(scaled[:rows_a]).reshape(blocks, rows_a, lanes)
    own_b = gather_plane_first(jnp.concatenate([scaled[rows_a:], square_parts], axis=0))
    own_b = own_b.reshape(blocks, features - rows_a + 16, lanes)
    pieces_a = [own_a] + [from_partner(own_a, "tp", mask) for mask in tp_masks()]
    pieces_b = [own_b] + [from_partner(own_b, "tp", mask) for mask in tp_masks()]
    squares = [
        jnp.sum(b[:, features - rows_a : features - rows_a + 3].astype(f32), axis=(0, 1))
        for b in pieces_b
    ]
    scale_own = lax.rsqrt(squares[0] / D + epsilon)
    scale_final = lax.rsqrt(jnp.concatenate(squares) / D + epsilon)

    vocab_rows = head.shape[0]
    where = jnp.stack([me, lax.axis_index(("seq", "tp")) * vocab_rows]).astype(i32)
    ids = lanes_by_index(ids_all)
    valid_here = lanes_by_index(valid_all)
    fits = cores == 2 and lanes % 128 == 0 and vocab_rows % 512 == 0 and 2 * features % 128 == 0
    if fits:
        pieces = (pieces_a[0], pieces_b[0], pieces_a[1], pieces_b[1])
        logits, stats, scaled_all = head_logits(
            where, ids, scale_final[None, :], *pieces, head, line
        )
    else:
        logits, stats, scaled_all = plain_logits(
            where, ids, scale_final, pieces_a, pieces_b, head, line
        )
    stats = stats[:4]
    for masks in plane_and_line():
        stats = merged([stats] + [from_partner(stats, "seq", mask) for mask in masks[1:]])
    stats = lanes_by_index(stats)
    stats = merged([stats] + [from_partner(stats, "tp", mask) for mask in tp_masks()])
    row_top, row_total, row_weighted, target_logit = lanes_by_index(stats)
    count = jnp.sum(valid_all) + rest_count[0].astype(f32)
    coef = loss_scale * valid_here / count
    row_values = jnp.stack([row_top, 1.0 / row_total, coef, scale_final])
    row_values = jnp.pad(row_values, ((0, 4), (0, 0)))
    back = head_back if fits else plain_back
    kept, sent, dlogits_scaled = back(where, ids, row_values, logits, head, blocks)
    dfinal = kept.reshape(blocks, features, lanes)
    for mask in tp_masks():
        piece = sent[..., (mask - 1) * lanes : mask * lanes]
        dfinal = dfinal + from_partner(piece, "tp", mask).astype(f32).reshape(dfinal.shape)
    dfinal = dfinal.reshape(line, plane, features, lanes)
    one, two, _ = scatter_two(dfinal[:, :, :rows_a].swapaxes(0, 1), dfinal[:, :, rows_a:])
    dfinal = jnp.concatenate([one, two], axis=0)

    total_dot = (coef * (row_weighted / row_total - target_logit))[:lanes] / scale_own
    dmixed = (
        scale_own * (dfinal * gain_final[:, None]) - mixed_f * (scale_own**3 * (total_dot / D))
    ).astype(bf16)
    dmixed = lanes_by_index(over_cores(dmixed))
    dmixed_prev = dot(dmixed, order_prev.astype(bf16), 1, 1).astype(bf16)
    dmixed_embed = dot(dmixed, order_embed.astype(bf16), 1, 1).astype(bf16)
    back_prev = dot(dmixed_prev, proj_hidden, 0, 1)
    back_embed = dot(dmixed_embed, proj_embed, 0, 1)
    one = jnp.concatenate([back_prev, back_embed[:, :cut]], axis=1)
    two = back_embed[:, cut:]
    one, two, done = scatter_two(
        one.reshape(plane, line, rows, width + cut),
        two.reshape(plane, line, rows, rest).swapaxes(0, 1),
        (
            lambda given: (
                dot(given[0], scaled_all, 1, 1).astype(bf16),
                dot(first[:, :width], given[1], 0, 1).astype(bf16),
                dot(
                    jnp.concatenate([first[:, width:], second[:, :rest]], axis=1), given[2], 0, 1
                ).astype(bf16),
            ),
            (dlogits_scaled, dmixed_prev, dmixed_embed),
        ),
    )
    grad_head, grad_proj_hidden, grad_proj_embed = done
    grad_prev = one[:, :width] * gain_hidden
    grad_embed = jnp.concatenate([one[:, width:], two], axis=1) * gain_embed
    dots = lax.psum(
        jnp.stack([jnp.sum(grad_prev * prev_f, axis=-1), jnp.sum(grad_embed * embed_f, axis=-1)]),
        "tp",
    )
    grad_prev_hidden = (
        scale_prev * grad_prev - prev_f * (scale_prev**3 * (dots[0] / D)[:, None])
    ).astype(bf16)
    grad_token_embed = (
        scale_embed * grad_embed - embed_f * (scale_embed**3 * (dots[1] / D)[:, None])
    ).astype(bf16)
    return (grad_prev_hidden, grad_token_embed, grad_proj_hidden, grad_proj_embed, grad_head)


def solution(mesh):
    return jax.shard_map(
        shards,
        mesh=mesh,
        in_specs=(
            P("seq", "tp"),
            P("seq", "tp"),
            P("tp"),
            P("tp"),
            P("seq"),
            P("tp", "seq"),
            P("tp", "seq"),
            P(("seq", "tp"), None),
            P("seq"),
            P("seq"),
            P(),
        ),
        out_specs=(
            P("seq", "tp"),
            P("seq", "tp"),
            P("tp", "seq"),
            P("tp", "seq"),
            P(("seq", "tp"), None),
        ),
        check_vma=False,
    )
```

```python
import jax
import jax.numpy as jnp
from jax import lax
from jax.experimental import pallas as pl
from jax.experimental.pallas import tpu as pltpu
from jax.sharding import PartitionSpec as P

D = 7168


loss_scale = 4096.0
epsilon = 1e-06

f32 = jnp.float32
bf16 = jnp.bfloat16
i32 = jnp.int32


def from_partner(array, axis, mask):
    size = lax.axis_size(axis)
    return lax.ppermute(array, axis, [(i, i ^ mask) for i in range(size)])


def bits_of(axis):
    return lax.axis_size(axis).bit_length() - 1


def gather(array, order):
    count, shape = len(order), array.shape
    for bit in order:
        array = jnp.stack([array, from_partner(array, "seq", 1 << bit)])
    dims = [count - 1 - order.index(bit) for bit in reversed(range(count))]
    array = array.transpose(dims + list(range(count, array.ndim)))
    return array.reshape((1 << count,) + shape)


def scatter(arrays, orders, beside=()):
    count = bits_of("seq")
    arrays = [array.reshape((2,) * count + array.shape[1:]) for array in arrays]
    left = [list(reversed(range(count))) for _ in arrays]
    results = []
    for step in range(count):
        for k, order in enumerate(orders):
            bit = order[step]
            dim = left[k].index(bit)
            left[k].remove(bit)
            sent = lax.index_in_dim(arrays[k], 1, dim, keepdims=False).astype(bf16)
            tied = k == 0 and step < len(beside)
            if tied:
                work, argument = beside[step]
                sent, argument = lax.optimization_barrier((sent, argument))
            came = from_partner(sent, "seq", 1 << bit)
            if tied:
                result, mark = work(argument, results)
                came, mark = lax.optimization_barrier((came, mark))
                results.append(result)
            kept = lax.index_in_dim(arrays[k], 0, dim, keepdims=False).astype(f32)
            arrays[k] = kept + came.astype(f32)
    return arrays, results


def orders_of():
    down = list(reversed(range(bits_of("seq"))))
    return [down, down[:-2] + [0, 1], [0, 1] + down[:-2]]


def cut_in_three(size, unit):
    third = round(0.25 * size / unit) * unit
    first = (size - third + unit) // (2 * unit) * unit
    return first, size - third


def tp_masks():
    return range(1, lax.axis_size("tp"))


def over_cores(array):
    return jnp.concatenate([array] + [from_partner(array, "tp", mask) for mask in tp_masks()], axis=-1)


def lanes_by_index(array):
    count = lax.axis_size("tp")
    pieces = jnp.split(array, count, axis=-1)
    me = lax.axis_index("tp")
    step = 1
    while step < count:
        flipped = [pieces[i ^ step] for i in range(count)]
        pieces = [jnp.where(me & step == 0, a, b) for a, b in zip(pieces, flipped)]
        step *= 2
    return jnp.concatenate(pieces, axis=-1)


def merged(group):
    tops, totals, weighted, targets = (jnp.stack([one[i] for one in group]) for i in range(4))
    top = jnp.max(tops, axis=0)
    shares = jnp.exp(tops - top)
    return jnp.stack(
        [
            top,
            jnp.sum(shares * totals, axis=0),
            jnp.sum(shares * weighted, axis=0),
            jnp.sum(targets, axis=0),
        ]
    )


def in_parts(values):
    high = lax.reduce_precision(values, 8, 7)
    middle = lax.reduce_precision(values - high, 8, 7)
    return high, middle, values - high - middle


def dot(left, right, on_left, on_right, precision=None):
    return lax.dot_general(
        left,
        right,
        (((on_left,), (on_right,)), ((), ())),
        precision=precision,
        preferred_element_type=f32,
    )


def logits_kernel(where, ids, scale, gain, *refs):
    *pieces, head, out, stats, all_features = refs
    step = pl.program_id(0)
    tile = head.shape[0]
    blocks, _, lanes = pieces[0].shape
    features = all_features.shape[0] // blocks

    @pl.when(step == 0)
    def _():
        for device in range(blocks):
            for side in range(2):
                start = device * features
                columns = slice(side * lanes, (side + 1) * lanes)
                for piece in pieces[3 * side : 3 * side + 3]:
                    rows = min(piece.shape[1], (device + 1) * features - start)
                    all_features[start : start + rows, columns] = piece[where[0] ^ device][:rows]
                    start += rows
        columns_of_gain = gain[...].T
        for k in range(gain.shape[0]):
            part = slice(128 * k, 128 * (k + 1))
            values = all_features[part, :].astype(f32) * scale[...] * columns_of_gain[:, k : k + 1]
            all_features[part, :] = values.astype(bf16)
        stats[...] = jnp.zeros_like(stats)
        stats[0:1, :] = jnp.full((1, stats.shape[1]), -jnp.inf, f32)

    logits = jnp.dot(head[...], all_features[...], preferred_element_type=f32)
    out[...] = logits
    entries = lax.broadcasted_iota(i32, logits.shape, 0) + (where[1] + step * tile)
    before = stats[0:1, :]
    top = jnp.maximum(before, jnp.max(logits, axis=0, keepdims=True))
    shrink = jnp.exp(before - top)
    expd = jnp.exp(logits - top)
    stats[0:1, :] = top
    stats[1:2, :] = stats[1:2, :] * shrink + jnp.sum(expd, axis=0, keepdims=True)
    stats[2:3, :] = stats[2:3, :] * shrink + jnp.sum(expd * logits, axis=0, keepdims=True)
    stats[3:4, :] = stats[3:4, :] + jnp.sum(
        jnp.where(entries == ids[...], logits, 0.0), axis=0, keepdims=True
    )


def head_logits(where, ids, scale, gain, pieces, head):
    vocab, tokens = head.shape[0], ids.shape[1]
    tile = 512
    gain = gain.reshape(-1, 128)
    whole = lambda array: pl.BlockSpec(array.shape, lambda i, w: (0,) * array.ndim)
    return pl.pallas_call(
        logits_kernel,
        grid_spec=pltpu.PrefetchScalarGridSpec(
            num_scalar_prefetch=1,
            grid=(vocab // tile,),
            in_specs=[
                whole(ids),
                whole(scale),
                whole(gain),
                *[whole(piece) for piece in pieces],
                pl.BlockSpec((tile, D), lambda i, w: (i, 0)),
            ],
            out_specs=[
                pl.BlockSpec((tile, tokens), lambda i, w: (i, 0)),
                pl.BlockSpec((8, tokens), lambda i, w: (0, 0)),
                pl.BlockSpec((D, tokens), lambda i, w: (0, 0)),
            ],
        ),
        out_shape=[
            jax.ShapeDtypeStruct((vocab, tokens), f32),
            jax.ShapeDtypeStruct((8, tokens), f32),
            jax.ShapeDtypeStruct((D, tokens), bf16),
        ],
        compiler_params=pltpu.CompilerParams(vmem_limit_bytes=44 << 20),
        cost_estimate=pl.CostEstimate(
            flops=2 * vocab * D * tokens,
            bytes_accessed=2 * vocab * D + 4 * D * tokens,
            transcendentals=vocab * tokens,
        ),
    )(where, ids, scale, gain, *pieces, head)


def dfinal_kernel(where, ids, rows, logits, head, kept, sent, plain, turned):
    step = pl.program_id(0)
    vocab, tokens = logits.shape
    lanes = kept.shape[3]

    @pl.when(step == 0)
    def _():
        top, share, coef = (rows[i : i + 1, :] for i in range(3))
        tile = 256
        for start in range(0, vocab, tile):
            probs = jnp.exp(logits[start : start + tile, :] - top) * share
            entries = lax.broadcasted_iota(i32, probs.shape, 0) + (where[1] + start)
            dlogits = coef * (probs - (entries == ids[...]).astype(f32))
            plain[start : start + tile, :] = dlogits.astype(bf16)
            turned[:, start : start + tile] = dlogits.T.astype(bf16)

    product = jnp.dot(turned[...], head[...], preferred_element_type=f32).T
    half = product.shape[0] // 2
    flip = where[0] & 1
    for piece in range(2):
        block = product[piece * half : (piece + 1) * half]
        kept[0, piece ^ flip] = block[:, :lanes]
        sent[0, piece ^ flip] = block[:, lanes:].astype(bf16)


def head_back(where, ids, rows, logits, head, blocks):
    vocab, tokens = logits.shape
    features = D // blocks
    lanes = tokens // 2
    pairs = blocks // 2
    whole = lambda array: pl.BlockSpec(array.shape, lambda i, w: (0,) * array.ndim)
    place = lambda i, w: (i ^ (w[0] >> 1), 0, 0, 0)
    return pl.pallas_call(
        dfinal_kernel,
        grid_spec=pltpu.PrefetchScalarGridSpec(
            num_scalar_prefetch=1,
            grid=(pairs,),
            in_specs=[
                whole(ids),
                whole(rows),
                whole(logits),
                pl.BlockSpec((vocab, 2 * features), lambda i, w: (0, i)),
            ],
            out_specs=[
                pl.BlockSpec((1, 2, features, lanes), place),
                pl.BlockSpec((1, 2, features, lanes), place),
                pl.BlockSpec((vocab, tokens), lambda i, w: (0, 0)),
            ],
            scratch_shapes=[pltpu.VMEM((tokens, vocab), bf16)],
        ),
        out_shape=[
            jax.ShapeDtypeStruct((pairs, 2, features, lanes), f32),
            jax.ShapeDtypeStruct((pairs, 2, features, lanes), bf16),
            jax.ShapeDtypeStruct((vocab, tokens), bf16),
        ],
        compiler_params=pltpu.CompilerParams(vmem_limit_bytes=32 << 20),
        cost_estimate=pl.CostEstimate(
            flops=2 * vocab * D * tokens,
            bytes_accessed=2 * vocab * D + 4 * D * tokens,
            transcendentals=vocab * tokens,
        ),
    )(where, ids, rows, logits, head)


def grad_head_kernel(left, features, *refs):
    out, mark = refs[-2:]
    out[...] = lax.dot_general(
        left[...], features[...], (((1,), (1,)), ((), ())), preferred_element_type=f32
    ).astype(bf16)
    mark[...] = jnp.zeros_like(mark)


def grad_head_rows(left, features, index, count, before):
    vocab, tokens = left.shape
    rows, tile = vocab // count, 1024
    given = () if before is None else (before,)
    return pl.pallas_call(
        grad_head_kernel,
        grid=(D // tile,),
        in_specs=[
            pl.BlockSpec((rows, tokens), lambda i: (index, 0)),
            pl.BlockSpec((tile, tokens), lambda i: (i, 0)),
            *[pl.BlockSpec(memory_space=pl.ANY) for _ in given],
        ],
        out_specs=[
            pl.BlockSpec((rows, tile), lambda i: (index, i)),
            pl.BlockSpec((8, 128), lambda i: (0, 0)),
        ],
        out_shape=[
            jax.ShapeDtypeStruct((vocab, D), bf16),
            jax.ShapeDtypeStruct((8, 128), f32),
        ],
        input_output_aliases={2: 0} if given else {},
        compiler_params=pltpu.CompilerParams(vmem_limit_bytes=20 << 20),
        cost_estimate=pl.CostEstimate(
            flops=2 * rows * D * tokens, bytes_accessed=2 * rows * D + 2 * D * tokens, transcendentals=0
        ),
    )(left, features, *given)


def plain_logits(where, ids, scale, gain, pieces, head):
    blocks, _, lanes = pieces[0].shape
    features = D // blocks
    sides = []
    for i in range(0, len(pieces), 3):
        side = jnp.concatenate(pieces[i : i + 3], axis=1)[:, :features]
        sides.append(side[where[0] ^ jnp.arange(blocks)].reshape(D, lanes))
    all_features = jnp.concatenate(sides, axis=1).astype(f32)
    all_features = (all_features * scale * gain[:, None]).astype(bf16)
    logits = dot(head, all_features, 1, 0)
    top = jnp.max(logits, axis=0)
    expd = jnp.exp(logits - top)
    onehot = (jnp.arange(head.shape[0])[:, None] + where[1]) == ids
    stats = [
        top,
        jnp.sum(expd, axis=0),
        jnp.sum(expd * logits, axis=0),
        jnp.sum(jnp.where(onehot, logits, 0.0), axis=0),
    ]
    return logits, jnp.stack(stats), all_features


def plain_back(where, ids, rows, logits, head, blocks):
    top, share, coef = rows[0], rows[1], rows[2]
    lanes = logits.shape[1] // lax.axis_size("tp")
    onehot = (jnp.arange(head.shape[0])[:, None] + where[1]) == ids
    dlogits = coef * (jnp.exp(logits - top) * share - onehot.astype(f32))
    dlogits = dlogits.astype(bf16)
    product = dot(head, dlogits, 0, 0).reshape(blocks, D // blocks, -1)
    product = product[where[0] ^ jnp.arange(blocks)]
    return product[..., :lanes], product[..., lanes:].astype(bf16), dlogits


def shards(
    prev_hidden,
    token_embed,
    gain_hidden,
    gain_embed,
    gain_final,
    proj_hidden,
    proj_embed,
    head,
    target_ids,
    valid,
    rest_count,
):
    blocks, cores = lax.axis_size("seq"), lax.axis_size("tp")
    down = orders_of()
    up = [order[::-1] for order in down]
    me = lax.axis_index("seq")
    rows, width = prev_hidden.shape
    features = proj_hidden.shape[1]
    tokens = rows * blocks
    lanes = tokens // cores

    prev_f = prev_hidden.astype(f32)
    embed_f = token_embed.astype(f32)
    sums = lax.psum(
        jnp.stack([jnp.sum(prev_f * prev_f, axis=-1), jnp.sum(embed_f * embed_f, axis=-1)]), "tp"
    )
    scales = lax.rsqrt(sums / D + epsilon)
    scale_prev, scale_embed = scales[0][:, None], scales[1][:, None]
    normed_prev = (prev_f * scale_prev * gain_hidden).astype(bf16)
    normed_embed = (embed_f * scale_embed * gain_embed).astype(bf16)
    main = round(0.75 * width / 128) * 128
    rest = width - main
    first, second, third, ids_here, valid_here, gain_here = lax.optimization_barrier(
        (
            normed_prev[:, :main],
            normed_embed[:, :main],
            jnp.concatenate([normed_prev[:, main:], normed_embed[:, main:]], axis=1),
            target_ids,
            valid,
            gain_final,
        )
    )
    facts = jnp.stack([ids_here // 256, ids_here % 256, valid_here]).astype(bf16)
    facts = dot(jnp.eye(rows, dtype=bf16), jnp.pad(facts, ((0, 5), (0, 0))), 1, 1).astype(bf16)
    gain_parts = jnp.stack(in_parts(gain_here)).astype(bf16).reshape(rows, -1)
    gain_columns = gain_parts.shape[1]
    facts = jnp.concatenate([facts, gain_parts], axis=1)
    facts = jnp.pad(facts, ((0, 0), (0, 128 - facts.shape[1])))

    first = gather(first, down[0]).reshape(tokens, main)
    second = gather(second, down[1]).reshape(tokens, main)
    third = gather(jnp.concatenate([third, facts], axis=1), down[2])
    third = third.reshape(tokens, 2 * rest + 128)

    row = lax.broadcasted_iota(i32, (tokens, 1), 0)
    position = (me ^ (row // rows)) * rows + row % rows
    column = lax.broadcasted_iota(i32, (1, tokens), 1)
    order_prev = position == column
    order_embed = position - 1 == column

    from_prev = dot(proj_hidden[:main], first, 0, 1) + dot(proj_hidden[main:], third[:, :rest], 0, 1)
    from_embed = dot(proj_embed[:main], second, 0, 1) + dot(
        proj_embed[main:], third[:, rest : 2 * rest], 0, 1
    )
    facts_all = third[:, 2 * rest :]
    facts_prev = dot(facts_all, order_prev.astype(bf16), 0, 0)
    partial_value = dot(
        jnp.concatenate([from_prev, from_embed], axis=1),
        jnp.concatenate([order_prev, order_embed], axis=0).astype(f32),
        1,
        0,
        lax.Precision.HIGHEST,
    )
    gain_all = facts_all[:, 8 : 8 + gain_columns].reshape(blocks, 3, features).astype(f32)
    gain_all = gain_all[:, 0] + gain_all[:, 1] + gain_all[:, 2]
    block = jnp.arange(blocks)
    gain_all = dot(
        ((me ^ block)[:, None] == block[None, :]).astype(f32), gain_all, 0, 0, lax.Precision.HIGHEST
    ).reshape(D)
    ids_all = (facts_prev[0:1] * 256 + facts_prev[1:2]).astype(i32)
    valid_all = facts_prev[2]
    core = lax.axis_index("tp")
    cut_of = lambda mask: lax.dynamic_slice_in_dim(partial_value, (core ^ mask) * lanes, lanes, 1)
    mixed_f = cut_of(0)
    for mask in tp_masks():
        mixed_f = mixed_f + from_partner(cut_of(mask), "tp", mask)
    mixed_f = mixed_f.astype(bf16).astype(f32)
    mixed = mixed_f.astype(bf16)
    square_parts = jnp.stack(in_parts(jnp.sum(mixed_f * mixed_f, axis=0))).astype(bf16)
    square_parts = jnp.pad(square_parts, ((0, 13), (0, 0)))
    one, two = cut_in_three(features, 16)
    pieces = [
        gather(part, order)
        for part, order in zip(
            (mixed[:one], mixed[one:two], jnp.concatenate([mixed[two:], square_parts], axis=0)),
            down,
        )
    ]
    for mask in tp_masks():
        pieces = pieces + [from_partner(piece, "tp", mask) for piece in pieces[:3]]
    squares = [
        jnp.sum(piece[:, features - two :][:, :3].astype(f32), axis=(0, 1)) for piece in pieces[2::3]
    ]
    scale_own = lax.rsqrt(squares[0] / D + epsilon)
    scale_final = lax.rsqrt(jnp.concatenate(squares) / D + epsilon)

    vocab_rows = head.shape[0]
    where = jnp.stack([me, lax.axis_index(("seq", "tp")) * vocab_rows]).astype(i32)
    ids = lanes_by_index(ids_all)
    valid_lanes = lanes_by_index(valid_all)
    fits = cores == 2 and lanes % 128 == 0 and vocab_rows % 512 == 0 and 2 * features % 128 == 0
    forward = head_logits if fits else plain_logits
    logits, stats, final_all = forward(where, ids, scale_final[None, :], gain_all, pieces, head)
    stats = stats[:4]
    for bit in range(bits_of("seq")):
        stats = merged([stats, from_partner(stats, "seq", 1 << bit)])
    stats = lanes_by_index(stats)
    stats = merged([stats] + [from_partner(stats, "tp", mask) for mask in tp_masks()])
    row_top, row_total, row_weighted, target_logit = lanes_by_index(stats)
    count = jnp.sum(valid_all) + rest_count[0].astype(f32)
    coef = loss_scale * valid_lanes / count
    row_values = jnp.stack([row_top, 1.0 / row_total, coef])
    row_values = jnp.pad(row_values, ((0, 5), (0, 0)))
    back = head_back if fits else plain_back
    kept, sent, dlogits = back(where, ids, row_values, logits, head, blocks)
    dfinal = kept.reshape(blocks, features, lanes)
    for mask in tp_masks():
        piece = sent[..., (mask - 1) * lanes : mask * lanes]
        dfinal = dfinal + from_partner(piece, "tp", mask).astype(f32).reshape(dfinal.shape)

    def grad_head_piece(index):
        if fits:
            return lambda left, results: grad_head_rows(
                left, final_all, index, 4, results[-1] if results else None
            )
        return lambda left, results: (dot(left, final_all, 1, 1).astype(bf16), left[:8])

    early = [(grad_head_piece(index), dlogits) for index in range(2 if fits else 1)]
    dfinal, results = scatter([dfinal[:, :one], dfinal[:, one:two], dfinal[:, two:]], up, early)
    dfinal = jnp.concatenate(dfinal, axis=0)

    total_dot = (coef * (row_weighted / row_total - target_logit))[:lanes] / scale_own
    dmixed = (
        scale_own * (dfinal * gain_final[:, None]) - mixed_f * (scale_own**3 * (total_dot / D))
    ).astype(bf16)
    dmixed = lanes_by_index(over_cores(dmixed))
    dmixed_prev = dot(dmixed, order_prev.astype(bf16), 1, 1).astype(bf16)
    dmixed_embed = dot(dmixed, order_embed.astype(bf16), 1, 1).astype(bf16)
    back_prev = dot(dmixed_prev, proj_hidden, 0, 1).reshape(blocks, rows, width)
    back_embed = dot(dmixed_embed, proj_embed, 0, 1).reshape(blocks, rows, width)

    def head_grad_end(left, before):
        grad_head = results[-1]
        mark = left[:8]
        if fits:
            for index in (2, 3):
                grad_head, mark = grad_head_rows(left, final_all, index, 4, grad_head)
        return grad_head, mark

    def proj_grad_hidden(given, before):
        rows_all = jnp.concatenate([first, third[:, :rest]], axis=1)
        out = dot(rows_all, given, 0, 1).astype(bf16)
        return out, out[:8]

    def proj_grad_embed(given, before):
        rows_all = jnp.concatenate([second, third[:, rest : 2 * rest]], axis=1)
        out = dot(rows_all, given, 0, 1).astype(bf16)
        return out, out[:8]

    (one, two, three), results = scatter(
        [
            back_prev[..., :main],
            back_embed[..., :main],
            jnp.concatenate([back_prev[..., main:], back_embed[..., main:]], axis=-1),
        ],
        up,
        [
            (head_grad_end, dlogits),
            (proj_grad_hidden, dmixed_prev),
            (proj_grad_embed, dmixed_embed),
        ],
    )
    grad_head, grad_proj_hidden, grad_proj_embed = results
    grad_prev = jnp.concatenate([one, three[:, :rest]], axis=1) * gain_hidden
    grad_embed = jnp.concatenate([two, three[:, rest:]], axis=1) * gain_embed
    dots = lax.psum(
        jnp.stack([jnp.sum(grad_prev * prev_f, axis=-1), jnp.sum(grad_embed * embed_f, axis=-1)]),
        "tp",
    )
    grad_prev_hidden = (
        scale_prev * grad_prev - prev_f * (scale_prev**3 * (dots[0] / D)[:, None])
    ).astype(bf16)
    grad_token_embed = (
        scale_embed * grad_embed - embed_f * (scale_embed**3 * (dots[1] / D)[:, None])
    ).astype(bf16)
    return (grad_prev_hidden, grad_token_embed, grad_proj_hidden, grad_proj_embed, grad_head)


def solution(mesh):
    return jax.shard_map(
        shards,
        mesh=mesh,
        in_specs=(
            P("seq", "tp"),
            P("seq", "tp"),
            P("tp"),
            P("tp"),
            P("seq"),
            P("tp", "seq"),
            P("tp", "seq"),
            P(("seq", "tp"), None),
            P("seq"),
            P("seq"),
            P(),
        ),
        out_specs=(
            P("seq", "tp"),
            P("seq", "tp"),
            P("tp", "seq"),
            P("tp", "seq"),
            P(("seq", "tp"), None),
        ),
        check_vma=False,
    )
```

```python
import jax
import jax.numpy as jnp
from jax import lax
from jax.experimental import pallas as pl
from jax.experimental.pallas import tpu as pltpu
from jax.sharding import PartitionSpec as P

D = 7168


loss_scale = 4096.0
epsilon = 1e-06

f32 = jnp.float32
bf16 = jnp.bfloat16
i32 = jnp.int32


def from_partner(array, axis, mask):
    size = lax.axis_size(axis)
    return lax.ppermute(array, axis, [(i, i ^ mask) for i in range(size)])


def bits_of(axis):
    return lax.axis_size(axis).bit_length() - 1


def after(array, *others):
    for other in others:
        array = array + (other.reshape(-1)[0] * 0).astype(array.dtype)
    return array


def in_order(array, order):
    count = len(order)
    dims = [count - 1 - order.index(bit) for bit in reversed(range(count))]
    array = array.transpose(dims + list(range(count, array.ndim)))
    return array.reshape((1 << count,) + array.shape[count:])


def gather(first, second, third, axis):
    high = list(reversed(range(2, bits_of("seq"))))
    cut = first.shape[axis]
    both = jnp.concatenate([first, second], axis=axis)
    axis -= both.ndim
    came = []
    for bit in high:
        came.append(from_partner(both, "seq", 1 << bit))
        both = jnp.stack([both, came[-1]])
    first = lax.slice_in_dim(both, 0, cut, axis=both.ndim + axis)
    second = lax.slice_in_dim(both, cut, both.shape[axis], axis=both.ndim + axis)
    third = after(third, came[0])
    for bit in (0, 1):
        first = jnp.stack([first, from_partner(first, "seq", 2 >> bit)])
        second = jnp.stack([second, from_partner(second, "seq", 1 << bit)])
        third = jnp.stack([third, from_partner(third, "seq", 1 << bit)])
    third = after(third, came[-1])
    for bit in high:
        third = jnp.stack([third, from_partner(third, "seq", 1 << bit)])
    return in_order(first, high + [1, 0]), in_order(second, high + [0, 1]), in_order(third, [0, 1] + high)


def scatter(first, second, third, axis, beside=()):
    count = bits_of("seq")
    cut = first.shape[axis]
    axis -= first.ndim
    results = []

    def halves(array, left, bit):
        dim = left.index(bit)
        sent = lax.index_in_dim(array, 1, dim, keepdims=False).astype(bf16)
        kept = lax.index_in_dim(array, 0, dim, keepdims=False).astype(f32)
        return kept, from_partner(sent, "seq", 1 << bit), [other for other in left if other != bit]

    def work_of(step):
        if step >= len(beside):
            return []
        result, mark = beside[step](results)
        results.append(result)
        return [mark]

    cut_up = lambda array: array.reshape((2,) * count + array.shape[1:])
    first, second, third = cut_up(first), cut_up(second), cut_up(third)
    bits = list(reversed(range(count)))
    left, left_second, left_third = bits, bits, bits
    line = bits[:-2][::-1]
    orders = [[0, 1], [1, 0], line + [1, 0]]
    for step in range(2):
        kept_one, came_one, left = halves(first, left, orders[0][step])
        kept_two, came_two, left_second = halves(second, left_second, orders[1][step])
        kept, came, left_third = halves(third, left_third, orders[2][step])
        first = after(kept_one + came_one.astype(f32), *work_of(step))
        second = kept_two + came_two.astype(f32)
        third = after(kept + came.astype(f32), came_one, came_two)
    both = jnp.concatenate([first, second], axis=first.ndim + axis)
    for step in range(2, count):
        kept_both, came_both, left = halves(both, left, orders[2][step - 2])
        kept, came, left_third = halves(third, left_third, orders[2][step])
        both = after(kept_both + came_both.astype(f32), *work_of(step))
        third = kept + came.astype(f32)
    first = lax.slice_in_dim(both, 0, cut, axis=both.ndim + axis)
    second = lax.slice_in_dim(both, cut, both.shape[axis], axis=both.ndim + axis)
    return first, second, third, results


def cut_in_three(size, unit):
    third = round(0.25 * size / unit) * unit
    first = (size - third + unit) // (2 * unit) * unit
    return first, size - third


def tp_masks():
    return range(1, lax.axis_size("tp"))


def over_cores(array):
    return jnp.concatenate([array] + [from_partner(array, "tp", mask) for mask in tp_masks()], axis=-1)


def lanes_by_index(array):
    count = lax.axis_size("tp")
    pieces = jnp.split(array, count, axis=-1)
    me = lax.axis_index("tp")
    step = 1
    while step < count:
        flipped = [pieces[i ^ step] for i in range(count)]
        pieces = [jnp.where(me & step == 0, a, b) for a, b in zip(pieces, flipped)]
        step *= 2
    return jnp.concatenate(pieces, axis=-1)


def merged(group):
    tops, totals, weighted, targets = (jnp.stack([one[i] for one in group]) for i in range(4))
    top = jnp.max(tops, axis=0)
    shares = jnp.exp(tops - top)
    return jnp.stack(
        [
            top,
            jnp.sum(shares * totals, axis=0),
            jnp.sum(shares * weighted, axis=0),
            jnp.sum(targets, axis=0),
        ]
    )


def in_parts(values):
    high = lax.reduce_precision(values, 8, 7)
    middle = lax.reduce_precision(values - high, 8, 7)
    return high, middle, values - high - middle


def dot(left, right, on_left, on_right, precision=None):
    return lax.dot_general(
        left,
        right,
        (((on_left,), (on_right,)), ((), ())),
        precision=precision,
        preferred_element_type=f32,
    )


def logits_kernel(where, ids, scale, gain, *refs):
    *pieces, head, out, stats, all_features = refs
    step = pl.program_id(0)
    tile = head.shape[0]
    blocks, _, lanes = pieces[0].shape
    features = all_features.shape[0] // blocks

    @pl.when(step == 0)
    def _():
        for device in range(blocks):
            for side in range(2):
                start = device * features
                columns = slice(side * lanes, (side + 1) * lanes)
                for piece in pieces[3 * side : 3 * side + 3]:
                    rows = min(piece.shape[1], (device + 1) * features - start)
                    all_features[start : start + rows, columns] = piece[where[0] ^ device][:rows]
                    start += rows
        columns_of_gain = gain[...].T
        for k in range(gain.shape[0]):
            part = slice(128 * k, 128 * (k + 1))
            values = all_features[part, :].astype(f32) * scale[...] * columns_of_gain[:, k : k + 1]
            all_features[part, :] = values.astype(bf16)
        stats[...] = jnp.zeros_like(stats)
        stats[0:1, :] = jnp.full((1, stats.shape[1]), -jnp.inf, f32)

    logits = jnp.dot(head[...], all_features[...], preferred_element_type=f32)
    out[...] = logits
    entries = lax.broadcasted_iota(i32, logits.shape, 0) + (where[1] + step * tile)
    before = stats[0:1, :]
    top = jnp.maximum(before, jnp.max(logits, axis=0, keepdims=True))
    shrink = jnp.exp(before - top)
    expd = jnp.exp(logits - top)
    stats[0:1, :] = top
    stats[1:2, :] = stats[1:2, :] * shrink + jnp.sum(expd, axis=0, keepdims=True)
    stats[2:3, :] = stats[2:3, :] * shrink + jnp.sum(expd * logits, axis=0, keepdims=True)
    stats[3:4, :] = stats[3:4, :] + jnp.sum(
        jnp.where(entries == ids[...], logits, 0.0), axis=0, keepdims=True
    )


def head_logits(where, ids, scale, gain, pieces, head):
    vocab, tokens = head.shape[0], ids.shape[1]
    tile = 512
    gain = gain.reshape(-1, 128)
    whole = lambda array: pl.BlockSpec(array.shape, lambda i, w: (0,) * array.ndim)
    return pl.pallas_call(
        logits_kernel,
        grid_spec=pltpu.PrefetchScalarGridSpec(
            num_scalar_prefetch=1,
            grid=(vocab // tile,),
            in_specs=[
                whole(ids),
                whole(scale),
                whole(gain),
                *[whole(piece) for piece in pieces],
                pl.BlockSpec((tile, D), lambda i, w: (i, 0)),
            ],
            out_specs=[
                pl.BlockSpec((tile, tokens), lambda i, w: (i, 0)),
                pl.BlockSpec((8, tokens), lambda i, w: (0, 0)),
                pl.BlockSpec((D, tokens), lambda i, w: (0, 0)),
            ],
        ),
        out_shape=[
            jax.ShapeDtypeStruct((vocab, tokens), f32),
            jax.ShapeDtypeStruct((8, tokens), f32),
            jax.ShapeDtypeStruct((D, tokens), bf16),
        ],
        compiler_params=pltpu.CompilerParams(vmem_limit_bytes=44 << 20),
        cost_estimate=pl.CostEstimate(
            flops=2 * vocab * D * tokens,
            bytes_accessed=2 * vocab * D + 4 * D * tokens,
            transcendentals=vocab * tokens,
        ),
    )(where, ids, scale, gain, *pieces, head)


def dfinal_kernel(where, ids, rows, logits, head, kept, sent, plain, turned):
    step = pl.program_id(0)
    vocab, tokens = logits.shape
    lanes = kept.shape[3]

    @pl.when(step == 0)
    def _():
        top, share, coef = (rows[i : i + 1, :] for i in range(3))
        tile = 256
        for start in range(0, vocab, tile):
            probs = jnp.exp(logits[start : start + tile, :] - top) * share
            entries = lax.broadcasted_iota(i32, probs.shape, 0) + (where[1] + start)
            dlogits = coef * (probs - (entries == ids[...]).astype(f32))
            plain[start : start + tile, :] = dlogits.astype(bf16)
            turned[:, start : start + tile] = dlogits.T.astype(bf16)

    product = jnp.dot(turned[...], head[...], preferred_element_type=f32).T
    half = product.shape[0] // 2
    flip = where[0] & 1
    for piece in range(2):
        block = product[piece * half : (piece + 1) * half]
        kept[0, piece ^ flip] = block[:, :lanes]
        sent[0, piece ^ flip] = block[:, lanes:].astype(bf16)


def head_back(where, ids, rows, logits, head, blocks):
    vocab, tokens = logits.shape
    features = D // blocks
    lanes = tokens // 2
    pairs = blocks // 2
    whole = lambda array: pl.BlockSpec(array.shape, lambda i, w: (0,) * array.ndim)
    place = lambda i, w: (i ^ (w[0] >> 1), 0, 0, 0)
    return pl.pallas_call(
        dfinal_kernel,
        grid_spec=pltpu.PrefetchScalarGridSpec(
            num_scalar_prefetch=1,
            grid=(pairs,),
            in_specs=[
                whole(ids),
                whole(rows),
                whole(logits),
                pl.BlockSpec((vocab, 2 * features), lambda i, w: (0, i)),
            ],
            out_specs=[
                pl.BlockSpec((1, 2, features, lanes), place),
                pl.BlockSpec((1, 2, features, lanes), place),
                pl.BlockSpec((vocab, tokens), lambda i, w: (0, 0)),
            ],
            scratch_shapes=[pltpu.VMEM((tokens, vocab), bf16)],
        ),
        out_shape=[
            jax.ShapeDtypeStruct((pairs, 2, features, lanes), f32),
            jax.ShapeDtypeStruct((pairs, 2, features, lanes), bf16),
            jax.ShapeDtypeStruct((vocab, tokens), bf16),
        ],
        compiler_params=pltpu.CompilerParams(vmem_limit_bytes=32 << 20),
        cost_estimate=pl.CostEstimate(
            flops=2 * vocab * D * tokens,
            bytes_accessed=2 * vocab * D + 4 * D * tokens,
            transcendentals=vocab * tokens,
        ),
    )(where, ids, rows, logits, head)


def grad_head_kernel(left, features, *refs):
    out, mark = refs[-2:]
    out[...] = lax.dot_general(
        left[...], features[...], (((1,), (1,)), ((), ())), preferred_element_type=f32
    ).astype(bf16)
    mark[...] = jnp.zeros_like(mark)


def grad_head_rows(left, features, index, count, before):
    vocab, tokens = left.shape
    rows, tile = vocab // count, 1024
    given = () if before is None else (before,)
    return pl.pallas_call(
        grad_head_kernel,
        grid=(D // tile,),
        in_specs=[
            pl.BlockSpec((rows, tokens), lambda i: (index, 0)),
            pl.BlockSpec((tile, tokens), lambda i: (i, 0)),
            *[pl.BlockSpec(memory_space=pl.ANY) for _ in given],
        ],
        out_specs=[
            pl.BlockSpec((rows, tile), lambda i: (index, i)),
            pl.BlockSpec((8, 128), lambda i: (0, 0)),
        ],
        out_shape=[
            jax.ShapeDtypeStruct((vocab, D), bf16),
            jax.ShapeDtypeStruct((8, 128), f32),
        ],
        input_output_aliases={2: 0} if given else {},
        compiler_params=pltpu.CompilerParams(vmem_limit_bytes=20 << 20),
        cost_estimate=pl.CostEstimate(
            flops=2 * rows * D * tokens, bytes_accessed=2 * rows * D + 2 * D * tokens, transcendentals=0
        ),
    )(left, features, *given)


def plain_logits(where, ids, scale, gain, pieces, head):
    blocks, _, lanes = pieces[0].shape
    features = D // blocks
    sides = []
    for i in range(0, len(pieces), 3):
        side = jnp.concatenate(pieces[i : i + 3], axis=1)[:, :features]
        sides.append(side[where[0] ^ jnp.arange(blocks)].reshape(D, lanes))
    all_features = jnp.concatenate(sides, axis=1).astype(f32)
    all_features = (all_features * scale * gain[:, None]).astype(bf16)
    logits = dot(head, all_features, 1, 0)
    top = jnp.max(logits, axis=0)
    expd = jnp.exp(logits - top)
    onehot = (jnp.arange(head.shape[0])[:, None] + where[1]) == ids
    stats = [
        top,
        jnp.sum(expd, axis=0),
        jnp.sum(expd * logits, axis=0),
        jnp.sum(jnp.where(onehot, logits, 0.0), axis=0),
    ]
    return logits, jnp.stack(stats), all_features


def plain_back(where, ids, rows, logits, head, blocks):
    top, share, coef = rows[0], rows[1], rows[2]
    lanes = logits.shape[1] // lax.axis_size("tp")
    onehot = (jnp.arange(head.shape[0])[:, None] + where[1]) == ids
    dlogits = coef * (jnp.exp(logits - top) * share - onehot.astype(f32))
    dlogits = dlogits.astype(bf16)
    product = dot(head, dlogits, 0, 0).reshape(blocks, D // blocks, -1)
    product = product[where[0] ^ jnp.arange(blocks)]
    return product[..., :lanes], product[..., lanes:].astype(bf16), dlogits


def shards(
    prev_hidden,
    token_embed,
    gain_hidden,
    gain_embed,
    gain_final,
    proj_hidden,
    proj_embed,
    head,
    target_ids,
    valid,
    rest_count,
):
    blocks, cores = lax.axis_size("seq"), lax.axis_size("tp")
    me = lax.axis_index("seq")
    rows, width = prev_hidden.shape
    features = proj_hidden.shape[1]
    tokens = rows * blocks
    lanes = tokens // cores

    prev_f = prev_hidden.astype(f32)
    embed_f = token_embed.astype(f32)
    sums = lax.psum(
        jnp.stack([jnp.sum(prev_f * prev_f, axis=-1), jnp.sum(embed_f * embed_f, axis=-1)]), "tp"
    )
    scales = lax.rsqrt(sums / D + epsilon)
    scale_prev, scale_embed = scales[0][:, None], scales[1][:, None]
    normed_prev = (prev_f * scale_prev * gain_hidden).astype(bf16)
    normed_embed = (embed_f * scale_embed * gain_embed).astype(bf16)
    main = round(0.75 * width / 128) * 128
    rest = width - main
    first, second, third, ids_here, valid_here, gain_here = lax.optimization_barrier(
        (
            normed_prev[:, :main],
            normed_embed[:, :main],
            jnp.concatenate([normed_prev[:, main:], normed_embed[:, main:]], axis=1),
            target_ids,
            valid,
            gain_final,
        )
    )
    facts = jnp.stack([ids_here // 256, ids_here % 256, valid_here]).astype(bf16)
    facts = dot(jnp.eye(rows, dtype=bf16), jnp.pad(facts, ((0, 5), (0, 0))), 1, 1).astype(bf16)
    gain_parts = jnp.stack(in_parts(gain_here)).astype(bf16).reshape(rows, -1)
    gain_columns = gain_parts.shape[1]
    facts = jnp.concatenate([facts, gain_parts], axis=1)
    facts = jnp.pad(facts, ((0, 0), (0, 128 - facts.shape[1])))

    first, second, third = gather(first, second, jnp.concatenate([third, facts], axis=1), 1)
    first, second = first.reshape(tokens, main), second.reshape(tokens, main)
    third = third.reshape(tokens, 2 * rest + 128)

    row = lax.broadcasted_iota(i32, (tokens, 1), 0)
    position = (me ^ (row // rows)) * rows + row % rows
    column = lax.broadcasted_iota(i32, (1, tokens), 1)
    order_prev = position == column
    order_embed = position - 1 == column

    from_prev = dot(proj_hidden[:main], first, 0, 1) + dot(proj_hidden[main:], third[:, :rest], 0, 1)
    from_embed = dot(proj_embed[:main], second, 0, 1) + dot(
        proj_embed[main:], third[:, rest : 2 * rest], 0, 1
    )
    facts_all = third[:, 2 * rest :]
    facts_prev = dot(facts_all, order_prev.astype(bf16), 0, 0)
    partial_value = dot(
        jnp.concatenate([from_prev, from_embed], axis=1),
        jnp.concatenate([order_prev, order_embed], axis=0).astype(f32),
        1,
        0,
        lax.Precision.HIGHEST,
    )
    gain_all = facts_all[:, 8 : 8 + gain_columns].reshape(blocks, 3, features).astype(f32)
    gain_all = gain_all[:, 0] + gain_all[:, 1] + gain_all[:, 2]
    block = jnp.arange(blocks)
    gain_all = dot(
        ((me ^ block)[:, None] == block[None, :]).astype(f32), gain_all, 0, 0, lax.Precision.HIGHEST
    ).reshape(D)
    ids_all = (facts_prev[0:1] * 256 + facts_prev[1:2]).astype(i32)
    valid_all = facts_prev[2]
    core = lax.axis_index("tp")
    cut_of = lambda mask: lax.dynamic_slice_in_dim(partial_value, (core ^ mask) * lanes, lanes, 1)
    mixed_f = cut_of(0)
    for mask in tp_masks():
        mixed_f = mixed_f + from_partner(cut_of(mask), "tp", mask)
    mixed_f = mixed_f.astype(bf16).astype(f32)
    mixed = mixed_f.astype(bf16)
    square_parts = jnp.stack(in_parts(jnp.sum(mixed_f * mixed_f, axis=0))).astype(bf16)
    square_parts = jnp.pad(square_parts, ((0, 13), (0, 0)))
    one, two = cut_in_three(features, 16)
    pieces = gather(
        mixed[:one], mixed[one:two], jnp.concatenate([mixed[two:], square_parts], axis=0), 0
    )
    pieces = list(pieces)
    for mask in tp_masks():
        pieces = pieces + [from_partner(piece, "tp", mask) for piece in pieces[:3]]
    squares = [
        jnp.sum(piece[:, features - two :][:, :3].astype(f32), axis=(0, 1)) for piece in pieces[2::3]
    ]
    scale_own = lax.rsqrt(squares[0] / D + epsilon)
    scale_final = lax.rsqrt(jnp.concatenate(squares) / D + epsilon)

    vocab_rows = head.shape[0]
    where = jnp.stack([me, lax.axis_index(("seq", "tp")) * vocab_rows]).astype(i32)
    ids = lanes_by_index(ids_all)
    valid_lanes = lanes_by_index(valid_all)
    fits = cores == 2 and lanes % 128 == 0 and vocab_rows % 512 == 0 and 2 * features % 128 == 0
    forward = head_logits if fits else plain_logits
    logits, stats, final_all = forward(where, ids, scale_final[None, :], gain_all, pieces, head)
    stats = stats[:4]
    for step in range(0, bits_of("seq"), 2):
        masks = [k << step for k in range(1, min(4, blocks >> step))]
        stats = merged([stats] + [from_partner(stats, "seq", mask) for mask in masks])
    stats = lanes_by_index(stats)
    stats = merged([stats] + [from_partner(stats, "tp", mask) for mask in tp_masks()])
    row_top, row_total, row_weighted, target_logit = lanes_by_index(stats)
    count = jnp.sum(valid_all) + rest_count[0].astype(f32)
    coef = loss_scale * valid_lanes / count
    row_values = jnp.stack([row_top, 1.0 / row_total, coef])
    row_values = jnp.pad(row_values, ((0, 5), (0, 0)))
    back = head_back if fits else plain_back
    kept, sent, dlogits = back(where, ids, row_values, logits, head, blocks)
    dfinal = kept.reshape(blocks, features, lanes)
    for mask in tp_masks():
        piece = sent[..., (mask - 1) * lanes : mask * lanes]
        dfinal = dfinal + from_partner(piece, "tp", mask).astype(f32).reshape(dfinal.shape)

    def grad_head_piece(index):
        if fits:
            return lambda results: grad_head_rows(
                dlogits, final_all, index, 4, results[-1] if results else None
            )
        return lambda results: (dot(dlogits, final_all, 1, 1).astype(bf16), dlogits)

    early = [grad_head_piece(index) for index in range(2 if fits else 1)]
    *dfinal, results = scatter(dfinal[:, :one], dfinal[:, one:two], dfinal[:, two:], 1, early)
    dfinal = jnp.concatenate(dfinal, axis=0)

    total_dot = (coef * (row_weighted / row_total - target_logit))[:lanes] / scale_own
    dmixed = (
        scale_own * (dfinal * gain_final[:, None]) - mixed_f * (scale_own**3 * (total_dot / D))
    ).astype(bf16)
    dmixed = lanes_by_index(over_cores(dmixed))
    dmixed_prev = dot(dmixed, order_prev.astype(bf16), 1, 1).astype(bf16)
    dmixed_embed = dot(dmixed, order_embed.astype(bf16), 1, 1).astype(bf16)
    back_prev = dot(dmixed_prev, proj_hidden, 0, 1).reshape(blocks, rows, width)
    back_embed = dot(dmixed_embed, proj_embed, 0, 1).reshape(blocks, rows, width)

    def grad_head_end(before):
        grad_head, mark = results[-1], dlogits
        if fits:
            for index in (2, 3):
                grad_head, mark = grad_head_rows(dlogits, final_all, index, 4, grad_head)
        return grad_head, mark

    def grad_proj(rows_in, rows_rest, back):
        rows_all = jnp.concatenate([rows_in, rows_rest], axis=1)
        out = dot(rows_all, back, 0, 1).astype(bf16)
        return out, out[:1, :1]

    one, two, three, results = scatter(
        back_prev[..., :main],
        back_embed[..., :main],
        jnp.concatenate([back_prev[..., main:], back_embed[..., main:]], axis=-1),
        2,
        [
            grad_head_end,
            lambda before: grad_proj(first, third[:, :rest], dmixed_prev),
            lambda before: grad_proj(second, third[:, rest : 2 * rest], dmixed_embed),
        ],
    )
    grad_head, grad_proj_hidden, grad_proj_embed = results
    grad_prev = jnp.concatenate([one, three[:, :rest]], axis=1) * gain_hidden
    grad_embed = jnp.concatenate([two, three[:, rest:]], axis=1) * gain_embed
    dots = lax.psum(
        jnp.stack([jnp.sum(grad_prev * prev_f, axis=-1), jnp.sum(grad_embed * embed_f, axis=-1)]),
        "tp",
    )
    grad_prev_hidden = (
        scale_prev * grad_prev - prev_f * (scale_prev**3 * (dots[0] / D)[:, None])
    ).astype(bf16)
    grad_token_embed = (
        scale_embed * grad_embed - embed_f * (scale_embed**3 * (dots[1] / D)[:, None])
    ).astype(bf16)
    return (grad_prev_hidden, grad_token_embed, grad_proj_hidden, grad_proj_embed, grad_head)


def solution(mesh):
    return jax.shard_map(
        shards,
        mesh=mesh,
        in_specs=(
            P("seq", "tp"),
            P("seq", "tp"),
            P("tp"),
            P("tp"),
            P("seq"),
            P("tp", "seq"),
            P("tp", "seq"),
            P(("seq", "tp"), None),
            P("seq"),
            P("seq"),
            P(),
        ),
        out_specs=(
            P("seq", "tp"),
            P("seq", "tp"),
            P("tp", "seq"),
            P("tp", "seq"),
            P(("seq", "tp"), None),
        ),
        check_vma=False,
    )
```

```python
import jax
import jax.numpy as jnp
from jax import lax
from jax.experimental import pallas as pl
from jax.experimental.pallas import tpu as pltpu
from jax.sharding import PartitionSpec as P

D = 7168


loss_scale = 4096.0
epsilon = 1e-06

f32 = jnp.float32
bf16 = jnp.bfloat16
i32 = jnp.int32


def from_partner(array, axis, mask):
    size = lax.axis_size(axis)
    return lax.ppermute(array, axis, [(i, i ^ mask) for i in range(size)])


def bits_of(axis):
    return lax.axis_size(axis).bit_length() - 1


def zero_of(array, shape):
    array = array[(0,) * (array.ndim - len(shape))] if array.ndim > len(shape) else array
    array = array[tuple(slice(0, size) for size in shape[len(shape) - array.ndim :])]
    return array * 0


def in_order(array, order):
    count = len(order)
    dims = [count - 1 - order.index(bit) for bit in reversed(range(count))]
    array = array.transpose(dims + list(range(count, array.ndim)))
    return array.reshape((1 << count,) + array.shape[count:])


def gather(first, second, third):
    high = list(reversed(range(2, bits_of("seq"))))
    came = []
    for bit in high:
        came = [from_partner(first, "seq", 1 << bit), from_partner(second, "seq", 1 << bit)]
        if bit == high[0]:
            third = third + zero_of(came[0], third.shape) + zero_of(came[1], third.shape)
        first, second = jnp.stack([first, came[0]]), jnp.stack([second, came[1]])
    for bit in (0, 1):
        first = jnp.stack([first, from_partner(first, "seq", 2 >> bit)])
        second = jnp.stack([second, from_partner(second, "seq", 1 << bit)])
        third = jnp.stack([third, from_partner(third, "seq", 1 << bit)])
    for block in came:
        third = third + zero_of(block, third.shape[2:])
    for bit in high:
        third = jnp.stack([third, from_partner(third, "seq", 1 << bit)])
    return in_order(first, high + [1, 0]), in_order(second, high + [0, 1]), in_order(third, [0, 1] + high)


def scatter(arrays, beside=()):
    count = bits_of("seq")
    arrays = [array.reshape((2,) * count + array.shape[1:]) for array in arrays]
    low, high = [0, 1], list(range(2, count))
    orders = [low + high, low[::-1] + high, high + low[::-1]]
    left = [list(reversed(range(count))) for _ in arrays]
    results = []
    last = None
    for step in range(count):
        kept, came = [], []
        for k, order in enumerate(orders):
            bit = order[step]
            dim = left[k].index(bit)
            left[k].remove(bit)
            sent = lax.index_in_dim(arrays[k], 1, dim, keepdims=False).astype(bf16)
            kept.append(lax.index_in_dim(arrays[k], 0, dim, keepdims=False).astype(f32))
            came.append(from_partner(sent, "seq", 1 << bit))
        sums = [one + other.astype(f32) for one, other in zip(kept, came)]
        if step < len(beside):
            result, zeros = beside[step](last, sums[0].shape, results)
            results.append(result)
            if zeros is not None:
                sums[0] = sums[0] + zeros
        if step < 2:
            sums[2] = sums[2] + zero_of(came[0], sums[2].shape) + zero_of(came[1], sums[2].shape)
        arrays, last = sums, came[0]
    return arrays, results


def cut_in_three(size, unit):
    third = round(0.25 * size / unit) * unit
    first = (size - third + unit) // (2 * unit) * unit
    return first, size - third


def tp_masks():
    return range(1, lax.axis_size("tp"))


def over_cores(array):
    return jnp.concatenate([array] + [from_partner(array, "tp", mask) for mask in tp_masks()], axis=-1)


def lanes_by_index(array):
    count = lax.axis_size("tp")
    pieces = jnp.split(array, count, axis=-1)
    me = lax.axis_index("tp")
    step = 1
    while step < count:
        flipped = [pieces[i ^ step] for i in range(count)]
        pieces = [jnp.where(me & step == 0, a, b) for a, b in zip(pieces, flipped)]
        step *= 2
    return jnp.concatenate(pieces, axis=-1)


def merged(group):
    tops, totals, weighted, targets = (jnp.stack([one[i] for one in group]) for i in range(4))
    top = jnp.max(tops, axis=0)
    shares = jnp.exp(tops - top)
    return jnp.stack(
        [
            top,
            jnp.sum(shares * totals, axis=0),
            jnp.sum(shares * weighted, axis=0),
            jnp.sum(targets, axis=0),
        ]
    )


def in_parts(values):
    high = lax.reduce_precision(values, 8, 7)
    middle = lax.reduce_precision(values - high, 8, 7)
    return high, middle, values - high - middle


def dot(left, right, on_left, on_right, precision=None):
    return lax.dot_general(
        left,
        right,
        (((on_left,), (on_right,)), ((), ())),
        precision=precision,
        preferred_element_type=f32,
    )


def logits_kernel(where, ids, scale, gain, *refs):
    *pieces, head, out, stats, all_features = refs
    step = pl.program_id(0)
    tile = head.shape[0]
    blocks, _, lanes = pieces[0].shape
    features = all_features.shape[0] // blocks

    @pl.when(step == 0)
    def _():
        for device in range(blocks):
            for side in range(2):
                start = device * features
                columns = slice(side * lanes, (side + 1) * lanes)
                for piece in pieces[3 * side : 3 * side + 3]:
                    rows = min(piece.shape[1], (device + 1) * features - start)
                    all_features[start : start + rows, columns] = piece[where[0] ^ device][:rows]
                    start += rows
        columns_of_gain = gain[...].T
        for k in range(gain.shape[0]):
            part = slice(128 * k, 128 * (k + 1))
            values = all_features[part, :].astype(f32) * scale[...] * columns_of_gain[:, k : k + 1]
            all_features[part, :] = values.astype(bf16)
        stats[...] = jnp.zeros_like(stats)
        stats[0:1, :] = jnp.full((1, stats.shape[1]), -jnp.inf, f32)

    logits = jnp.dot(head[...], all_features[...], preferred_element_type=f32)
    out[...] = logits
    entries = lax.broadcasted_iota(i32, logits.shape, 0) + (where[1] + step * tile)
    before = stats[0:1, :]
    top = jnp.maximum(before, jnp.max(logits, axis=0, keepdims=True))
    shrink = jnp.exp(before - top)
    expd = jnp.exp(logits - top)
    stats[0:1, :] = top
    stats[1:2, :] = stats[1:2, :] * shrink + jnp.sum(expd, axis=0, keepdims=True)
    stats[2:3, :] = stats[2:3, :] * shrink + jnp.sum(expd * logits, axis=0, keepdims=True)
    stats[3:4, :] = stats[3:4, :] + jnp.sum(
        jnp.where(entries == ids[...], logits, 0.0), axis=0, keepdims=True
    )


def head_logits(where, ids, scale, gain, pieces, head):
    vocab, tokens = head.shape[0], ids.shape[1]
    tile = 512
    gain = gain.reshape(-1, 128)
    whole = lambda array: pl.BlockSpec(array.shape, lambda i, w: (0,) * array.ndim)
    return pl.pallas_call(
        logits_kernel,
        grid_spec=pltpu.PrefetchScalarGridSpec(
            num_scalar_prefetch=1,
            grid=(vocab // tile,),
            in_specs=[
                whole(ids),
                whole(scale),
                whole(gain),
                *[whole(piece) for piece in pieces],
                pl.BlockSpec((tile, D), lambda i, w: (i, 0)),
            ],
            out_specs=[
                pl.BlockSpec((tile, tokens), lambda i, w: (i, 0)),
                pl.BlockSpec((8, tokens), lambda i, w: (0, 0)),
                pl.BlockSpec((D, tokens), lambda i, w: (0, 0)),
            ],
        ),
        out_shape=[
            jax.ShapeDtypeStruct((vocab, tokens), f32),
            jax.ShapeDtypeStruct((8, tokens), f32),
            jax.ShapeDtypeStruct((D, tokens), bf16),
        ],
        compiler_params=pltpu.CompilerParams(vmem_limit_bytes=44 << 20),
        cost_estimate=pl.CostEstimate(
            flops=2 * vocab * D * tokens,
            bytes_accessed=2 * vocab * D + 4 * D * tokens,
            transcendentals=vocab * tokens,
        ),
    )(where, ids, scale, gain, *pieces, head)


def dfinal_kernel(where, ids, rows, logits, head, kept, sent, plain, turned):
    step = pl.program_id(0)
    vocab, tokens = logits.shape
    lanes = kept.shape[3]

    @pl.when(step == 0)
    def _():
        top, share, coef = (rows[i : i + 1, :] for i in range(3))
        tile = 256
        for start in range(0, vocab, tile):
            probs = jnp.exp(logits[start : start + tile, :] - top) * share
            entries = lax.broadcasted_iota(i32, probs.shape, 0) + (where[1] + start)
            dlogits = coef * (probs - (entries == ids[...]).astype(f32))
            plain[start : start + tile, :] = dlogits.astype(bf16)
            turned[:, start : start + tile] = dlogits.T.astype(bf16)

    product = jnp.dot(turned[...], head[...], preferred_element_type=f32).T
    half = product.shape[0] // 2
    flip = where[0] & 1
    for piece in range(2):
        block = product[piece * half : (piece + 1) * half]
        kept[0, piece ^ flip] = block[:, :lanes]
        sent[0, piece ^ flip] = block[:, lanes:].astype(bf16)


def head_back(where, ids, rows, logits, head, blocks):
    vocab, tokens = logits.shape
    features = D // blocks
    lanes = tokens // 2
    pairs = blocks // 2
    whole = lambda array: pl.BlockSpec(array.shape, lambda i, w: (0,) * array.ndim)
    place = lambda i, w: (i ^ (w[0] >> 1), 0, 0, 0)
    return pl.pallas_call(
        dfinal_kernel,
        grid_spec=pltpu.PrefetchScalarGridSpec(
            num_scalar_prefetch=1,
            grid=(pairs,),
            in_specs=[
                whole(ids),
                whole(rows),
                whole(logits),
                pl.BlockSpec((vocab, 2 * features), lambda i, w: (0, i)),
            ],
            out_specs=[
                pl.BlockSpec((1, 2, features, lanes), place),
                pl.BlockSpec((1, 2, features, lanes), place),
                pl.BlockSpec((vocab, tokens), lambda i, w: (0, 0)),
            ],
            scratch_shapes=[pltpu.VMEM((tokens, vocab), bf16)],
        ),
        out_shape=[
            jax.ShapeDtypeStruct((pairs, 2, features, lanes), f32),
            jax.ShapeDtypeStruct((pairs, 2, features, lanes), bf16),
            jax.ShapeDtypeStruct((vocab, tokens), bf16),
        ],
        compiler_params=pltpu.CompilerParams(vmem_limit_bytes=32 << 20),
        cost_estimate=pl.CostEstimate(
            flops=2 * vocab * D * tokens,
            bytes_accessed=2 * vocab * D + 4 * D * tokens,
            transcendentals=vocab * tokens,
        ),
    )(where, ids, rows, logits, head)


def grad_head_kernel(left, features, *refs):
    out, zeros = refs[-2:]
    out[...] = lax.dot_general(
        left[...], features[...], (((1,), (1,)), ((), ())), preferred_element_type=f32
    ).astype(bf16)

    @pl.when(pl.program_id(0) == 0)
    def _():
        zeros[...] = jnp.zeros_like(zeros)


def grad_head_rows(left, features, index, count, later_than, shape, before):
    vocab, tokens = left.shape
    rows, tile = vocab // count, 1024
    given = (later_than,) if before is None else (later_than, before)
    return pl.pallas_call(
        grad_head_kernel,
        grid=(D // tile,),
        in_specs=[
            pl.BlockSpec((rows, tokens), lambda i: (index, 0)),
            pl.BlockSpec((tile, tokens), lambda i: (i, 0)),
            *[pl.BlockSpec(memory_space=pl.ANY) for _ in given],
        ],
        out_specs=[
            pl.BlockSpec((rows, tile), lambda i: (index, i)),
            pl.BlockSpec(shape, lambda i: (0,) * len(shape)),
        ],
        out_shape=[
            jax.ShapeDtypeStruct((vocab, D), bf16),
            jax.ShapeDtypeStruct(shape, f32),
        ],
        input_output_aliases={3: 0} if before is not None else {},
        compiler_params=pltpu.CompilerParams(vmem_limit_bytes=20 << 20),
        cost_estimate=pl.CostEstimate(
            flops=2 * rows * D * tokens, bytes_accessed=2 * rows * D + 2 * D * tokens, transcendentals=0
        ),
    )(left, features, *given)


def plain_logits(where, ids, scale, gain, pieces, head):
    blocks, _, lanes = pieces[0].shape
    features = D // blocks
    sides = []
    for i in range(0, len(pieces), 3):
        side = jnp.concatenate(pieces[i : i + 3], axis=1)[:, :features]
        sides.append(side[where[0] ^ jnp.arange(blocks)].reshape(D, lanes))
    all_features = jnp.concatenate(sides, axis=1).astype(f32)
    all_features = (all_features * scale * gain[:, None]).astype(bf16)
    logits = dot(head, all_features, 1, 0)
    top = jnp.max(logits, axis=0)
    expd = jnp.exp(logits - top)
    onehot = (jnp.arange(head.shape[0])[:, None] + where[1]) == ids
    stats = [
        top,
        jnp.sum(expd, axis=0),
        jnp.sum(expd * logits, axis=0),
        jnp.sum(jnp.where(onehot, logits, 0.0), axis=0),
    ]
    return logits, jnp.stack(stats), all_features


def plain_back(where, ids, rows, logits, head, blocks):
    top, share, coef = rows[0], rows[1], rows[2]
    lanes = logits.shape[1] // lax.axis_size("tp")
    onehot = (jnp.arange(head.shape[0])[:, None] + where[1]) == ids
    dlogits = coef * (jnp.exp(logits - top) * share - onehot.astype(f32))
    dlogits = dlogits.astype(bf16)
    product = dot(head, dlogits, 0, 0).reshape(blocks, D // blocks, -1)
    product = product[where[0] ^ jnp.arange(blocks)]
    return product[..., :lanes], product[..., lanes:].astype(bf16), dlogits


def shards(
    prev_hidden,
    token_embed,
    gain_hidden,
    gain_embed,
    gain_final,
    proj_hidden,
    proj_embed,
    head,
    target_ids,
    valid,
    rest_count,
):
    blocks, cores = lax.axis_size("seq"), lax.axis_size("tp")
    me = lax.axis_index("seq")
    rows, width = prev_hidden.shape
    features = proj_hidden.shape[1]
    tokens = rows * blocks
    lanes = tokens // cores

    prev_f = prev_hidden.astype(f32)
    embed_f = token_embed.astype(f32)
    sums = lax.psum(
        jnp.stack([jnp.sum(prev_f * prev_f, axis=-1), jnp.sum(embed_f * embed_f, axis=-1)]), "tp"
    )
    scales = lax.rsqrt(sums / D + epsilon)
    scale_prev, scale_embed = scales[0][:, None], scales[1][:, None]
    normed_prev = (prev_f * scale_prev * gain_hidden).astype(bf16)
    normed_embed = (embed_f * scale_embed * gain_embed).astype(bf16)
    main = round(0.75 * width / 128) * 128
    rest = width - main
    first, second, third, ids_here, valid_here, gain_here = lax.optimization_barrier(
        (
            normed_prev[:, :main],
            normed_embed[:, :main],
            jnp.concatenate([normed_prev[:, main:], normed_embed[:, main:]], axis=1),
            target_ids,
            valid,
            gain_final,
        )
    )
    facts = jnp.stack([ids_here // 256, ids_here % 256, valid_here]).astype(bf16)
    facts = dot(jnp.eye(rows, dtype=bf16), jnp.pad(facts, ((0, 5), (0, 0))), 1, 1).astype(bf16)
    gain_parts = jnp.stack(in_parts(gain_here)).astype(bf16).reshape(rows, -1)
    gain_columns = gain_parts.shape[1]
    facts = jnp.concatenate([facts, gain_parts], axis=1)
    facts = jnp.pad(facts, ((0, 0), (0, 128 - facts.shape[1])))

    first, second, third = gather(first, second, jnp.concatenate([third, facts], axis=1))
    first, second = first.reshape(tokens, main), second.reshape(tokens, main)
    third = third.reshape(tokens, 2 * rest + 128)

    row = lax.broadcasted_iota(i32, (tokens, 1), 0)
    position = (me ^ (row // rows)) * rows + row % rows
    column = lax.broadcasted_iota(i32, (1, tokens), 1)
    order_prev = position == column
    order_embed = position - 1 == column

    from_prev = dot(proj_hidden[:main], first, 0, 1) + dot(proj_hidden[main:], third[:, :rest], 0, 1)
    from_embed = dot(proj_embed[:main], second, 0, 1) + dot(
        proj_embed[main:], third[:, rest : 2 * rest], 0, 1
    )
    facts_all = third[:, 2 * rest :]
    facts_prev = dot(facts_all, order_prev.astype(bf16), 0, 0)
    partial_value = dot(
        jnp.concatenate([from_prev, from_embed], axis=1),
        jnp.concatenate([order_prev, order_embed], axis=0).astype(f32),
        1,
        0,
        lax.Precision.HIGHEST,
    )
    gain_all = facts_all[:, 8 : 8 + gain_columns].reshape(blocks, 3, features).astype(f32)
    gain_all = gain_all[:, 0] + gain_all[:, 1] + gain_all[:, 2]
    block = jnp.arange(blocks)
    gain_all = dot(
        ((me ^ block)[:, None] == block[None, :]).astype(f32), gain_all, 0, 0, lax.Precision.HIGHEST
    ).reshape(D)
    ids_all = (facts_prev[0:1] * 256 + facts_prev[1:2]).astype(i32)
    valid_all = facts_prev[2]
    core = lax.axis_index("tp")
    cut_of = lambda mask: lax.dynamic_slice_in_dim(partial_value, (core ^ mask) * lanes, lanes, 1)
    mixed_f = cut_of(0)
    for mask in tp_masks():
        mixed_f = mixed_f + from_partner(cut_of(mask), "tp", mask)
    mixed_f = mixed_f.astype(bf16).astype(f32)
    mixed = mixed_f.astype(bf16)
    square_parts = jnp.stack(in_parts(jnp.sum(mixed_f * mixed_f, axis=0))).astype(bf16)
    square_parts = jnp.pad(square_parts, ((0, 13), (0, 0)))
    one, two = cut_in_three(features, 16)
    pieces = gather(
        mixed[:one], mixed[one:two], jnp.concatenate([mixed[two:], square_parts], axis=0)
    )
    pieces = list(pieces)
    for mask in tp_masks():
        pieces = pieces + [from_partner(piece, "tp", mask) for piece in pieces[:3]]
    squares = [
        jnp.sum(piece[:, features - two :][:, :3].astype(f32), axis=(0, 1)) for piece in pieces[2::3]
    ]
    scale_own = lax.rsqrt(squares[0] / D + epsilon)
    scale_final = lax.rsqrt(jnp.concatenate(squares) / D + epsilon)

    vocab_rows = head.shape[0]
    where = jnp.stack([me, lax.axis_index(("seq", "tp")) * vocab_rows]).astype(i32)
    ids = lanes_by_index(ids_all)
    valid_lanes = lanes_by_index(valid_all)
    fits = cores == 2 and lanes % 128 == 0 and vocab_rows % 512 == 0 and 2 * features % 128 == 0
    forward = head_logits if fits else plain_logits
    logits, stats, final_all = forward(where, ids, scale_final[None, :], gain_all, pieces, head)
    stats = stats[:4]
    for step in range(0, bits_of("seq"), 2):
        masks = [k << step for k in range(1, min(4, blocks >> step))]
        stats = merged([stats] + [from_partner(stats, "seq", mask) for mask in masks])
    stats = lanes_by_index(stats)
    stats = merged([stats] + [from_partner(stats, "tp", mask) for mask in tp_masks()])
    row_top, row_total, row_weighted, target_logit = lanes_by_index(stats)
    count = jnp.sum(valid_all) + rest_count[0].astype(f32)
    coef = loss_scale * valid_lanes / count
    row_values = jnp.stack([row_top, 1.0 / row_total, coef])
    row_values = jnp.pad(row_values, ((0, 5), (0, 0)))
    back = head_back if fits else plain_back
    kept, sent, dlogits = back(where, ids, row_values, logits, head, blocks)
    dfinal = kept.reshape(blocks, features, lanes)
    for mask in tp_masks():
        piece = sent[..., (mask - 1) * lanes : mask * lanes]
        from_core = from_partner(piece, "tp", mask)
        dfinal = dfinal + from_core.astype(f32).reshape(dfinal.shape)

    def grad_head_piece(index, tied):
        def work(last, shape, results):
            if not fits:
                return dot(dlogits, final_all, 1, 1).astype(bf16), None
            before = results[-1] if results else None
            shape = shape if tied else (8, 128)
            out, zeros = grad_head_rows(
                dlogits, final_all, index, 4, from_core if last is None else last, shape, before
            )
            return out, (zeros if tied else None)

        return work

    early = [grad_head_piece(index, index == 1) for index in range(2 if fits else 1)]
    dfinal, results = scatter([dfinal[:, :one], dfinal[:, one:two], dfinal[:, two:]], early)
    dfinal = jnp.concatenate(dfinal, axis=0)

    total_dot = (coef * (row_weighted / row_total - target_logit))[:lanes] / scale_own
    dmixed = (
        scale_own * (dfinal * gain_final[:, None]) - mixed_f * (scale_own**3 * (total_dot / D))
    ).astype(bf16)
    dmixed = lanes_by_index(over_cores(dmixed))
    dmixed_prev = dot(dmixed, order_prev.astype(bf16), 1, 1).astype(bf16)
    dmixed_embed = dot(dmixed, order_embed.astype(bf16), 1, 1).astype(bf16)
    back_prev = dot(dmixed_prev, proj_hidden, 0, 1).reshape(blocks, rows, width)
    back_embed = dot(dmixed_embed, proj_embed, 0, 1).reshape(blocks, rows, width)

    def grad_head_end(last, shape, before):
        grad_head = results[-1]
        if fits:
            for index in (2, 3):
                grad_head, _ = grad_head_rows(
                    dlogits, final_all, index, 4, dmixed_prev, (8, 128), grad_head
                )
        return grad_head, None

    def grad_proj(rows_in, rows_rest, back):
        rows_all = jnp.concatenate([rows_in, rows_rest], axis=1)
        return dot(rows_all, back, 0, 1).astype(bf16), None

    (one, two, three), results = scatter(
        [
            back_prev[..., :main],
            back_embed[..., :main],
            jnp.concatenate([back_prev[..., main:], back_embed[..., main:]], axis=-1),
        ],
        [
            grad_head_end,
            lambda *_: grad_proj(first, third[:, :rest], dmixed_prev),
            lambda *_: grad_proj(second, third[:, rest : 2 * rest], dmixed_embed),
        ],
    )
    grad_head, grad_proj_hidden, grad_proj_embed = results
    grad_prev = jnp.concatenate([one, three[:, :rest]], axis=1) * gain_hidden
    grad_embed = jnp.concatenate([two, three[:, rest:]], axis=1) * gain_embed
    dots = lax.psum(
        jnp.stack([jnp.sum(grad_prev * prev_f, axis=-1), jnp.sum(grad_embed * embed_f, axis=-1)]),
        "tp",
    )
    grad_prev_hidden = (
        scale_prev * grad_prev - prev_f * (scale_prev**3 * (dots[0] / D)[:, None])
    ).astype(bf16)
    grad_token_embed = (
        scale_embed * grad_embed - embed_f * (scale_embed**3 * (dots[1] / D)[:, None])
    ).astype(bf16)
    return (grad_prev_hidden, grad_token_embed, grad_proj_hidden, grad_proj_embed, grad_head)


def solution(mesh):
    return jax.shard_map(
        shards,
        mesh=mesh,
        in_specs=(
            P("seq", "tp"),
            P("seq", "tp"),
            P("tp"),
            P("tp"),
            P("seq"),
            P("tp", "seq"),
            P("tp", "seq"),
            P(("seq", "tp"), None),
            P("seq"),
            P("seq"),
            P(),
        ),
        out_specs=(
            P("seq", "tp"),
            P("seq", "tp"),
            P("tp", "seq"),
            P("tp", "seq"),
            P(("seq", "tp"), None),
        ),
        check_vma=False,
    )
```

```python
import jax
import jax.numpy as jnp
from jax import lax
from jax.experimental import pallas as pl
from jax.experimental.pallas import tpu as pltpu
from jax.sharding import PartitionSpec as P

D = 7168


loss_scale = 4096.0
epsilon = 1e-06

f32 = jnp.float32
bf16 = jnp.bfloat16
i32 = jnp.int32


def from_partner(array, axis, mask):
    size = lax.axis_size(axis)
    return lax.ppermute(array, axis, [(i, i ^ mask) for i in range(size)])


def bits_of(axis):
    return lax.axis_size(axis).bit_length() - 1


def zero_of(array, shape):
    array = array[(0,) * (array.ndim - len(shape))] if array.ndim > len(shape) else array
    array = array[tuple(slice(0, size) for size in shape[len(shape) - array.ndim :])]
    return array * 0


def in_order(array, order):
    count = len(order)
    dims = [count - 1 - order.index(bit) for bit in reversed(range(count))]
    array = array.transpose(dims + list(range(count, array.ndim)))
    return array.reshape((1 << count,) + array.shape[count:])


def gather(first, second, third):
    high = list(reversed(range(2, bits_of("seq"))))
    array_shape = third.shape
    came = []
    for bit in high:
        came = [from_partner(first, "seq", 1 << bit), from_partner(second, "seq", 1 << bit)]
        if bit == high[0]:
            third = third + zero_of(came[0], third.shape) + zero_of(came[1], third.shape)
        first, second = jnp.stack([first, came[0]]), jnp.stack([second, came[1]])
    waits = [came]
    for bit in (0, 1):
        waits.append([from_partner(first, "seq", 2 >> bit), from_partner(second, "seq", 1 << bit)])
        first, second = jnp.stack([first, waits[-1][0]]), jnp.stack([second, waits[-1][1]])
        third = jnp.stack([third, from_partner(third, "seq", 1 << bit)])
    for step, bit in enumerate(high):
        for block in waits[step] if step < 2 else ():
            third = third + zero_of(block, array_shape)
        third = jnp.stack([third, from_partner(third, "seq", 1 << bit)])
    return in_order(first, high + [1, 0]), in_order(second, high + [0, 1]), in_order(third, [0, 1] + high)


def scatter(arrays, beside=()):
    count = bits_of("seq")
    arrays = [array.reshape((2,) * count + array.shape[1:]) for array in arrays]
    low, high = [0, 1], list(range(2, count))
    orders = [low + high, low[::-1] + high, high + low[::-1]]
    left = [list(reversed(range(count))) for _ in arrays]
    results = []
    last = None
    for step in range(count):
        kept, came = [], []
        for k, order in enumerate(orders):
            bit = order[step]
            dim = left[k].index(bit)
            left[k].remove(bit)
            sent = lax.index_in_dim(arrays[k], 1, dim, keepdims=False).astype(bf16)
            kept.append(lax.index_in_dim(arrays[k], 0, dim, keepdims=False).astype(f32))
            came.append(from_partner(sent, "seq", 1 << bit))
        sums = [one + other.astype(f32) for one, other in zip(kept, came)]
        if step < len(beside):
            result, zeros = beside[step](came[2] if last is None else last, sums[0].shape, results)
            results.append(result)
            if zeros is not None:
                sums[0] = sums[0] + zeros
        if step < 2:
            sums[2] = sums[2] + zero_of(came[0], sums[2].shape) + zero_of(came[1], sums[2].shape)
        arrays, last = sums, came[0]
    return arrays, results


def cut_in_three(size, unit):
    third = round(0.25 * size / unit) * unit
    first = (size - third + unit) // (2 * unit) * unit
    return first, size - third


def tp_masks():
    return range(1, lax.axis_size("tp"))


def over_cores(array):
    return jnp.concatenate([array] + [from_partner(array, "tp", mask) for mask in tp_masks()], axis=-1)


def lanes_by_index(array):
    count = lax.axis_size("tp")
    pieces = jnp.split(array, count, axis=-1)
    me = lax.axis_index("tp")
    step = 1
    while step < count:
        flipped = [pieces[i ^ step] for i in range(count)]
        pieces = [jnp.where(me & step == 0, a, b) for a, b in zip(pieces, flipped)]
        step *= 2
    return jnp.concatenate(pieces, axis=-1)


def merged(group):
    tops, totals, weighted, targets = (jnp.stack([one[i] for one in group]) for i in range(4))
    top = jnp.max(tops, axis=0)
    shares = jnp.exp(tops - top)
    return jnp.stack(
        [
            top,
            jnp.sum(shares * totals, axis=0),
            jnp.sum(shares * weighted, axis=0),
            jnp.sum(targets, axis=0),
        ]
    )


def in_parts(values):
    high = lax.reduce_precision(values, 8, 7)
    middle = lax.reduce_precision(values - high, 8, 7)
    return high, middle, values - high - middle


def dot(left, right, on_left, on_right, precision=None):
    return lax.dot_general(
        left,
        right,
        (((on_left,), (on_right,)), ((), ())),
        precision=precision,
        preferred_element_type=f32,
    )


def logits_kernel(where, ids, scale, gain, *refs):
    *pieces, head, out, stats, all_features = refs
    step = pl.program_id(0)
    tile = head.shape[0]
    blocks, _, lanes = pieces[0].shape
    features = all_features.shape[0] // blocks

    @pl.when(step == 0)
    def _():
        for device in range(blocks):
            for side in range(2):
                start = device * features
                columns = slice(side * lanes, (side + 1) * lanes)
                for piece in pieces[3 * side : 3 * side + 3]:
                    rows = min(piece.shape[1], (device + 1) * features - start)
                    all_features[start : start + rows, columns] = piece[where[0] ^ device][:rows]
                    start += rows
        columns_of_gain = gain[...].T
        for k in range(gain.shape[0]):
            part = slice(128 * k, 128 * (k + 1))
            values = all_features[part, :].astype(f32) * scale[...] * columns_of_gain[:, k : k + 1]
            all_features[part, :] = values.astype(bf16)
        stats[...] = jnp.zeros_like(stats)
        stats[0:1, :] = jnp.full((1, stats.shape[1]), -jnp.inf, f32)

    logits = jnp.dot(head[...], all_features[...], preferred_element_type=f32)
    out[...] = logits
    entries = lax.broadcasted_iota(i32, logits.shape, 0) + (where[1] + step * tile)
    before = stats[0:1, :]
    top = jnp.maximum(before, jnp.max(logits, axis=0, keepdims=True))
    shrink = jnp.exp(before - top)
    expd = jnp.exp(logits - top)
    stats[0:1, :] = top
    stats[1:2, :] = stats[1:2, :] * shrink + jnp.sum(expd, axis=0, keepdims=True)
    stats[2:3, :] = stats[2:3, :] * shrink + jnp.sum(expd * logits, axis=0, keepdims=True)
    stats[3:4, :] = stats[3:4, :] + jnp.sum(
        jnp.where(entries == ids[...], logits, 0.0), axis=0, keepdims=True
    )


def head_logits(where, ids, scale, gain, pieces, head):
    vocab, tokens = head.shape[0], ids.shape[1]
    tile = 512
    gain = gain.reshape(-1, 128)
    whole = lambda array: pl.BlockSpec(array.shape, lambda i, w: (0,) * array.ndim)
    return pl.pallas_call(
        logits_kernel,
        grid_spec=pltpu.PrefetchScalarGridSpec(
            num_scalar_prefetch=1,
            grid=(vocab // tile,),
            in_specs=[
                whole(ids),
                whole(scale),
                whole(gain),
                *[whole(piece) for piece in pieces],
                pl.BlockSpec((tile, D), lambda i, w: (i, 0)),
            ],
            out_specs=[
                pl.BlockSpec((tile, tokens), lambda i, w: (i, 0)),
                pl.BlockSpec((8, tokens), lambda i, w: (0, 0)),
                pl.BlockSpec((D, tokens), lambda i, w: (0, 0)),
            ],
        ),
        out_shape=[
            jax.ShapeDtypeStruct((vocab, tokens), f32),
            jax.ShapeDtypeStruct((8, tokens), f32),
            jax.ShapeDtypeStruct((D, tokens), bf16),
        ],
        compiler_params=pltpu.CompilerParams(vmem_limit_bytes=44 << 20),
        cost_estimate=pl.CostEstimate(
            flops=2 * vocab * D * tokens,
            bytes_accessed=2 * vocab * D + 4 * D * tokens,
            transcendentals=vocab * tokens,
        ),
    )(where, ids, scale, gain, *pieces, head)


def dfinal_kernel(where, ids, rows, logits, head, kept, sent, plain, turned):
    step = pl.program_id(0)
    vocab, tokens = logits.shape
    lanes = kept.shape[3]

    @pl.when(step == 0)
    def _():
        top, share, coef = (rows[i : i + 1, :] for i in range(3))
        tile = 256
        for start in range(0, vocab, tile):
            probs = jnp.exp(logits[start : start + tile, :] - top) * share
            entries = lax.broadcasted_iota(i32, probs.shape, 0) + (where[1] + start)
            dlogits = coef * (probs - (entries == ids[...]).astype(f32))
            plain[start : start + tile, :] = dlogits.astype(bf16)
            turned[:, start : start + tile] = dlogits.T.astype(bf16)

    product = jnp.dot(turned[...], head[...], preferred_element_type=f32).T
    half = product.shape[0] // 2
    flip = where[0] & 1
    for piece in range(2):
        block = product[piece * half : (piece + 1) * half]
        kept[0, piece ^ flip] = block[:, :lanes]
        sent[0, piece ^ flip] = block[:, lanes:].astype(bf16)


def head_back(where, ids, rows, logits, head, blocks):
    vocab, tokens = logits.shape
    features = D // blocks
    lanes = tokens // 2
    pairs = blocks // 2
    whole = lambda array: pl.BlockSpec(array.shape, lambda i, w: (0,) * array.ndim)
    place = lambda i, w: (i ^ (w[0] >> 1), 0, 0, 0)
    return pl.pallas_call(
        dfinal_kernel,
        grid_spec=pltpu.PrefetchScalarGridSpec(
            num_scalar_prefetch=1,
            grid=(pairs,),
            in_specs=[
                whole(ids),
                whole(rows),
                whole(logits),
                pl.BlockSpec((vocab, 2 * features), lambda i, w: (0, i)),
            ],
            out_specs=[
                pl.BlockSpec((1, 2, features, lanes), place),
                pl.BlockSpec((1, 2, features, lanes), place),
                pl.BlockSpec((vocab, tokens), lambda i, w: (0, 0)),
            ],
            scratch_shapes=[pltpu.VMEM((tokens, vocab), bf16)],
        ),
        out_shape=[
            jax.ShapeDtypeStruct((pairs, 2, features, lanes), f32),
            jax.ShapeDtypeStruct((pairs, 2, features, lanes), bf16),
            jax.ShapeDtypeStruct((vocab, tokens), bf16),
        ],
        compiler_params=pltpu.CompilerParams(vmem_limit_bytes=32 << 20),
        cost_estimate=pl.CostEstimate(
            flops=2 * vocab * D * tokens,
            bytes_accessed=2 * vocab * D + 4 * D * tokens,
            transcendentals=vocab * tokens,
        ),
    )(where, ids, rows, logits, head)


def grad_head_kernel(left, features, *refs):
    out, zeros = refs[-2:]
    out[...] = lax.dot_general(
        left[...], features[...], (((1,), (1,)), ((), ())), preferred_element_type=f32
    ).astype(bf16)

    @pl.when(pl.program_id(0) == 0)
    def _():
        zeros[...] = jnp.zeros_like(zeros)


def grad_head_rows(left, features, index, count, later_than, shape, before):
    vocab, tokens = left.shape
    rows, tile = vocab // count, 1024
    given = (later_than,) if before is None else (later_than, before)
    return pl.pallas_call(
        grad_head_kernel,
        grid=(D // tile,),
        in_specs=[
            pl.BlockSpec((rows, tokens), lambda i: (index, 0)),
            pl.BlockSpec((tile, tokens), lambda i: (i, 0)),
            *[pl.BlockSpec(memory_space=pl.ANY) for _ in given],
        ],
        out_specs=[
            pl.BlockSpec((rows, tile), lambda i: (index, i)),
            pl.BlockSpec(shape, lambda i: (0,) * len(shape)),
        ],
        out_shape=[
            jax.ShapeDtypeStruct((vocab, D), bf16),
            jax.ShapeDtypeStruct(shape, f32),
        ],
        input_output_aliases={3: 0} if before is not None else {},
        compiler_params=pltpu.CompilerParams(vmem_limit_bytes=20 << 20),
        cost_estimate=pl.CostEstimate(
            flops=2 * rows * D * tokens, bytes_accessed=2 * rows * D + 2 * D * tokens, transcendentals=0
        ),
    )(left, features, *given)


def plain_logits(where, ids, scale, gain, pieces, head):
    blocks, _, lanes = pieces[0].shape
    features = D // blocks
    sides = []
    for i in range(0, len(pieces), 3):
        side = jnp.concatenate(pieces[i : i + 3], axis=1)[:, :features]
        sides.append(side[where[0] ^ jnp.arange(blocks)].reshape(D, lanes))
    all_features = jnp.concatenate(sides, axis=1).astype(f32)
    all_features = (all_features * scale * gain[:, None]).astype(bf16)
    logits = dot(head, all_features, 1, 0)
    top = jnp.max(logits, axis=0)
    expd = jnp.exp(logits - top)
    onehot = (jnp.arange(head.shape[0])[:, None] + where[1]) == ids
    stats = [
        top,
        jnp.sum(expd, axis=0),
        jnp.sum(expd * logits, axis=0),
        jnp.sum(jnp.where(onehot, logits, 0.0), axis=0),
    ]
    return logits, jnp.stack(stats), all_features


def plain_back(where, ids, rows, logits, head, blocks):
    top, share, coef = rows[0], rows[1], rows[2]
    lanes = logits.shape[1] // lax.axis_size("tp")
    onehot = (jnp.arange(head.shape[0])[:, None] + where[1]) == ids
    dlogits = coef * (jnp.exp(logits - top) * share - onehot.astype(f32))
    dlogits = dlogits.astype(bf16)
    product = dot(head, dlogits, 0, 0).reshape(blocks, D // blocks, -1)
    product = product[where[0] ^ jnp.arange(blocks)]
    return product[..., :lanes], product[..., lanes:].astype(bf16), dlogits


def shards(
    prev_hidden,
    token_embed,
    gain_hidden,
    gain_embed,
    gain_final,
    proj_hidden,
    proj_embed,
    head,
    target_ids,
    valid,
    rest_count,
):
    blocks, cores = lax.axis_size("seq"), lax.axis_size("tp")
    me = lax.axis_index("seq")
    rows, width = prev_hidden.shape
    features = proj_hidden.shape[1]
    tokens = rows * blocks
    lanes = tokens // cores

    prev_f = prev_hidden.astype(f32)
    embed_f = token_embed.astype(f32)
    sums = lax.psum(
        jnp.stack([jnp.sum(prev_f * prev_f, axis=-1), jnp.sum(embed_f * embed_f, axis=-1)]), "tp"
    )
    scales = lax.rsqrt(sums / D + epsilon)
    scale_prev, scale_embed = scales[0][:, None], scales[1][:, None]
    normed_prev = (prev_f * scale_prev * gain_hidden).astype(bf16)
    normed_embed = (embed_f * scale_embed * gain_embed).astype(bf16)
    main = round(0.75 * width / 128) * 128
    rest = width - main
    first, second, third, ids_here, valid_here, gain_here = lax.optimization_barrier(
        (
            normed_prev[:, :main],
            normed_embed[:, :main],
            jnp.concatenate([normed_prev[:, main:], normed_embed[:, main:]], axis=1),
            target_ids,
            valid,
            gain_final,
        )
    )
    facts = jnp.stack([ids_here // 256, ids_here % 256, valid_here]).astype(bf16)
    facts = dot(jnp.eye(rows, dtype=bf16), jnp.pad(facts, ((0, 5), (0, 0))), 1, 1).astype(bf16)
    gain_parts = jnp.stack(in_parts(gain_here)).astype(bf16).reshape(rows, -1)
    gain_columns = gain_parts.shape[1]
    facts = jnp.concatenate([facts, gain_parts], axis=1)
    facts = jnp.pad(facts, ((0, 0), (0, 128 - facts.shape[1])))

    first, second, third = gather(first, second, jnp.concatenate([third, facts], axis=1))
    first, second = first.reshape(tokens, main), second.reshape(tokens, main)
    third = third.reshape(tokens, 2 * rest + 128)

    row = lax.broadcasted_iota(i32, (tokens, 1), 0)
    position = (me ^ (row // rows)) * rows + row % rows
    column = lax.broadcasted_iota(i32, (1, tokens), 1)
    order_prev = position == column
    order_embed = position - 1 == column

    from_prev = dot(proj_hidden[:main], first, 0, 1) + dot(proj_hidden[main:], third[:, :rest], 0, 1)
    from_embed = dot(proj_embed[:main], second, 0, 1) + dot(
        proj_embed[main:], third[:, rest : 2 * rest], 0, 1
    )
    facts_all = third[:, 2 * rest :]
    facts_prev = dot(facts_all, order_prev.astype(bf16), 0, 0)
    partial_value = dot(
        jnp.concatenate([from_prev, from_embed], axis=1),
        jnp.concatenate([order_prev, order_embed], axis=0).astype(f32),
        1,
        0,
        lax.Precision.HIGHEST,
    )
    gain_all = facts_all[:, 8 : 8 + gain_columns].reshape(blocks, 3, features).astype(f32)
    gain_all = gain_all[:, 0] + gain_all[:, 1] + gain_all[:, 2]
    block = jnp.arange(blocks)
    gain_all = dot(
        ((me ^ block)[:, None] == block[None, :]).astype(f32), gain_all, 0, 0, lax.Precision.HIGHEST
    ).reshape(D)
    ids_all = (facts_prev[0:1] * 256 + facts_prev[1:2]).astype(i32)
    valid_all = facts_prev[2]
    core = lax.axis_index("tp")
    cut_of = lambda mask: lax.dynamic_slice_in_dim(partial_value, (core ^ mask) * lanes, lanes, 1)
    mixed_f = cut_of(0)
    for mask in tp_masks():
        mixed_f = mixed_f + from_partner(cut_of(mask), "tp", mask)
    mixed_f = mixed_f.astype(bf16).astype(f32)
    mixed = mixed_f.astype(bf16)
    square_parts = jnp.stack(in_parts(jnp.sum(mixed_f * mixed_f, axis=0))).astype(bf16)
    square_parts = jnp.pad(square_parts, ((0, 13), (0, 0)))
    one, two = cut_in_three(features, 16)
    pieces = gather(
        mixed[:one], mixed[one:two], jnp.concatenate([mixed[two:], square_parts], axis=0)
    )
    pieces = list(pieces)
    for mask in tp_masks():
        pieces = pieces + [from_partner(piece, "tp", mask) for piece in pieces[:3]]
    squares = [
        jnp.sum(piece[:, features - two :][:, :3].astype(f32), axis=(0, 1)) for piece in pieces[2::3]
    ]
    scale_own = lax.rsqrt(squares[0] / D + epsilon)
    scale_final = lax.rsqrt(jnp.concatenate(squares) / D + epsilon)

    vocab_rows = head.shape[0]
    where = jnp.stack([me, lax.axis_index(("seq", "tp")) * vocab_rows]).astype(i32)
    ids = lanes_by_index(ids_all)
    valid_lanes = lanes_by_index(valid_all)
    fits = cores == 2 and lanes % 128 == 0 and vocab_rows % 512 == 0 and 2 * features % 128 == 0
    forward = head_logits if fits else plain_logits
    logits, stats, final_all = forward(where, ids, scale_final[None, :], gain_all, pieces, head)
    stats = stats[:4]
    for step in range(0, bits_of("seq"), 2):
        masks = [k << step for k in range(1, min(4, blocks >> step))]
        stats = merged([stats] + [from_partner(stats, "seq", mask) for mask in masks])
    stats = lanes_by_index(stats)
    stats = merged([stats] + [from_partner(stats, "tp", mask) for mask in tp_masks()])
    row_top, row_total, row_weighted, target_logit = lanes_by_index(stats)
    count = jnp.sum(valid_all) + rest_count[0].astype(f32)
    coef = loss_scale * valid_lanes / count
    row_values = jnp.stack([row_top, 1.0 / row_total, coef])
    row_values = jnp.pad(row_values, ((0, 5), (0, 0)))
    back = head_back if fits else plain_back
    kept, sent, dlogits = back(where, ids, row_values, logits, head, blocks)
    dfinal = kept.reshape(blocks, features, lanes)
    for mask in tp_masks():
        piece = sent[..., (mask - 1) * lanes : mask * lanes]
        from_core = from_partner(piece, "tp", mask)
        dfinal = dfinal + from_core.astype(f32).reshape(dfinal.shape)

    def grad_head_piece(index, tied):
        def work(last, shape, results):
            if not fits:
                return dot(dlogits, final_all, 1, 1).astype(bf16), None
            before = results[-1] if results else None
            shape = shape if tied else (8, 128)
            out, zeros = grad_head_rows(
                dlogits, final_all, index, 4, last if tied else from_core, shape, before
            )
            return out, (zeros if tied else None)

        return work

    early = [grad_head_piece(index, index == 1) for index in range(2 if fits else 1)]
    dfinal, results = scatter([dfinal[:, :one], dfinal[:, one:two], dfinal[:, two:]], early)
    dfinal = jnp.concatenate(dfinal, axis=0)

    total_dot = (coef * (row_weighted / row_total - target_logit))[:lanes] / scale_own
    dmixed = (
        scale_own * (dfinal * gain_final[:, None]) - mixed_f * (scale_own**3 * (total_dot / D))
    ).astype(bf16)
    dmixed = lanes_by_index(over_cores(dmixed))
    dmixed_prev = dot(dmixed, order_prev.astype(bf16), 1, 1).astype(bf16)
    dmixed_embed = dot(dmixed, order_embed.astype(bf16), 1, 1).astype(bf16)
    back_prev = dot(dmixed_prev, proj_hidden, 0, 1).reshape(blocks, rows, width)
    back_embed = dot(dmixed_embed, proj_embed, 0, 1).reshape(blocks, rows, width)

    def grad_head_end(index):
        def work(last, shape, before):
            grad_head = before[-1] if before else results[-1]
            if not fits:
                return grad_head, None
            shape = shape if index == 3 else (8, 128)
            out, zeros = grad_head_rows(dlogits, final_all, index, 4, last, shape, grad_head)
            return out, (zeros if index == 3 else None)

        return work

    def grad_proj(rows_in, rows_rest, back):
        rows_all = jnp.concatenate([rows_in, rows_rest], axis=1)
        return dot(rows_all, back, 0, 1).astype(bf16)

    (one, two, three), ends = scatter(
        [
            back_prev[..., :main],
            back_embed[..., :main],
            jnp.concatenate([back_prev[..., main:], back_embed[..., main:]], axis=-1),
        ],
        [grad_head_end(2), grad_head_end(3)],
    )
    grad_head = ends[-1]
    grad_proj_hidden = grad_proj(first, third[:, :rest], dmixed_prev)
    grad_proj_embed = grad_proj(second, third[:, rest : 2 * rest], dmixed_embed)
    grad_prev = jnp.concatenate([one, three[:, :rest]], axis=1) * gain_hidden
    grad_embed = jnp.concatenate([two, three[:, rest:]], axis=1) * gain_embed
    dots = lax.psum(
        jnp.stack([jnp.sum(grad_prev * prev_f, axis=-1), jnp.sum(grad_embed * embed_f, axis=-1)]),
        "tp",
    )
    grad_prev_hidden = (
        scale_prev * grad_prev - prev_f * (scale_prev**3 * (dots[0] / D)[:, None])
    ).astype(bf16)
    grad_token_embed = (
        scale_embed * grad_embed - embed_f * (scale_embed**3 * (dots[1] / D)[:, None])
    ).astype(bf16)
    return (grad_prev_hidden, grad_token_embed, grad_proj_hidden, grad_proj_embed, grad_head)


def solution(mesh):
    return jax.shard_map(
        shards,
        mesh=mesh,
        in_specs=(
            P("seq", "tp"),
            P("seq", "tp"),
            P("tp"),
            P("tp"),
            P("seq"),
            P("tp", "seq"),
            P("tp", "seq"),
            P(("seq", "tp"), None),
            P("seq"),
            P("seq"),
            P(),
        ),
        out_specs=(
            P("seq", "tp"),
            P("seq", "tp"),
            P("tp", "seq"),
            P("tp", "seq"),
            P(("seq", "tp"), None),
        ),
        check_vma=False,
    )
```

```python
import jax
import jax.numpy as jnp
from jax import lax
from jax.experimental import pallas as pl
from jax.experimental.pallas import tpu as pltpu
from jax.sharding import PartitionSpec as P

D = 7168


loss_scale = 4096.0
epsilon = 1e-06

f32 = jnp.float32
bf16 = jnp.bfloat16
i32 = jnp.int32


def from_partner(array, axis, mask):
    size = lax.axis_size(axis)
    return lax.ppermute(array, axis, [(i, i ^ mask) for i in range(size)])


def bits_of(axis):
    return lax.axis_size(axis).bit_length() - 1


def zero_of(array, shape):
    array = array[(0,) * (array.ndim - len(shape))] if array.ndim > len(shape) else array
    array = array[tuple(slice(0, size) for size in shape[len(shape) - array.ndim :])]
    return array * 0


def in_order(array, order):
    count = len(order)
    dims = [count - 1 - order.index(bit) for bit in reversed(range(count))]
    array = array.transpose(dims + list(range(count, array.ndim)))
    return array.reshape((1 << count,) + array.shape[count:])


def gather(first, second, third):
    high = list(reversed(range(2, bits_of("seq"))))
    third_shape = third.shape
    came = []
    for bit in high:
        came = [from_partner(first, "seq", 1 << bit), from_partner(second, "seq", 1 << bit)]
        if bit == high[0]:
            third = third + zero_of(came[0], third.shape) + zero_of(came[1], third.shape)
        first, second = jnp.stack([first, came[0]]), jnp.stack([second, came[1]])
    for bit in (0, 1):
        first = jnp.stack([first, from_partner(first, "seq", 2 >> bit)])
        second = jnp.stack([second, from_partner(second, "seq", 1 << bit)])
        third = jnp.stack([third, from_partner(third, "seq", 1 << bit)])
    for block in came:
        third = third + zero_of(block, third_shape)
    far = range(1, 1 << len(high))
    third = jnp.stack([third] + [from_partner(third, "seq", place << 2) for place in far])
    third = third.reshape((-1,) + third_shape)
    return in_order(first, high + [1, 0]), in_order(second, high + [0, 1]), third


def scatter(arrays, beside=()):
    count = bits_of("seq")
    low, high = [0, 1], list(range(2, count))
    third = arrays[2].reshape((1 << len(high), 2, 2) + arrays[2].shape[1:])
    far = [
        from_partner(third[place].astype(bf16), "seq", place << 2)
        for place in range(1, 1 << len(high))
    ]
    arrays = [array.reshape((2,) * count + array.shape[1:]) for array in arrays[:2]]
    orders = [low + high, low[::-1] + high, [None, None, 1, 0] + [None] * len(high[2:])]
    left = [list(reversed(range(count))), list(reversed(range(count))), [1, 0]]
    results = []
    last = far[0]
    for step in range(count):
        sums, came = [], []
        for k, array in enumerate(arrays):
            bit = orders[k][step]
            if bit is None:
                sums.append(array)
                continue
            dim = left[k].index(bit)
            left[k].remove(bit)
            sent = lax.index_in_dim(array, 1, dim, keepdims=False).astype(bf16)
            kept = lax.index_in_dim(array, 0, dim, keepdims=False).astype(f32)
            came.append(from_partner(sent, "seq", 1 << bit))
            sums.append(kept + came[-1].astype(f32))
        if step < len(beside):
            result, zeros = beside[step](last, sums[0].shape, results)
            results.append(result)
            if zeros is not None:
                sums[0] = sums[0] + zeros
        if step == 1:
            total = third[0].astype(f32)
            for block in far:
                total = total + block.astype(f32)
            shape = third.shape[3:]
            sums.append(total + zero_of(came[0], shape) + zero_of(came[1], shape))
        arrays, last = sums, came[0]
    return arrays, results


def cut_in_three(size, unit):
    third = round(0.25 * size / unit) * unit
    first = (size - third + unit) // (2 * unit) * unit
    return first, size - third


def tp_masks():
    return range(1, lax.axis_size("tp"))


def over_cores(array):
    return jnp.concatenate([array] + [from_partner(array, "tp", mask) for mask in tp_masks()], axis=-1)


def lanes_by_index(array):
    count = lax.axis_size("tp")
    pieces = jnp.split(array, count, axis=-1)
    me = lax.axis_index("tp")
    step = 1
    while step < count:
        flipped = [pieces[i ^ step] for i in range(count)]
        pieces = [jnp.where(me & step == 0, a, b) for a, b in zip(pieces, flipped)]
        step *= 2
    return jnp.concatenate(pieces, axis=-1)


def merged(group):
    tops, totals, weighted, targets = (jnp.stack([one[i] for one in group]) for i in range(4))
    top = jnp.max(tops, axis=0)
    shares = jnp.exp(tops - top)
    return jnp.stack(
        [
            top,
            jnp.sum(shares * totals, axis=0),
            jnp.sum(shares * weighted, axis=0),
            jnp.sum(targets, axis=0),
        ]
    )


def in_parts(values):
    high = lax.reduce_precision(values, 8, 7)
    middle = lax.reduce_precision(values - high, 8, 7)
    return high, middle, values - high - middle


def dot(left, right, on_left, on_right, precision=None):
    return lax.dot_general(
        left,
        right,
        (((on_left,), (on_right,)), ((), ())),
        precision=precision,
        preferred_element_type=f32,
    )


def logits_kernel(where, ids, scale, gain, *refs):
    *pieces, head, out, stats, all_features = refs
    step = pl.program_id(0)
    tile = head.shape[0]
    blocks, _, lanes = pieces[0].shape
    features = all_features.shape[0] // blocks

    @pl.when(step == 0)
    def _():
        for device in range(blocks):
            for side in range(2):
                done = 0
                columns = slice(side * lanes, (side + 1) * lanes)
                for piece in pieces[3 * side : 3 * side + 3]:
                    rows = min(piece.shape[1], features - done)
                    values = piece[where[0] ^ device][:rows].astype(f32) * scale[:, columns]
                    values = values * gain[done : done + rows, device : device + 1]
                    start = device * features + done
                    all_features[start : start + rows, columns] = values.astype(bf16)
                    done += rows
        stats[...] = jnp.zeros_like(stats)
        stats[0:1, :] = jnp.full((1, stats.shape[1]), -jnp.inf, f32)

    logits = jnp.dot(head[...], all_features[...], preferred_element_type=f32)
    out[...] = logits
    entries = lax.broadcasted_iota(i32, logits.shape, 0) + (where[1] + step * tile)
    before = stats[0:1, :]
    top = jnp.maximum(before, jnp.max(logits, axis=0, keepdims=True))
    shrink = jnp.exp(before - top)
    expd = jnp.exp(logits - top)
    stats[0:1, :] = top
    stats[1:2, :] = stats[1:2, :] * shrink + jnp.sum(expd, axis=0, keepdims=True)
    stats[2:3, :] = stats[2:3, :] * shrink + jnp.sum(expd * logits, axis=0, keepdims=True)
    stats[3:4, :] = stats[3:4, :] + jnp.sum(
        jnp.where(entries == ids[...], logits, 0.0), axis=0, keepdims=True
    )


def head_logits(where, ids, scale, gain, pieces, head):
    vocab, tokens = head.shape[0], ids.shape[1]
    tile = 512
    gain = gain.reshape(pieces[0].shape[0], -1).T
    whole = lambda array: pl.BlockSpec(array.shape, lambda i, w: (0,) * array.ndim)
    return pl.pallas_call(
        logits_kernel,
        grid_spec=pltpu.PrefetchScalarGridSpec(
            num_scalar_prefetch=1,
            grid=(vocab // tile,),
            in_specs=[
                whole(ids),
                whole(scale),
                whole(gain),
                *[whole(piece) for piece in pieces],
                pl.BlockSpec((tile, D), lambda i, w: (i, 0)),
            ],
            out_specs=[
                pl.BlockSpec((tile, tokens), lambda i, w: (i, 0)),
                pl.BlockSpec((8, tokens), lambda i, w: (0, 0)),
                pl.BlockSpec((D, tokens), lambda i, w: (0, 0)),
            ],
        ),
        out_shape=[
            jax.ShapeDtypeStruct((vocab, tokens), f32),
            jax.ShapeDtypeStruct((8, tokens), f32),
            jax.ShapeDtypeStruct((D, tokens), bf16),
        ],
        compiler_params=pltpu.CompilerParams(vmem_limit_bytes=44 << 20),
        cost_estimate=pl.CostEstimate(
            flops=2 * vocab * D * tokens,
            bytes_accessed=2 * vocab * D + 4 * D * tokens,
            transcendentals=vocab * tokens,
        ),
    )(where, ids, scale, gain, *pieces, head)


def dfinal_kernel(where, ids, rows, logits, head, kept, sent, plain, turned):
    step = pl.program_id(0)
    vocab, tokens = logits.shape
    lanes = kept.shape[3]

    @pl.when(step == 0)
    def _():
        top, share, coef = (rows[i : i + 1, :] for i in range(3))
        tile = 256
        for start in range(0, vocab, tile):
            probs = jnp.exp(logits[start : start + tile, :] - top) * share
            entries = lax.broadcasted_iota(i32, probs.shape, 0) + (where[1] + start)
            dlogits = coef * (probs - (entries == ids[...]).astype(f32))
            plain[start : start + tile, :] = dlogits.astype(bf16)
            turned[:, start : start + tile] = dlogits.astype(bf16).T

    product = jnp.dot(turned[...], head[...], preferred_element_type=f32)
    mine, other = product[:lanes].T, product[lanes:].astype(bf16).T
    half = mine.shape[0] // 2
    flip = where[0] & 1
    for piece in range(2):
        kept[0, piece ^ flip] = mine[piece * half : (piece + 1) * half]
        sent[0, piece ^ flip] = other[piece * half : (piece + 1) * half]


def head_back(where, ids, rows, logits, head, blocks):
    vocab, tokens = logits.shape
    features = D // blocks
    lanes = tokens // 2
    pairs = blocks // 2
    whole = lambda array: pl.BlockSpec(array.shape, lambda i, w: (0,) * array.ndim)
    place = lambda i, w: (i ^ (w[0] >> 1), 0, 0, 0)
    return pl.pallas_call(
        dfinal_kernel,
        grid_spec=pltpu.PrefetchScalarGridSpec(
            num_scalar_prefetch=1,
            grid=(pairs,),
            in_specs=[
                whole(ids),
                whole(rows),
                whole(logits),
                pl.BlockSpec((vocab, 2 * features), lambda i, w: (0, i)),
            ],
            out_specs=[
                pl.BlockSpec((1, 2, features, lanes), place),
                pl.BlockSpec((1, 2, features, lanes), place),
                pl.BlockSpec((vocab, tokens), lambda i, w: (0, 0)),
            ],
            scratch_shapes=[pltpu.VMEM((tokens, vocab), bf16)],
        ),
        out_shape=[
            jax.ShapeDtypeStruct((pairs, 2, features, lanes), f32),
            jax.ShapeDtypeStruct((pairs, 2, features, lanes), bf16),
            jax.ShapeDtypeStruct((vocab, tokens), bf16),
        ],
        compiler_params=pltpu.CompilerParams(vmem_limit_bytes=32 << 20),
        cost_estimate=pl.CostEstimate(
            flops=2 * vocab * D * tokens,
            bytes_accessed=2 * vocab * D + 4 * D * tokens,
            transcendentals=vocab * tokens,
        ),
    )(where, ids, rows, logits, head)


def grad_head_kernel(left, features, *refs):
    out, zeros = refs[-2:]
    out[...] = lax.dot_general(
        left[...], features[...], (((1,), (1,)), ((), ())), preferred_element_type=f32
    ).astype(bf16)

    @pl.when(pl.program_id(0) == 0)
    def _():
        zeros[...] = jnp.zeros_like(zeros)


def grad_head_rows(left, features, index, count, later_than, shape, before):
    vocab, tokens = left.shape
    rows, tile = vocab // count, 1024
    given = (later_than,) if before is None else (later_than, before)
    return pl.pallas_call(
        grad_head_kernel,
        grid=(D // tile,),
        in_specs=[
            pl.BlockSpec((rows, tokens), lambda i: (index, 0)),
            pl.BlockSpec((tile, tokens), lambda i: (i, 0)),
            *[pl.BlockSpec(memory_space=pl.ANY) for _ in given],
        ],
        out_specs=[
            pl.BlockSpec((rows, tile), lambda i: (index, i)),
            pl.BlockSpec(shape, lambda i: (0,) * len(shape)),
        ],
        out_shape=[
            jax.ShapeDtypeStruct((vocab, D), bf16),
            jax.ShapeDtypeStruct(shape, f32),
        ],
        input_output_aliases={3: 0} if before is not None else {},
        compiler_params=pltpu.CompilerParams(vmem_limit_bytes=20 << 20),
        cost_estimate=pl.CostEstimate(
            flops=2 * rows * D * tokens, bytes_accessed=2 * rows * D + 2 * D * tokens, transcendentals=0
        ),
    )(left, features, *given)


def plain_logits(where, ids, scale, gain, pieces, head):
    blocks, _, lanes = pieces[0].shape
    features = D // blocks
    sides = []
    for i in range(0, len(pieces), 3):
        side = jnp.concatenate(pieces[i : i + 3], axis=1)[:, :features]
        sides.append(side[where[0] ^ jnp.arange(blocks)].reshape(D, lanes))
    all_features = jnp.concatenate(sides, axis=1).astype(f32)
    all_features = (all_features * scale * gain[:, None]).astype(bf16)
    logits = dot(head, all_features, 1, 0)
    top = jnp.max(logits, axis=0)
    expd = jnp.exp(logits - top)
    onehot = (jnp.arange(head.shape[0])[:, None] + where[1]) == ids
    stats = [
        top,
        jnp.sum(expd, axis=0),
        jnp.sum(expd * logits, axis=0),
        jnp.sum(jnp.where(onehot, logits, 0.0), axis=0),
    ]
    return logits, jnp.stack(stats), all_features


def plain_back(where, ids, rows, logits, head, blocks):
    top, share, coef = rows[0], rows[1], rows[2]
    lanes = logits.shape[1] // lax.axis_size("tp")
    onehot = (jnp.arange(head.shape[0])[:, None] + where[1]) == ids
    dlogits = coef * (jnp.exp(logits - top) * share - onehot.astype(f32))
    dlogits = dlogits.astype(bf16)
    product = dot(head, dlogits, 0, 0).reshape(blocks, D // blocks, -1)
    product = product[where[0] ^ jnp.arange(blocks)]
    return product[..., :lanes], product[..., lanes:].astype(bf16), dlogits


def shards(
    prev_hidden,
    token_embed,
    gain_hidden,
    gain_embed,
    gain_final,
    proj_hidden,
    proj_embed,
    head,
    target_ids,
    valid,
    rest_count,
):
    blocks, cores = lax.axis_size("seq"), lax.axis_size("tp")
    me = lax.axis_index("seq")
    rows, width = prev_hidden.shape
    features = proj_hidden.shape[1]
    tokens = rows * blocks
    lanes = tokens // cores

    prev_f = prev_hidden.astype(f32)
    embed_f = token_embed.astype(f32)
    sums = lax.psum(
        jnp.stack([jnp.sum(prev_f * prev_f, axis=-1), jnp.sum(embed_f * embed_f, axis=-1)]), "tp"
    )
    scales = lax.rsqrt(sums / D + epsilon)
    scale_prev, scale_embed = scales[0][:, None], scales[1][:, None]
    normed_prev = (prev_f * scale_prev * gain_hidden).astype(bf16)
    normed_embed = (embed_f * scale_embed * gain_embed).astype(bf16)
    main = round(0.75 * width / 128) * 128
    rest = width - main
    first, second, third, ids_here, valid_here, gain_here = lax.optimization_barrier(
        (
            normed_prev[:, :main],
            normed_embed[:, :main],
            jnp.concatenate([normed_prev[:, main:], normed_embed[:, main:]], axis=1),
            target_ids,
            valid,
            gain_final,
        )
    )
    facts = jnp.stack([ids_here // 256, ids_here % 256, valid_here]).astype(bf16)
    facts = dot(jnp.eye(rows, dtype=bf16), jnp.pad(facts, ((0, 5), (0, 0))), 1, 1).astype(bf16)
    gain_parts = jnp.stack(in_parts(gain_here)).astype(bf16).reshape(rows, -1)
    gain_columns = gain_parts.shape[1]
    facts = jnp.concatenate([facts, gain_parts], axis=1)
    facts = jnp.pad(facts, ((0, 0), (0, 128 - facts.shape[1])))

    first, second, third = gather(first, second, jnp.concatenate([third, facts], axis=1))
    first, second = first.reshape(tokens, main), second.reshape(tokens, main)
    third = third.reshape(tokens, 2 * rest + 128)

    row = lax.broadcasted_iota(i32, (tokens, 1), 0)
    position = (me ^ (row // rows)) * rows + row % rows
    column = lax.broadcasted_iota(i32, (1, tokens), 1)
    order_prev = position == column
    order_embed = position - 1 == column

    from_prev = dot(proj_hidden[:main], first, 0, 1) + dot(proj_hidden[main:], third[:, :rest], 0, 1)
    from_embed = dot(proj_embed[:main], second, 0, 1) + dot(
        proj_embed[main:], third[:, rest : 2 * rest], 0, 1
    )
    facts_all = third[:, 2 * rest :]
    facts_prev = dot(facts_all, order_prev.astype(bf16), 0, 0)
    partial_value = dot(
        jnp.concatenate([from_prev, from_embed], axis=1),
        jnp.concatenate([order_prev, order_embed], axis=0).astype(f32),
        1,
        0,
        lax.Precision.HIGHEST,
    )
    gain_all = facts_all[:, 8 : 8 + gain_columns].reshape(blocks, 3, features).astype(f32)
    gain_all = gain_all[:, 0] + gain_all[:, 1] + gain_all[:, 2]
    block = jnp.arange(blocks)
    gain_all = dot(
        ((me ^ block)[:, None] == block[None, :]).astype(f32), gain_all, 0, 0, lax.Precision.HIGHEST
    ).reshape(D)
    ids_all = (facts_prev[0:1] * 256 + facts_prev[1:2]).astype(i32)
    valid_all = facts_prev[2]
    core = lax.axis_index("tp")
    cut_of = lambda mask: lax.dynamic_slice_in_dim(partial_value, (core ^ mask) * lanes, lanes, 1)
    mixed_f = cut_of(0)
    for mask in tp_masks():
        mixed_f = mixed_f + from_partner(cut_of(mask), "tp", mask)
    mixed_f = mixed_f.astype(bf16).astype(f32)
    mixed = mixed_f.astype(bf16)
    square_parts = jnp.stack(in_parts(jnp.sum(mixed_f * mixed_f, axis=0))).astype(bf16)
    square_parts = jnp.pad(square_parts, ((0, 13), (0, 0)))
    one, two = cut_in_three(features, 16)
    pieces = gather(
        mixed[:one], mixed[one:two], jnp.concatenate([mixed[two:], square_parts], axis=0)
    )
    pieces = list(pieces)
    for mask in tp_masks():
        pieces = pieces + [from_partner(piece, "tp", mask) for piece in pieces[:3]]
    squares = [
        jnp.sum(piece[:, features - two :][:, :3].astype(f32), axis=(0, 1)) for piece in pieces[2::3]
    ]
    scale_own = lax.rsqrt(squares[0] / D + epsilon)
    scale_final = lax.rsqrt(jnp.concatenate(squares) / D + epsilon)

    vocab_rows = head.shape[0]
    where = jnp.stack([me, lax.axis_index(("seq", "tp")) * vocab_rows]).astype(i32)
    ids = lanes_by_index(ids_all)
    valid_lanes = lanes_by_index(valid_all)
    fits = cores == 2 and lanes % 128 == 0 and vocab_rows % 512 == 0 and 2 * features % 128 == 0
    forward = head_logits if fits else plain_logits
    logits, stats, final_all = forward(where, ids, scale_final[None, :], gain_all, pieces, head)
    stats = stats[:4]
    for step in range(0, bits_of("seq"), 2):
        masks = [k << step for k in range(1, min(4, blocks >> step))]
        stats = merged([stats] + [from_partner(stats, "seq", mask) for mask in masks])
    stats = lanes_by_index(stats)
    stats = merged([stats] + [from_partner(stats, "tp", mask) for mask in tp_masks()])
    row_top, row_total, row_weighted, target_logit = lanes_by_index(stats)
    count = jnp.sum(valid_all) + rest_count[0].astype(f32)
    coef = loss_scale * valid_lanes / count
    row_values = jnp.stack([row_top, 1.0 / row_total, coef])
    row_values = jnp.pad(row_values, ((0, 5), (0, 0)))
    back = head_back if fits else plain_back
    kept, sent, dlogits = back(where, ids, row_values, logits, head, blocks)
    dfinal = kept.reshape(blocks, features, lanes)
    for mask in tp_masks():
        piece = sent[..., (mask - 1) * lanes : mask * lanes]
        from_core = from_partner(piece, "tp", mask)
        dfinal = dfinal + from_core.astype(f32).reshape(dfinal.shape)

    def grad_head_piece(index, tied):
        def work(last, shape, results):
            if not fits:
                return dot(dlogits, final_all, 1, 1).astype(bf16), None
            before = results[-1] if results else None
            shape = shape if tied else (8, 128)
            later_than = last if tied else from_core
            out, zeros = grad_head_rows(dlogits, final_all, index, 4, later_than, shape, before)
            return out, (zeros if tied else None)

        return work

    early = [grad_head_piece(index, index == 1) for index in range(2 if fits else 1)]
    dfinal, results = scatter([dfinal[:, :one], dfinal[:, one:two], dfinal[:, two:]], early)
    dfinal = jnp.concatenate(dfinal, axis=0)

    total_dot = (coef * (row_weighted / row_total - target_logit))[:lanes] / scale_own
    dmixed = (
        scale_own * (dfinal * gain_final[:, None]) - mixed_f * (scale_own**3 * (total_dot / D))
    ).astype(bf16)
    dmixed = lanes_by_index(over_cores(dmixed))
    dmixed_prev = dot(dmixed, order_prev.astype(bf16), 1, 1).astype(bf16)
    dmixed_embed = dot(dmixed, order_embed.astype(bf16), 1, 1).astype(bf16)
    back_prev = dot(dmixed_prev, proj_hidden, 0, 1).reshape(blocks, rows, width)
    back_embed = dot(dmixed_embed, proj_embed, 0, 1).reshape(blocks, rows, width)

    def grad_head_end(index):
        def work(last, shape, before):
            grad_head = before[-1] if before else results[-1]
            if not fits:
                return grad_head, None
            return grad_head_rows(dlogits, final_all, index, 4, last, shape, grad_head)

        return work

    def grad_proj(rows_in, rows_rest, back):
        rows_all = jnp.concatenate([rows_in, rows_rest], axis=1)
        return dot(rows_all, back, 0, 1).astype(bf16)

    (one, two, three), ends = scatter(
        [
            back_prev[..., :main],
            back_embed[..., :main],
            jnp.concatenate([back_prev[..., main:], back_embed[..., main:]], axis=-1),
        ],
        [grad_head_end(2), grad_head_end(3)],
    )
    grad_head = ends[-1]
    grad_proj_hidden = grad_proj(first, third[:, :rest], dmixed_prev)
    grad_proj_embed = grad_proj(second, third[:, rest : 2 * rest], dmixed_embed)
    grad_prev = jnp.concatenate([one, three[:, :rest]], axis=1) * gain_hidden
    grad_embed = jnp.concatenate([two, three[:, rest:]], axis=1) * gain_embed
    dots = lax.psum(
        jnp.stack([jnp.sum(grad_prev * prev_f, axis=-1), jnp.sum(grad_embed * embed_f, axis=-1)]),
        "tp",
    )
    grad_prev_hidden = (
        scale_prev * grad_prev - prev_f * (scale_prev**3 * (dots[0] / D)[:, None])
    ).astype(bf16)
    grad_token_embed = (
        scale_embed * grad_embed - embed_f * (scale_embed**3 * (dots[1] / D)[:, None])
    ).astype(bf16)
    return (grad_prev_hidden, grad_token_embed, grad_proj_hidden, grad_proj_embed, grad_head)


def solution(mesh):
    return jax.shard_map(
        shards,
        mesh=mesh,
        in_specs=(
            P("seq", "tp"),
            P("seq", "tp"),
            P("tp"),
            P("tp"),
            P("seq"),
            P("tp", "seq"),
            P("tp", "seq"),
            P(("seq", "tp"), None),
            P("seq"),
            P("seq"),
            P(),
        ),
        out_specs=(
            P("seq", "tp"),
            P("seq", "tp"),
            P("tp", "seq"),
            P("tp", "seq"),
            P(("seq", "tp"), None),
        ),
        check_vma=False,
    )
```

```python
import jax
import jax.numpy as jnp
from jax import lax
from jax.experimental import pallas as pl
from jax.experimental.pallas import tpu as pltpu
from jax.sharding import PartitionSpec as P

D = 7168


loss_scale = 4096.0
epsilon = 1e-06

f32 = jnp.float32
bf16 = jnp.bfloat16
i32 = jnp.int32


def from_partner(array, axis, mask):
    size = lax.axis_size(axis)
    return lax.ppermute(array, axis, [(i, i ^ mask) for i in range(size)])


def bits_of(axis):
    return lax.axis_size(axis).bit_length() - 1


def zero_of(array, shape):
    array = array[(0,) * (array.ndim - len(shape))] if array.ndim > len(shape) else array
    array = array[tuple(slice(0, size) for size in shape[len(shape) - array.ndim :])]
    return array * 0


def in_order(array, order):
    count = len(order)
    dims = [count - 1 - order.index(bit) for bit in reversed(range(count))]
    array = array.transpose(dims + list(range(count, array.ndim)))
    return array.reshape((1 << count,) + array.shape[count:])


def gather(first, second, third, last=False):
    high = list(reversed(range(2, bits_of("seq"))))
    third_shape = third.shape
    came = []
    for bit in high:
        came = [from_partner(first, "seq", 1 << bit), from_partner(second, "seq", 1 << bit)]
        if bit == high[0]:
            third = third + zero_of(came[0], third.shape) + zero_of(came[1], third.shape)
        first, second = jnp.stack([first, came[0]]), jnp.stack([second, came[1]])
    for bit in (0, 1):
        ends = [from_partner(first, "seq", 2 >> bit), from_partner(second, "seq", 1 << bit)]
        first, second = jnp.stack([first, ends[0]]), jnp.stack([second, ends[1]])
        third = jnp.stack([third, from_partner(third, "seq", 1 << bit)])
    for block in came:
        third = third + zero_of(block, third_shape)
    far = range(1, 1 << len(high))
    third = jnp.stack([third] + [from_partner(third, "seq", place << 2) for place in far])
    third = third.reshape((-1,) + third_shape)
    for block in ends if last else ():
        third = third + zero_of(block, third_shape)
    return in_order(first, high + [1, 0]), in_order(second, high + [0, 1]), third


def scatter(arrays, beside=()):
    count = bits_of("seq")
    low, high = [0, 1], list(range(2, count))
    third = arrays[2].reshape((1 << len(high), 2, 2) + arrays[2].shape[1:])
    far = [
        from_partner(third[place].astype(bf16), "seq", place << 2)
        for place in range(1, 1 << len(high))
    ]
    arrays = [array.reshape((2,) * count + array.shape[1:]) for array in arrays[:2]]
    orders = [low + high, low[::-1] + high, [None, None, 1, 0] + [None] * len(high[2:])]
    left = [list(reversed(range(count))), list(reversed(range(count))), [1, 0]]
    results = []
    last = far[0]
    for step in range(count):
        sums, came = [], []
        for k, array in enumerate(arrays):
            bit = orders[k][step]
            if bit is None:
                sums.append(array)
                continue
            dim = left[k].index(bit)
            left[k].remove(bit)
            sent = lax.index_in_dim(array, 1, dim, keepdims=False).astype(bf16)
            kept = lax.index_in_dim(array, 0, dim, keepdims=False).astype(f32)
            came.append(from_partner(sent, "seq", 1 << bit))
            sums.append(kept + came[-1].astype(f32))
        if step < len(beside):
            result, zeros = beside[step](last, sums[0].shape, results)
            results.append(result)
            if zeros is not None:
                sums[0] = sums[0] + zeros
        if step == 1:
            total = third[0].astype(f32)
            for block in far:
                total = total + block.astype(f32)
            shape = third.shape[3:]
            sums.append(total + zero_of(came[0], shape) + zero_of(came[1], shape))
        arrays, last = sums, came[0]
    return arrays, results


def cut_in_three(size, unit):
    third = round(0.25 * size / unit) * unit
    first = (size - third + unit) // (2 * unit) * unit
    return first, size - third


def tp_masks():
    return range(1, lax.axis_size("tp"))


def over_cores(array):
    return jnp.concatenate([array] + [from_partner(array, "tp", mask) for mask in tp_masks()], axis=-1)


def lanes_by_index(array):
    count = lax.axis_size("tp")
    pieces = jnp.split(array, count, axis=-1)
    me = lax.axis_index("tp")
    step = 1
    while step < count:
        flipped = [pieces[i ^ step] for i in range(count)]
        pieces = [jnp.where(me & step == 0, a, b) for a, b in zip(pieces, flipped)]
        step *= 2
    return jnp.concatenate(pieces, axis=-1)


def merged(group):
    tops, totals, weighted, targets = (jnp.stack([one[i] for one in group]) for i in range(4))
    top = jnp.max(tops, axis=0)
    shares = jnp.exp(tops - top)
    return jnp.stack(
        [
            top,
            jnp.sum(shares * totals, axis=0),
            jnp.sum(shares * weighted, axis=0),
            jnp.sum(targets, axis=0),
        ]
    )


def in_parts(values):
    high = lax.reduce_precision(values, 8, 7)
    middle = lax.reduce_precision(values - high, 8, 7)
    return high, middle, values - high - middle


def dot(left, right, on_left, on_right, precision=None):
    return lax.dot_general(
        left,
        right,
        (((on_left,), (on_right,)), ((), ())),
        precision=precision,
        preferred_element_type=f32,
    )


def logits_kernel(where, ids, scale, gain, *refs):
    *pieces, head, out, stats, all_features = refs
    step = pl.program_id(0)
    tile = head.shape[0]
    blocks, _, lanes = pieces[0].shape
    features = all_features.shape[0] // blocks

    @pl.when(step == 0)
    def _():
        for device in range(blocks):
            for side in range(2):
                done = 0
                columns = slice(side * lanes, (side + 1) * lanes)
                for piece in pieces[3 * side : 3 * side + 3]:
                    rows = min(piece.shape[1], features - done)
                    values = piece[where[0] ^ device][:rows].astype(f32) * scale[:, columns]
                    values = values * gain[done : done + rows, device : device + 1]
                    start = device * features + done
                    all_features[start : start + rows, columns] = values.astype(bf16)
                    done += rows
        stats[...] = jnp.zeros_like(stats)
        stats[0:1, :] = jnp.full((1, stats.shape[1]), -jnp.inf, f32)

    logits = jnp.dot(head[...], all_features[...], preferred_element_type=f32)
    out[...] = logits
    entries = lax.broadcasted_iota(i32, logits.shape, 0) + (where[1] + step * tile)
    before = stats[0:1, :]
    top = jnp.maximum(before, jnp.max(logits, axis=0, keepdims=True))
    shrink = jnp.exp(before - top)
    expd = jnp.exp(logits - top)
    stats[0:1, :] = top
    stats[1:2, :] = stats[1:2, :] * shrink + jnp.sum(expd, axis=0, keepdims=True)
    stats[2:3, :] = stats[2:3, :] * shrink + jnp.sum(expd * logits, axis=0, keepdims=True)
    stats[3:4, :] = stats[3:4, :] + jnp.sum(
        jnp.where(entries == ids[...], logits, 0.0), axis=0, keepdims=True
    )


def head_logits(where, ids, scale, gain, pieces, head):
    vocab, tokens = head.shape[0], ids.shape[1]
    tile = 512
    gain = gain.reshape(pieces[0].shape[0], -1).T
    whole = lambda array: pl.BlockSpec(array.shape, lambda i, w: (0,) * array.ndim)
    return pl.pallas_call(
        logits_kernel,
        grid_spec=pltpu.PrefetchScalarGridSpec(
            num_scalar_prefetch=1,
            grid=(vocab // tile,),
            in_specs=[
                whole(ids),
                whole(scale),
                whole(gain),
                *[whole(piece) for piece in pieces],
                pl.BlockSpec((tile, D), lambda i, w: (i, 0)),
            ],
            out_specs=[
                pl.BlockSpec((tile, tokens), lambda i, w: (i, 0)),
                pl.BlockSpec((8, tokens), lambda i, w: (0, 0)),
                pl.BlockSpec((D, tokens), lambda i, w: (0, 0)),
            ],
        ),
        out_shape=[
            jax.ShapeDtypeStruct((vocab, tokens), f32),
            jax.ShapeDtypeStruct((8, tokens), f32),
            jax.ShapeDtypeStruct((D, tokens), bf16),
        ],
        compiler_params=pltpu.CompilerParams(vmem_limit_bytes=44 << 20),
        cost_estimate=pl.CostEstimate(
            flops=2 * vocab * D * tokens,
            bytes_accessed=2 * vocab * D + 4 * D * tokens,
            transcendentals=vocab * tokens,
        ),
    )(where, ids, scale, gain, *pieces, head)


def dfinal_kernel(where, ids, rows, logits, head, kept, sent, plain, turned):
    step = pl.program_id(0)
    vocab, tokens = logits.shape
    lanes = kept.shape[3]

    @pl.when(step == 0)
    def _():
        top, share, coef = (rows[i : i + 1, :] for i in range(3))
        tile = 256
        for start in range(0, vocab, tile):
            probs = jnp.exp(logits[start : start + tile, :] - top) * share
            entries = lax.broadcasted_iota(i32, probs.shape, 0) + (where[1] + start)
            dlogits = coef * (probs - (entries == ids[...]).astype(f32))
            plain[start : start + tile, :] = dlogits.astype(bf16)
            turned[:, start : start + tile] = dlogits.astype(bf16).T

    product = jnp.dot(turned[...], head[...], preferred_element_type=f32)
    mine, other = product[:lanes].T, product[lanes:].astype(bf16).T
    half = mine.shape[0] // 2
    flip = where[0] & 1
    for piece in range(2):
        kept[0, piece ^ flip] = mine[piece * half : (piece + 1) * half]
        sent[0, piece ^ flip] = other[piece * half : (piece + 1) * half]


def head_back(where, ids, rows, logits, head, blocks):
    vocab, tokens = logits.shape
    features = D // blocks
    lanes = tokens // 2
    pairs = blocks // 2
    whole = lambda array: pl.BlockSpec(array.shape, lambda i, w: (0,) * array.ndim)
    place = lambda i, w: (i ^ (w[0] >> 1), 0, 0, 0)
    return pl.pallas_call(
        dfinal_kernel,
        grid_spec=pltpu.PrefetchScalarGridSpec(
            num_scalar_prefetch=1,
            grid=(pairs,),
            in_specs=[
                whole(ids),
                whole(rows),
                whole(logits),
                pl.BlockSpec((vocab, 2 * features), lambda i, w: (0, i)),
            ],
            out_specs=[
                pl.BlockSpec((1, 2, features, lanes), place),
                pl.BlockSpec((1, 2, features, lanes), place),
                pl.BlockSpec((vocab, tokens), lambda i, w: (0, 0)),
            ],
            scratch_shapes=[pltpu.VMEM((tokens, vocab), bf16)],
        ),
        out_shape=[
            jax.ShapeDtypeStruct((pairs, 2, features, lanes), f32),
            jax.ShapeDtypeStruct((pairs, 2, features, lanes), bf16),
            jax.ShapeDtypeStruct((vocab, tokens), bf16),
        ],
        compiler_params=pltpu.CompilerParams(vmem_limit_bytes=32 << 20),
        cost_estimate=pl.CostEstimate(
            flops=2 * vocab * D * tokens,
            bytes_accessed=2 * vocab * D + 4 * D * tokens,
            transcendentals=vocab * tokens,
        ),
    )(where, ids, rows, logits, head)


def grad_head_kernel(left, features, *refs):
    out, zeros = refs[-2:]
    out[...] = lax.dot_general(
        left[...], features[...], (((1,), (1,)), ((), ())), preferred_element_type=f32
    ).astype(bf16)

    @pl.when((pl.program_id(0) == 0) & (pl.program_id(1) == 0))
    def _():
        zeros[...] = jnp.zeros_like(zeros)


def grad_head_rows(left, features, start, count, later_than, shape, before):
    vocab, tokens = left.shape
    rows, tile = 256, 1792
    given = (later_than,) if before is None else (later_than, before)
    return pl.pallas_call(
        grad_head_kernel,
        grid=(D // tile, count),
        in_specs=[
            pl.BlockSpec((rows, tokens), lambda i, j: (start + j, 0)),
            pl.BlockSpec((tile, tokens), lambda i, j: (i, 0)),
            *[pl.BlockSpec(memory_space=pl.ANY) for _ in given],
        ],
        out_specs=[
            pl.BlockSpec((rows, tile), lambda i, j: (start + j, i)),
            pl.BlockSpec(shape, lambda i, j: (0,) * len(shape)),
        ],
        out_shape=[
            jax.ShapeDtypeStruct((vocab, D), bf16),
            jax.ShapeDtypeStruct(shape, f32),
        ],
        input_output_aliases={3: 0} if before is not None else {},
        compiler_params=pltpu.CompilerParams(vmem_limit_bytes=20 << 20),
        cost_estimate=pl.CostEstimate(
            flops=2 * count * rows * D * tokens,
            bytes_accessed=2 * count * rows * D + 2 * D * tokens,
            transcendentals=0,
        ),
    )(left, features, *given)


def plain_logits(where, ids, scale, gain, pieces, head):
    blocks, _, lanes = pieces[0].shape
    features = D // blocks
    sides = []
    for i in range(0, len(pieces), 3):
        side = jnp.concatenate(pieces[i : i + 3], axis=1)[:, :features]
        sides.append(side[where[0] ^ jnp.arange(blocks)].reshape(D, lanes))
    all_features = jnp.concatenate(sides, axis=1).astype(f32)
    all_features = (all_features * scale * gain[:, None]).astype(bf16)
    logits = dot(head, all_features, 1, 0)
    top = jnp.max(logits, axis=0)
    expd = jnp.exp(logits - top)
    onehot = (jnp.arange(head.shape[0])[:, None] + where[1]) == ids
    stats = [
        top,
        jnp.sum(expd, axis=0),
        jnp.sum(expd * logits, axis=0),
        jnp.sum(jnp.where(onehot, logits, 0.0), axis=0),
    ]
    return logits, jnp.stack(stats), all_features


def plain_back(where, ids, rows, logits, head, blocks):
    top, share, coef = rows[0], rows[1], rows[2]
    lanes = logits.shape[1] // lax.axis_size("tp")
    onehot = (jnp.arange(head.shape[0])[:, None] + where[1]) == ids
    dlogits = coef * (jnp.exp(logits - top) * share - onehot.astype(f32))
    dlogits = dlogits.astype(bf16)
    product = dot(head, dlogits, 0, 0).reshape(blocks, D // blocks, -1)
    product = product[where[0] ^ jnp.arange(blocks)]
    return product[..., :lanes], product[..., lanes:].astype(bf16), dlogits


def shards(
    prev_hidden,
    token_embed,
    gain_hidden,
    gain_embed,
    gain_final,
    proj_hidden,
    proj_embed,
    head,
    target_ids,
    valid,
    rest_count,
):
    blocks, cores = lax.axis_size("seq"), lax.axis_size("tp")
    me = lax.axis_index("seq")
    rows, width = prev_hidden.shape
    features = proj_hidden.shape[1]
    tokens = rows * blocks
    lanes = tokens // cores

    prev_f = prev_hidden.astype(f32)
    embed_f = token_embed.astype(f32)
    sums = lax.psum(
        jnp.stack([jnp.sum(prev_f * prev_f, axis=-1), jnp.sum(embed_f * embed_f, axis=-1)]), "tp"
    )
    scales = lax.rsqrt(sums / D + epsilon)
    scale_prev, scale_embed = scales[0][:, None], scales[1][:, None]
    normed_prev = (prev_f * scale_prev * gain_hidden).astype(bf16)
    normed_embed = (embed_f * scale_embed * gain_embed).astype(bf16)
    main = round(0.75 * width / 128) * 128
    rest = width - main
    first, second, third, ids_here, valid_here, gain_here = lax.optimization_barrier(
        (
            normed_prev[:, :main],
            normed_embed[:, :main],
            jnp.concatenate([normed_prev[:, main:], normed_embed[:, main:]], axis=1),
            target_ids,
            valid,
            gain_final,
        )
    )
    facts = jnp.stack([ids_here // 256, ids_here % 256, valid_here]).astype(bf16)
    facts = dot(jnp.eye(rows, dtype=bf16), jnp.pad(facts, ((0, 5), (0, 0))), 1, 1).astype(bf16)
    gain_parts = jnp.stack(in_parts(gain_here)).astype(bf16).reshape(rows, -1)
    gain_columns = gain_parts.shape[1]
    facts = jnp.concatenate([facts, gain_parts], axis=1)
    facts = jnp.pad(facts, ((0, 0), (0, 128 - facts.shape[1])))

    first, second, third = gather(first, second, jnp.concatenate([third, facts], axis=1), True)
    first, second = first.reshape(tokens, main), second.reshape(tokens, main)
    third = third.reshape(tokens, 2 * rest + 128)

    row = lax.broadcasted_iota(i32, (tokens, 1), 0)
    position = (me ^ (row // rows)) * rows + row % rows
    column = lax.broadcasted_iota(i32, (1, tokens), 1)
    order_prev = position == column
    order_embed = position - 1 == column

    from_prev = dot(proj_hidden[:main], first, 0, 1) + dot(proj_hidden[main:], third[:, :rest], 0, 1)
    from_embed = dot(proj_embed[:main], second, 0, 1) + dot(
        proj_embed[main:], third[:, rest : 2 * rest], 0, 1
    )
    facts_all = third[:, 2 * rest :]
    facts_prev = dot(facts_all, order_prev.astype(bf16), 0, 0)
    partial_value = dot(
        jnp.concatenate([from_prev, from_embed], axis=1),
        jnp.concatenate([order_prev, order_embed], axis=0).astype(f32),
        1,
        0,
        lax.Precision.HIGHEST,
    )
    gain_all = facts_all[:, 8 : 8 + gain_columns].reshape(blocks, 3, features).astype(f32)
    gain_all = gain_all[:, 0] + gain_all[:, 1] + gain_all[:, 2]
    block = jnp.arange(blocks)
    gain_all = dot(
        ((me ^ block)[:, None] == block[None, :]).astype(f32), gain_all, 0, 0, lax.Precision.HIGHEST
    ).reshape(D)
    ids_all = (facts_prev[0:1] * 256 + facts_prev[1:2]).astype(i32)
    valid_all = facts_prev[2]
    core = lax.axis_index("tp")
    cut_of = lambda mask: lax.dynamic_slice_in_dim(partial_value, (core ^ mask) * lanes, lanes, 1)
    mixed_f = cut_of(0)
    for mask in tp_masks():
        mixed_f = mixed_f + from_partner(cut_of(mask), "tp", mask)
    mixed_f = mixed_f.astype(bf16).astype(f32)
    mixed = mixed_f.astype(bf16)
    square_parts = jnp.stack(in_parts(jnp.sum(mixed_f * mixed_f, axis=0))).astype(bf16)
    square_parts = jnp.pad(square_parts, ((0, 13), (0, 0)))
    one, two = cut_in_three(features, 16)
    pieces = gather(
        mixed[:one], mixed[one:two], jnp.concatenate([mixed[two:], square_parts], axis=0)
    )
    pieces = list(pieces)
    for mask in tp_masks():
        pieces = pieces + [from_partner(piece, "tp", mask) for piece in pieces[:3]]
    squares = [
        jnp.sum(piece[:, features - two :][:, :3].astype(f32), axis=(0, 1)) for piece in pieces[2::3]
    ]
    scale_own = lax.rsqrt(squares[0] / D + epsilon)
    scale_final = lax.rsqrt(jnp.concatenate(squares) / D + epsilon)

    vocab_rows = head.shape[0]
    where = jnp.stack([me, lax.axis_index(("seq", "tp")) * vocab_rows]).astype(i32)
    ids = lanes_by_index(ids_all)
    valid_lanes = lanes_by_index(valid_all)
    fits = cores == 2 and lanes % 128 == 0 and vocab_rows % 2048 == 0 and 2 * features % 128 == 0
    forward = head_logits if fits else plain_logits
    logits, stats, final_all = forward(where, ids, scale_final[None, :], gain_all, pieces, head)
    stats = stats[:4]
    for step in range(0, bits_of("seq"), 2):
        masks = [k << step for k in range(1, min(4, blocks >> step))]
        stats = merged([stats] + [from_partner(stats, "seq", mask) for mask in masks])
    stats = lanes_by_index(stats)
    stats = merged([stats] + [from_partner(stats, "tp", mask) for mask in tp_masks()])
    row_top, row_total, row_weighted, target_logit = lanes_by_index(stats)
    count = jnp.sum(valid_all) + rest_count[0].astype(f32)
    coef = loss_scale * valid_lanes / count
    row_values = jnp.stack([row_top, 1.0 / row_total, coef])
    row_values = jnp.pad(row_values, ((0, 5), (0, 0)))
    back = head_back if fits else plain_back
    kept, sent, dlogits = back(where, ids, row_values, logits, head, blocks)
    dfinal = kept.reshape(blocks, features, lanes)
    for mask in tp_masks():
        piece = sent[..., (mask - 1) * lanes : mask * lanes]
        from_core = from_partner(piece, "tp", mask)
        dfinal = dfinal + from_core.astype(f32).reshape(dfinal.shape)

    def grad_head_piece(start, count, tied):
        def work(last, shape, results):
            if not fits:
                return dot(dlogits, final_all, 1, 1).astype(bf16), None
            before = results[-1] if results else None
            shape = shape if tied else (8, 128)
            later_than = last if tied else from_core
            out, zeros = grad_head_rows(dlogits, final_all, start, count, later_than, shape, before)
            return out, (zeros if tied else None)

        return work

    quarter = vocab_rows // 1024
    early = [grad_head_piece(0, quarter, False)]
    if fits:
        early.append(grad_head_piece(quarter, quarter // 2, True))
    ahead = quarter + quarter // 2
    behind = vocab_rows // 256 - ahead - quarter
    dfinal, results = scatter([dfinal[:, :one], dfinal[:, one:two], dfinal[:, two:]], early)
    dfinal = jnp.concatenate(dfinal, axis=0)

    total_dot = (coef * (row_weighted / row_total - target_logit))[:lanes] / scale_own
    dmixed = (
        scale_own * (dfinal * gain_final[:, None]) - mixed_f * (scale_own**3 * (total_dot / D))
    ).astype(bf16)
    dmixed = lanes_by_index(over_cores(dmixed))
    dmixed_prev = dot(dmixed, order_prev.astype(bf16), 1, 1).astype(bf16)
    dmixed_embed = dot(dmixed, order_embed.astype(bf16), 1, 1).astype(bf16)
    back_prev = dot(dmixed_prev, proj_hidden, 0, 1).reshape(blocks, rows, width)
    back_embed = dot(dmixed_embed, proj_embed, 0, 1).reshape(blocks, rows, width)

    def grad_head_end(start, count):
        def work(last, shape, before):
            grad_head = before[-1] if before else results[-1]
            if not fits:
                return grad_head, None
            return grad_head_rows(dlogits, final_all, start, count, last, shape, grad_head)

        return work

    def grad_proj(rows_in, rows_rest, back):
        rows_all = jnp.concatenate([rows_in, rows_rest], axis=1)
        return dot(rows_all, back, 0, 1).astype(bf16)

    (one, two, three), ends = scatter(
        [
            back_prev[..., :main],
            back_embed[..., :main],
            jnp.concatenate([back_prev[..., main:], back_embed[..., main:]], axis=-1),
        ],
        [grad_head_end(ahead, behind), grad_head_end(ahead + behind, quarter)],
    )
    grad_head = ends[-1]
    grad_proj_hidden = grad_proj(first, third[:, :rest], dmixed_prev)
    grad_proj_embed = grad_proj(second, third[:, rest : 2 * rest], dmixed_embed)
    grad_prev = jnp.concatenate([one, three[:, :rest]], axis=1) * gain_hidden
    grad_embed = jnp.concatenate([two, three[:, rest:]], axis=1) * gain_embed
    dots = lax.psum(
        jnp.stack([jnp.sum(grad_prev * prev_f, axis=-1), jnp.sum(grad_embed * embed_f, axis=-1)]),
        "tp",
    )
    grad_prev_hidden = (
        scale_prev * grad_prev - prev_f * (scale_prev**3 * (dots[0] / D)[:, None])
    ).astype(bf16)
    grad_token_embed = (
        scale_embed * grad_embed - embed_f * (scale_embed**3 * (dots[1] / D)[:, None])
    ).astype(bf16)
    return (grad_prev_hidden, grad_token_embed, grad_proj_hidden, grad_proj_embed, grad_head)


def solution(mesh):
    return jax.shard_map(
        shards,
        mesh=mesh,
        in_specs=(
            P("seq", "tp"),
            P("seq", "tp"),
            P("tp"),
            P("tp"),
            P("seq"),
            P("tp", "seq"),
            P("tp", "seq"),
            P(("seq", "tp"), None),
            P("seq"),
            P("seq"),
            P(),
        ),
        out_specs=(
            P("seq", "tp"),
            P("seq", "tp"),
            P("tp", "seq"),
            P("tp", "seq"),
            P(("seq", "tp"), None),
        ),
        check_vma=False,
    )
```

```python
import jax
import jax.numpy as jnp
from jax import lax
from jax.experimental import pallas as pl
from jax.experimental.pallas import tpu as pltpu
from jax.sharding import PartitionSpec as P

D = 7168


loss_scale = 4096.0
epsilon = 1e-06

f32 = jnp.float32
bf16 = jnp.bfloat16
i32 = jnp.int32


def from_partner(array, axis, mask):
    size = lax.axis_size(axis)
    return lax.ppermute(array, axis, [(i, i ^ mask) for i in range(size)])


def bits_of(axis):
    return lax.axis_size(axis).bit_length() - 1


def zero_of(array, shape):
    array = array[(0,) * (array.ndim - len(shape))] if array.ndim > len(shape) else array
    array = array[tuple(slice(0, size) for size in shape[len(shape) - array.ndim :])]
    return array * 0


def in_order(array, order):
    count = len(order)
    dims = [count - 1 - order.index(bit) for bit in reversed(range(count))]
    array = array.transpose(dims + list(range(count, array.ndim)))
    return array.reshape((1 << count,) + array.shape[count:])


def gather_alone(array, order):
    for bit in order:
        array = jnp.stack([array, from_partner(array, "seq", 1 << bit)])
    return in_order(array, order)


def gather(first, second, third):
    high = list(reversed(range(2, bits_of("seq"))))
    third_shape = third.shape
    came = []
    for bit in high:
        came = [from_partner(first, "seq", 1 << bit), from_partner(second, "seq", 1 << bit)]
        if bit == high[0]:
            third = third + zero_of(came[0], third.shape) + zero_of(came[1], third.shape)
        first, second = jnp.stack([first, came[0]]), jnp.stack([second, came[1]])
    for bit in (0, 1):
        ends = [from_partner(first, "seq", 2 >> bit), from_partner(second, "seq", 1 << bit)]
        first, second = jnp.stack([first, ends[0]]), jnp.stack([second, ends[1]])
        third = jnp.stack([third, from_partner(third, "seq", 1 << bit)])
    for block in came:
        third = third + zero_of(block, third_shape)
    far = range(1, 1 << len(high))
    third = jnp.stack([third] + [from_partner(third, "seq", place << 2) for place in far])
    third = third.reshape((-1,) + third_shape)
    return in_order(first, high + [1, 0]), in_order(second, high + [0, 1]), third


def scatter(arrays, beside=()):
    count = bits_of("seq")
    low, high = [0, 1], list(range(2, count))
    third = arrays[2].reshape((1 << len(high), 2, 2) + arrays[2].shape[1:])
    far = [
        from_partner(third[place].astype(bf16), "seq", place << 2)
        for place in range(1, 1 << len(high))
    ]
    arrays = [array.reshape((2,) * count + array.shape[1:]) for array in arrays[:2]]
    orders = [low + high, low[::-1] + high, [None, None, 1, 0] + [None] * len(high[2:])]
    left = [list(reversed(range(count))), list(reversed(range(count))), [1, 0]]
    results = []
    last = far[0]
    for step in range(count):
        sums, came = [], []
        for k, array in enumerate(arrays):
            bit = orders[k][step]
            if bit is None:
                sums.append(array)
                continue
            dim = left[k].index(bit)
            left[k].remove(bit)
            sent = lax.index_in_dim(array, 1, dim, keepdims=False).astype(bf16)
            kept = lax.index_in_dim(array, 0, dim, keepdims=False).astype(f32)
            came.append(from_partner(sent, "seq", 1 << bit))
            sums.append(kept + came[-1].astype(f32))
        if step < len(beside):
            result, zeros = beside[step](last, sums[0].shape, results)
            results.append(result)
            if zeros is not None:
                sums[0] = sums[0] + zeros
        if step == 1:
            total = third[0].astype(f32)
            for block in far:
                total = total + block.astype(f32)
            shape = third.shape[3:]
            sums.append(total + zero_of(came[0], shape) + zero_of(came[1], shape))
        arrays, last = sums, came[0]
    return arrays, results


def cut_in_three(size, unit):
    third = round(0.25 * size / unit) * unit
    first = (size - third + unit) // (2 * unit) * unit
    return first, size - third


def tp_masks():
    return range(1, lax.axis_size("tp"))


def over_cores(array):
    return jnp.concatenate([array] + [from_partner(array, "tp", mask) for mask in tp_masks()], axis=-1)


def lanes_by_index(array):
    count = lax.axis_size("tp")
    pieces = jnp.split(array, count, axis=-1)
    me = lax.axis_index("tp")
    step = 1
    while step < count:
        flipped = [pieces[i ^ step] for i in range(count)]
        pieces = [jnp.where(me & step == 0, a, b) for a, b in zip(pieces, flipped)]
        step *= 2
    return jnp.concatenate(pieces, axis=-1)


def merged(group):
    tops, totals, weighted, targets = (jnp.stack([one[i] for one in group]) for i in range(4))
    top = jnp.max(tops, axis=0)
    shares = jnp.exp(tops - top)
    return jnp.stack(
        [
            top,
            jnp.sum(shares * totals, axis=0),
            jnp.sum(shares * weighted, axis=0),
            jnp.sum(targets, axis=0),
        ]
    )


def in_parts(values):
    high = lax.reduce_precision(values, 8, 7)
    middle = lax.reduce_precision(values - high, 8, 7)
    return high, middle, values - high - middle


def dot(left, right, on_left, on_right, precision=None):
    return lax.dot_general(
        left,
        right,
        (((on_left,), (on_right,)), ((), ())),
        precision=precision,
        preferred_element_type=f32,
    )


def logits_kernel(where, ids, scale, gain, *refs):
    *pieces, head, out, stats, all_features = refs
    step = pl.program_id(0)
    tile = head.shape[0]
    blocks, _, lanes = pieces[0].shape
    features = all_features.shape[0] // blocks

    @pl.when(step == 0)
    def _():
        for device in range(blocks):
            for side in range(2):
                done = 0
                columns = slice(side * lanes, (side + 1) * lanes)
                for piece in pieces[3 * side : 3 * side + 3]:
                    rows = min(piece.shape[1], features - done)
                    values = piece[where[0] ^ device][:rows].astype(f32) * scale[:, columns]
                    values = values * gain[done : done + rows, device : device + 1]
                    start = device * features + done
                    all_features[start : start + rows, columns] = values.astype(bf16)
                    done += rows
        stats[...] = jnp.zeros_like(stats)
        stats[0:1, :] = jnp.full((1, stats.shape[1]), -jnp.inf, f32)

    logits = jnp.dot(head[...], all_features[...], preferred_element_type=f32)
    out[...] = logits
    entries = lax.broadcasted_iota(i32, logits.shape, 0) + (where[1] + step * tile)
    before = stats[0:1, :]
    top = jnp.maximum(before, jnp.max(logits, axis=0, keepdims=True))
    shrink = jnp.exp(before - top)
    expd = jnp.exp(logits - top)
    stats[0:1, :] = top
    stats[1:2, :] = stats[1:2, :] * shrink + jnp.sum(expd, axis=0, keepdims=True)
    stats[2:3, :] = stats[2:3, :] * shrink + jnp.sum(expd * logits, axis=0, keepdims=True)
    stats[3:4, :] = stats[3:4, :] + jnp.sum(
        jnp.where(entries == ids[...], logits, 0.0), axis=0, keepdims=True
    )


def head_logits(where, ids, scale, gain, pieces, head):
    vocab, tokens = head.shape[0], ids.shape[1]
    tile = 512
    gain = gain.reshape(pieces[0].shape[0], -1).T
    whole = lambda array: pl.BlockSpec(array.shape, lambda i, w: (0,) * array.ndim)
    return pl.pallas_call(
        logits_kernel,
        grid_spec=pltpu.PrefetchScalarGridSpec(
            num_scalar_prefetch=1,
            grid=(vocab // tile,),
            in_specs=[
                whole(ids),
                whole(scale),
                whole(gain),
                *[whole(piece) for piece in pieces],
                pl.BlockSpec((tile, D), lambda i, w: (i, 0)),
            ],
            out_specs=[
                pl.BlockSpec((tile, tokens), lambda i, w: (i, 0)),
                pl.BlockSpec((8, tokens), lambda i, w: (0, 0)),
                pl.BlockSpec((D, tokens), lambda i, w: (0, 0)),
            ],
        ),
        out_shape=[
            jax.ShapeDtypeStruct((vocab, tokens), f32),
            jax.ShapeDtypeStruct((8, tokens), f32),
            jax.ShapeDtypeStruct((D, tokens), bf16),
        ],
        compiler_params=pltpu.CompilerParams(vmem_limit_bytes=44 << 20),
        cost_estimate=pl.CostEstimate(
            flops=2 * vocab * D * tokens,
            bytes_accessed=2 * vocab * D + 4 * D * tokens,
            transcendentals=vocab * tokens,
        ),
    )(where, ids, scale, gain, *pieces, head)


def dfinal_kernel(where, ids, rows, logits, head, kept, sent, plain, turned):
    step = pl.program_id(0)
    vocab, tokens = logits.shape
    lanes = kept.shape[3]

    @pl.when(step == 0)
    def _():
        top, share, coef = (rows[i : i + 1, :] for i in range(3))
        tile = 256
        for start in range(0, vocab, tile):
            probs = jnp.exp(logits[start : start + tile, :] - top) * share
            entries = lax.broadcasted_iota(i32, probs.shape, 0) + (where[1] + start)
            dlogits = coef * (probs - (entries == ids[...]).astype(f32))
            plain[start : start + tile, :] = dlogits.astype(bf16)
            turned[:, start : start + tile] = dlogits.astype(bf16).T

    product = jnp.dot(turned[...], head[...], preferred_element_type=f32)
    mine, other = product[:lanes].T, product[lanes:].astype(bf16).T
    half = mine.shape[0] // 2
    flip = where[0] & 1
    for piece in range(2):
        kept[0, piece ^ flip] = mine[piece * half : (piece + 1) * half]
        sent[0, piece ^ flip] = other[piece * half : (piece + 1) * half]


def head_back(where, ids, rows, logits, head, blocks):
    vocab, tokens = logits.shape
    features = D // blocks
    lanes = tokens // 2
    pairs = blocks // 2
    whole = lambda array: pl.BlockSpec(array.shape, lambda i, w: (0,) * array.ndim)
    place = lambda i, w: (i ^ (w[0] >> 1), 0, 0, 0)
    return pl.pallas_call(
        dfinal_kernel,
        grid_spec=pltpu.PrefetchScalarGridSpec(
            num_scalar_prefetch=1,
            grid=(pairs,),
            in_specs=[
                whole(ids),
                whole(rows),
                whole(logits),
                pl.BlockSpec((vocab, 2 * features), lambda i, w: (0, i)),
            ],
            out_specs=[
                pl.BlockSpec((1, 2, features, lanes), place),
                pl.BlockSpec((1, 2, features, lanes), place),
                pl.BlockSpec((vocab, tokens), lambda i, w: (0, 0)),
            ],
            scratch_shapes=[pltpu.VMEM((tokens, vocab), bf16)],
        ),
        out_shape=[
            jax.ShapeDtypeStruct((pairs, 2, features, lanes), f32),
            jax.ShapeDtypeStruct((pairs, 2, features, lanes), bf16),
            jax.ShapeDtypeStruct((vocab, tokens), bf16),
        ],
        compiler_params=pltpu.CompilerParams(vmem_limit_bytes=32 << 20),
        cost_estimate=pl.CostEstimate(
            flops=2 * vocab * D * tokens,
            bytes_accessed=2 * vocab * D + 4 * D * tokens,
            transcendentals=vocab * tokens,
        ),
    )(where, ids, rows, logits, head)


def grad_head_kernel(left, features, *refs):
    out, zeros = refs[-2:]
    out[...] = lax.dot_general(
        left[...], features[...], (((1,), (1,)), ((), ())), preferred_element_type=f32
    ).astype(bf16)

    @pl.when((pl.program_id(0) == 0) & (pl.program_id(1) == 0))
    def _():
        zeros[...] = jnp.zeros_like(zeros)


def grad_head_rows(left, features, start, count, later_than, shape, before):
    vocab, tokens = left.shape
    rows, tile = 256, 1792
    given = (later_than,) if before is None else (later_than, before)
    return pl.pallas_call(
        grad_head_kernel,
        grid=(D // tile, count),
        in_specs=[
            pl.BlockSpec((rows, tokens), lambda i, j: (start + j, 0)),
            pl.BlockSpec((tile, tokens), lambda i, j: (i, 0)),
            *[pl.BlockSpec(memory_space=pl.ANY) for _ in given],
        ],
        out_specs=[
            pl.BlockSpec((rows, tile), lambda i, j: (start + j, i)),
            pl.BlockSpec(shape, lambda i, j: (0,) * len(shape)),
        ],
        out_shape=[
            jax.ShapeDtypeStruct((vocab, D), bf16),
            jax.ShapeDtypeStruct(shape, f32),
        ],
        input_output_aliases={3: 0} if before is not None else {},
        compiler_params=pltpu.CompilerParams(vmem_limit_bytes=20 << 20),
        cost_estimate=pl.CostEstimate(
            flops=2 * count * rows * D * tokens,
            bytes_accessed=2 * count * rows * D + 2 * D * tokens,
            transcendentals=0,
        ),
    )(left, features, *given)


def plain_logits(where, ids, scale, gain, pieces, head):
    blocks, _, lanes = pieces[0].shape
    features = D // blocks
    sides = []
    for i in range(0, len(pieces), 3):
        side = jnp.concatenate(pieces[i : i + 3], axis=1)[:, :features]
        sides.append(side[where[0] ^ jnp.arange(blocks)].reshape(D, lanes))
    all_features = jnp.concatenate(sides, axis=1).astype(f32)
    all_features = (all_features * scale * gain[:, None]).astype(bf16)
    logits = dot(head, all_features, 1, 0)
    top = jnp.max(logits, axis=0)
    expd = jnp.exp(logits - top)
    onehot = (jnp.arange(head.shape[0])[:, None] + where[1]) == ids
    stats = [
        top,
        jnp.sum(expd, axis=0),
        jnp.sum(expd * logits, axis=0),
        jnp.sum(jnp.where(onehot, logits, 0.0), axis=0),
    ]
    return logits, jnp.stack(stats), all_features


def plain_back(where, ids, rows, logits, head, blocks):
    top, share, coef = rows[0], rows[1], rows[2]
    lanes = logits.shape[1] // lax.axis_size("tp")
    onehot = (jnp.arange(head.shape[0])[:, None] + where[1]) == ids
    dlogits = coef * (jnp.exp(logits - top) * share - onehot.astype(f32))
    dlogits = dlogits.astype(bf16)
    product = dot(head, dlogits, 0, 0).reshape(blocks, D // blocks, -1)
    product = product[where[0] ^ jnp.arange(blocks)]
    return product[..., :lanes], product[..., lanes:].astype(bf16), dlogits


def shards(
    prev_hidden,
    token_embed,
    gain_hidden,
    gain_embed,
    gain_final,
    proj_hidden,
    proj_embed,
    head,
    target_ids,
    valid,
    rest_count,
):
    blocks, cores = lax.axis_size("seq"), lax.axis_size("tp")
    me = lax.axis_index("seq")
    rows, width = prev_hidden.shape
    features = proj_hidden.shape[1]
    tokens = rows * blocks
    lanes = tokens // cores

    prev_f = prev_hidden.astype(f32)
    embed_f = token_embed.astype(f32)
    sums = lax.psum(
        jnp.stack([jnp.sum(prev_f * prev_f, axis=-1), jnp.sum(embed_f * embed_f, axis=-1)]), "tp"
    )
    scales = lax.rsqrt(sums / D + epsilon)
    scale_prev, scale_embed = scales[0][:, None], scales[1][:, None]
    normed_prev = (prev_f * scale_prev * gain_hidden).astype(bf16)
    normed_embed = (embed_f * scale_embed * gain_embed).astype(bf16)
    main = round(0.75 * width / 128) * 128
    rest = width - main
    first, second, third, ids_here, valid_here, gain_here = lax.optimization_barrier(
        (
            normed_prev[:, :main],
            normed_embed[:, :main],
            jnp.concatenate([normed_prev[:, main:], normed_embed[:, main:]], axis=1),
            target_ids,
            valid,
            gain_final,
        )
    )
    facts = jnp.stack([ids_here // 256, ids_here % 256, valid_here]).astype(bf16)
    facts = dot(jnp.eye(rows, dtype=bf16), jnp.pad(facts, ((0, 5), (0, 0))), 1, 1).astype(bf16)
    gain_parts = jnp.stack(in_parts(gain_here)).astype(bf16).reshape(rows, -1)
    gain_columns = gain_parts.shape[1]
    facts = jnp.concatenate([facts, gain_parts], axis=1)
    facts = jnp.pad(facts, ((0, 0), (0, 128 - facts.shape[1])))

    high = list(reversed(range(2, bits_of("seq"))))
    first = gather_alone(first, high + [1, 0])
    second = gather_alone(second, high + [0, 1])
    third = gather_alone(jnp.concatenate([third, facts], axis=1), [0, 1] + high)
    first, second = first.reshape(tokens, main), second.reshape(tokens, main)
    third = third.reshape(tokens, 2 * rest + 128)

    row = lax.broadcasted_iota(i32, (tokens, 1), 0)
    position = (me ^ (row // rows)) * rows + row % rows
    column = lax.broadcasted_iota(i32, (1, tokens), 1)
    order_prev = position == column
    order_embed = position - 1 == column

    from_prev = dot(proj_hidden[:main], first, 0, 1) + dot(proj_hidden[main:], third[:, :rest], 0, 1)
    from_embed = dot(proj_embed[:main], second, 0, 1) + dot(
        proj_embed[main:], third[:, rest : 2 * rest], 0, 1
    )
    facts_all = third[:, 2 * rest :]
    facts_prev = dot(facts_all, order_prev.astype(bf16), 0, 0)
    partial_value = dot(
        jnp.concatenate([from_prev, from_embed], axis=1),
        jnp.concatenate([order_prev, order_embed], axis=0).astype(f32),
        1,
        0,
        lax.Precision.HIGHEST,
    )
    gain_all = facts_all[:, 8 : 8 + gain_columns].reshape(blocks, 3, features).astype(f32)
    gain_all = gain_all[:, 0] + gain_all[:, 1] + gain_all[:, 2]
    block = jnp.arange(blocks)
    gain_all = dot(
        ((me ^ block)[:, None] == block[None, :]).astype(f32), gain_all, 0, 0, lax.Precision.HIGHEST
    ).reshape(D)
    ids_all = (facts_prev[0:1] * 256 + facts_prev[1:2]).astype(i32)
    valid_all = facts_prev[2]
    core = lax.axis_index("tp")
    cut_of = lambda mask: lax.dynamic_slice_in_dim(partial_value, (core ^ mask) * lanes, lanes, 1)
    mixed_f = cut_of(0)
    for mask in tp_masks():
        mixed_f = mixed_f + from_partner(cut_of(mask), "tp", mask)
    mixed_f = mixed_f.astype(bf16).astype(f32)
    mixed = mixed_f.astype(bf16)
    square_parts = jnp.stack(in_parts(jnp.sum(mixed_f * mixed_f, axis=0))).astype(bf16)
    square_parts = jnp.pad(square_parts, ((0, 13), (0, 0)))
    one, two = cut_in_three(features, 16)
    pieces = gather(
        mixed[:one], mixed[one:two], jnp.concatenate([mixed[two:], square_parts], axis=0)
    )
    pieces = list(pieces)
    for mask in tp_masks():
        pieces = pieces + [from_partner(piece, "tp", mask) for piece in pieces[:3]]
    squares = [
        jnp.sum(piece[:, features - two :][:, :3].astype(f32), axis=(0, 1)) for piece in pieces[2::3]
    ]
    scale_own = lax.rsqrt(squares[0] / D + epsilon)
    scale_final = lax.rsqrt(jnp.concatenate(squares) / D + epsilon)

    vocab_rows = head.shape[0]
    where = jnp.stack([me, lax.axis_index(("seq", "tp")) * vocab_rows]).astype(i32)
    ids = lanes_by_index(ids_all)
    valid_lanes = lanes_by_index(valid_all)
    fits = cores == 2 and lanes % 128 == 0 and vocab_rows % 2048 == 0 and 2 * features % 128 == 0
    forward = head_logits if fits else plain_logits
    logits, stats, final_all = forward(where, ids, scale_final[None, :], gain_all, pieces, head)
    stats = stats[:4]
    for step in range(0, bits_of("seq"), 2):
        masks = [k << step for k in range(1, min(4, blocks >> step))]
        stats = merged([stats] + [from_partner(stats, "seq", mask) for mask in masks])
    stats = lanes_by_index(stats)
    stats = merged([stats] + [from_partner(stats, "tp", mask) for mask in tp_masks()])
    row_top, row_total, row_weighted, target_logit = lanes_by_index(stats)
    count = jnp.sum(valid_all) + rest_count[0].astype(f32)
    coef = loss_scale * valid_lanes / count
    row_values = jnp.stack([row_top, 1.0 / row_total, coef])
    row_values = jnp.pad(row_values, ((0, 5), (0, 0)))
    back = head_back if fits else plain_back
    kept, sent, dlogits = back(where, ids, row_values, logits, head, blocks)
    dfinal = kept.reshape(blocks, features, lanes)
    for mask in tp_masks():
        piece = sent[..., (mask - 1) * lanes : mask * lanes]
        from_core = from_partner(piece, "tp", mask)
        dfinal = dfinal + from_core.astype(f32).reshape(dfinal.shape)

    def grad_head_piece(start, count, tied):
        def work(last, shape, results):
            if not fits:
                return dot(dlogits, final_all, 1, 1).astype(bf16), None
            before = results[-1] if results else None
            shape = shape if tied else (8, 128)
            later_than = last if tied else from_core
            out, zeros = grad_head_rows(dlogits, final_all, start, count, later_than, shape, before)
            return out, (zeros if tied else None)

        return work

    quarter = vocab_rows // 1024
    early = [grad_head_piece(0, quarter, False)]
    if fits:
        early.append(grad_head_piece(quarter, quarter // 2, True))
    ahead = quarter + quarter // 2
    dfinal, results = scatter([dfinal[:, :one], dfinal[:, one:two], dfinal[:, two:]], early)
    dfinal = jnp.concatenate(dfinal, axis=0)

    total_dot = (coef * (row_weighted / row_total - target_logit))[:lanes] / scale_own
    dmixed = (
        scale_own * (dfinal * gain_final[:, None]) - mixed_f * (scale_own**3 * (total_dot / D))
    ).astype(bf16)
    dmixed = lanes_by_index(over_cores(dmixed))
    dmixed_prev = dot(dmixed, order_prev.astype(bf16), 1, 1).astype(bf16)
    dmixed_embed = dot(dmixed, order_embed.astype(bf16), 1, 1).astype(bf16)
    back_prev = dot(dmixed_prev, proj_hidden, 0, 1).reshape(blocks, rows, width)
    back_embed = dot(dmixed_embed, proj_embed, 0, 1).reshape(blocks, rows, width)

    def grad_head_end(start, count):
        def work(last, shape, before):
            grad_head = before[-1] if before else results[-1]
            if not fits:
                return grad_head, None
            return grad_head_rows(dlogits, final_all, start, count, last, shape, grad_head)

        return work

    def grad_proj(rows_in, rows_rest, back):
        rows_all = jnp.concatenate([rows_in, rows_rest], axis=1)
        return dot(rows_all, back, 0, 1).astype(bf16)

    (one, two, three), ends = scatter(
        [
            back_prev[..., :main],
            back_embed[..., :main],
            jnp.concatenate([back_prev[..., main:], back_embed[..., main:]], axis=-1),
        ],
        [
            grad_head_end(ahead, quarter),
            grad_head_end(ahead + quarter, quarter),
            grad_head_end(ahead + 2 * quarter, quarter // 2),
        ],
    )
    grad_head = ends[-1]
    grad_proj_hidden = grad_proj(first, third[:, :rest], dmixed_prev)
    grad_proj_embed = grad_proj(second, third[:, rest : 2 * rest], dmixed_embed)
    grad_prev = jnp.concatenate([one, three[:, :rest]], axis=1) * gain_hidden
    grad_embed = jnp.concatenate([two, three[:, rest:]], axis=1) * gain_embed
    dots = lax.psum(
        jnp.stack([jnp.sum(grad_prev * prev_f, axis=-1), jnp.sum(grad_embed * embed_f, axis=-1)]),
        "tp",
    )
    grad_prev_hidden = (
        scale_prev * grad_prev - prev_f * (scale_prev**3 * (dots[0] / D)[:, None])
    ).astype(bf16)
    grad_token_embed = (
        scale_embed * grad_embed - embed_f * (scale_embed**3 * (dots[1] / D)[:, None])
    ).astype(bf16)
    return (grad_prev_hidden, grad_token_embed, grad_proj_hidden, grad_proj_embed, grad_head)


def solution(mesh):
    return jax.shard_map(
        shards,
        mesh=mesh,
        in_specs=(
            P("seq", "tp"),
            P("seq", "tp"),
            P("tp"),
            P("tp"),
            P("seq"),
            P("tp", "seq"),
            P("tp", "seq"),
            P(("seq", "tp"), None),
            P("seq"),
            P("seq"),
            P(),
        ),
        out_specs=(
            P("seq", "tp"),
            P("seq", "tp"),
            P("tp", "seq"),
            P("tp", "seq"),
            P(("seq", "tp"), None),
        ),
        check_vma=False,
    )
```

```python
import jax
import jax.numpy as jnp
from jax import lax
from jax.experimental import pallas as pl
from jax.experimental.pallas import tpu as pltpu
from jax.sharding import PartitionSpec as P

D = 7168


loss_scale = 4096.0
epsilon = 1e-06

f32 = jnp.float32
bf16 = jnp.bfloat16
i32 = jnp.int32


def from_partner(array, axis, mask):
    size = lax.axis_size(axis)
    return lax.ppermute(array, axis, [(i, i ^ mask) for i in range(size)])


def bits_of(axis):
    return lax.axis_size(axis).bit_length() - 1


def zero_of(array, shape):
    array = array[(0,) * (array.ndim - len(shape))] if array.ndim > len(shape) else array
    array = array[tuple(slice(0, size) for size in shape[len(shape) - array.ndim :])]
    return array * 0


def in_order(array, order):
    count = len(order)
    dims = [count - 1 - order.index(bit) for bit in reversed(range(count))]
    array = array.transpose(dims + list(range(count, array.ndim)))
    return array.reshape((1 << count,) + array.shape[count:])


def gather_alone(array, order):
    for bit in order:
        array = jnp.stack([array, from_partner(array, "seq", 1 << bit)])
    return in_order(array, order)


def gather(first, second, third):
    high = list(reversed(range(2, bits_of("seq"))))
    third_shape = third.shape
    came = []
    for bit in high:
        came = [from_partner(first, "seq", 1 << bit), from_partner(second, "seq", 1 << bit)]
        if bit == high[0]:
            third = third + zero_of(came[0], third.shape) + zero_of(came[1], third.shape)
        first, second = jnp.stack([first, came[0]]), jnp.stack([second, came[1]])
    for bit in (0, 1):
        ends = [from_partner(first, "seq", 2 >> bit), from_partner(second, "seq", 1 << bit)]
        first, second = jnp.stack([first, ends[0]]), jnp.stack([second, ends[1]])
        third = jnp.stack([third, from_partner(third, "seq", 1 << bit)])
    for block in came:
        third = third + zero_of(block, third_shape)
    far = range(1, 1 << len(high))
    third = jnp.stack([third] + [from_partner(third, "seq", place << 2) for place in far])
    third = third.reshape((-1,) + third_shape)
    return in_order(first, high + [1, 0]), in_order(second, high + [0, 1]), third


def scatter(arrays, beside=()):
    count = bits_of("seq")
    low, high = [0, 1], list(range(2, count))
    third = arrays[2].reshape((1 << len(high), 2, 2) + arrays[2].shape[1:])
    far = [
        from_partner(third[place].astype(bf16), "seq", place << 2)
        for place in range(1, 1 << len(high))
    ]
    arrays = [array.reshape((2,) * count + array.shape[1:]) for array in arrays[:2]]
    orders = [low + high, low[::-1] + high, [None, None, 1, 0] + [None] * len(high[2:])]
    left = [list(reversed(range(count))), list(reversed(range(count))), [1, 0]]
    results = []
    last = far[0]
    for step in range(count):
        sums, came = [], []
        for k, array in enumerate(arrays):
            bit = orders[k][step]
            if bit is None:
                sums.append(array)
                continue
            dim = left[k].index(bit)
            left[k].remove(bit)
            sent = lax.index_in_dim(array, 1, dim, keepdims=False).astype(bf16)
            kept = lax.index_in_dim(array, 0, dim, keepdims=False).astype(f32)
            came.append(from_partner(sent, "seq", 1 << bit))
            sums.append(kept + came[-1].astype(f32))
        if step < len(beside):
            result, zeros = beside[step](last, sums[0].shape, results)
            results.append(result)
            if zeros is not None:
                sums[0] = sums[0] + zeros
        if step == 1:
            total = third[0].astype(f32)
            for block in far:
                total = total + block.astype(f32)
            shape = third.shape[3:]
            sums.append(total + zero_of(came[0], shape) + zero_of(came[1], shape))
        arrays, last = sums, came[0]
    return arrays, results


def cut_in_three(size, unit):
    third = round(0.25 * size / unit) * unit
    first = (size - third + unit) // (2 * unit) * unit
    return first, size - third


def tp_masks():
    return range(1, lax.axis_size("tp"))


def over_cores(array):
    return jnp.concatenate([array] + [from_partner(array, "tp", mask) for mask in tp_masks()], axis=-1)


def lanes_by_index(array):
    count = lax.axis_size("tp")
    pieces = jnp.split(array, count, axis=-1)
    me = lax.axis_index("tp")
    step = 1
    while step < count:
        flipped = [pieces[i ^ step] for i in range(count)]
        pieces = [jnp.where(me & step == 0, a, b) for a, b in zip(pieces, flipped)]
        step *= 2
    return jnp.concatenate(pieces, axis=-1)


def merged(group):
    tops, totals, weighted, targets = (jnp.stack([one[i] for one in group]) for i in range(4))
    top = jnp.max(tops, axis=0)
    shares = jnp.exp(tops - top)
    return jnp.stack(
        [
            top,
            jnp.sum(shares * totals, axis=0),
            jnp.sum(shares * weighted, axis=0),
            jnp.sum(targets, axis=0),
        ]
    )


def in_parts(values):
    high = lax.reduce_precision(values, 8, 7)
    middle = lax.reduce_precision(values - high, 8, 7)
    return high, middle, values - high - middle


def dot(left, right, on_left, on_right, precision=None):
    return lax.dot_general(
        left,
        right,
        (((on_left,), (on_right,)), ((), ())),
        precision=precision,
        preferred_element_type=f32,
    )


def logits_kernel(where, ids, scale, gain, *refs):
    *pieces, head, out, stats, all_features = refs
    step = pl.program_id(0)
    tile = head.shape[0]
    blocks, _, lanes = pieces[0].shape
    features = all_features.shape[0] // blocks

    @pl.when(step == 0)
    def _():
        for device in range(blocks):
            for side in range(2):
                done = 0
                columns = slice(side * lanes, (side + 1) * lanes)
                for piece in pieces[3 * side : 3 * side + 3]:
                    rows = min(piece.shape[1], features - done)
                    values = piece[where[0] ^ device][:rows].astype(f32) * scale[:, columns]
                    values = values * gain[done : done + rows, device : device + 1]
                    start = device * features + done
                    all_features[start : start + rows, columns] = values.astype(bf16)
                    done += rows
        stats[...] = jnp.zeros_like(stats)
        stats[0:1, :] = jnp.full((1, stats.shape[1]), -jnp.inf, f32)

    logits = jnp.dot(head[...], all_features[...], preferred_element_type=f32)
    out[...] = logits
    entries = lax.broadcasted_iota(i32, logits.shape, 0) + (where[1] + step * tile)
    before = stats[0:1, :]
    top = jnp.maximum(before, jnp.max(logits, axis=0, keepdims=True))
    shrink = jnp.exp(before - top)
    expd = jnp.exp(logits - top)
    stats[0:1, :] = top
    stats[1:2, :] = stats[1:2, :] * shrink + jnp.sum(expd, axis=0, keepdims=True)
    stats[2:3, :] = stats[2:3, :] * shrink + jnp.sum(expd * logits, axis=0, keepdims=True)
    stats[3:4, :] = stats[3:4, :] + jnp.sum(
        jnp.where(entries == ids[...], logits, 0.0), axis=0, keepdims=True
    )


def head_logits(where, ids, scale, gain, pieces, head):
    vocab, tokens = head.shape[0], ids.shape[1]
    tile = 256
    gain = gain.reshape(pieces[0].shape[0], -1).T
    whole = lambda array: pl.BlockSpec(array.shape, lambda i, w: (0,) * array.ndim)
    return pl.pallas_call(
        logits_kernel,
        grid_spec=pltpu.PrefetchScalarGridSpec(
            num_scalar_prefetch=1,
            grid=(vocab // tile,),
            in_specs=[
                whole(ids),
                whole(scale),
                whole(gain),
                *[whole(piece) for piece in pieces],
                pl.BlockSpec((tile, D), lambda i, w: (i, 0)),
            ],
            out_specs=[
                pl.BlockSpec((tile, tokens), lambda i, w: (i, 0)),
                pl.BlockSpec((8, tokens), lambda i, w: (0, 0)),
                pl.BlockSpec((D, tokens), lambda i, w: (0, 0)),
            ],
        ),
        out_shape=[
            jax.ShapeDtypeStruct((vocab, tokens), f32),
            jax.ShapeDtypeStruct((8, tokens), f32),
            jax.ShapeDtypeStruct((D, tokens), bf16),
        ],
        compiler_params=pltpu.CompilerParams(vmem_limit_bytes=44 << 20),
        cost_estimate=pl.CostEstimate(
            flops=2 * vocab * D * tokens,
            bytes_accessed=2 * vocab * D + 4 * D * tokens,
            transcendentals=vocab * tokens,
        ),
    )(where, ids, scale, gain, *pieces, head)


def dfinal_kernel(where, ids, rows, logits, head, kept, sent, plain, turned):
    step = pl.program_id(0)
    vocab, tokens = logits.shape
    lanes = kept.shape[3]

    @pl.when(step == 0)
    def _():
        top, share, coef = (rows[i : i + 1, :] for i in range(3))
        tile = 256
        for start in range(0, vocab, tile):
            probs = jnp.exp(logits[start : start + tile, :] - top) * share
            entries = lax.broadcasted_iota(i32, probs.shape, 0) + (where[1] + start)
            dlogits = coef * (probs - (entries == ids[...]).astype(f32))
            plain[start : start + tile, :] = dlogits.astype(bf16)
            turned[:, start : start + tile] = dlogits.astype(bf16).T

    product = jnp.dot(turned[...], head[...], preferred_element_type=f32)
    mine, other = product[:lanes].T, product[lanes:].astype(bf16).T
    half = mine.shape[0] // 2
    flip = where[0] & 1
    for piece in range(2):
        kept[0, piece ^ flip] = mine[piece * half : (piece + 1) * half]
        sent[0, piece ^ flip] = other[piece * half : (piece + 1) * half]


def head_back(where, ids, rows, logits, head, blocks):
    vocab, tokens = logits.shape
    features = D // blocks
    lanes = tokens // 2
    pairs = blocks // 2
    whole = lambda array: pl.BlockSpec(array.shape, lambda i, w: (0,) * array.ndim)
    place = lambda i, w: (i ^ (w[0] >> 1), 0, 0, 0)
    return pl.pallas_call(
        dfinal_kernel,
        grid_spec=pltpu.PrefetchScalarGridSpec(
            num_scalar_prefetch=1,
            grid=(pairs,),
            in_specs=[
                whole(ids),
                whole(rows),
                whole(logits),
                pl.BlockSpec((vocab, 2 * features), lambda i, w: (0, i)),
            ],
            out_specs=[
                pl.BlockSpec((1, 2, features, lanes), place),
                pl.BlockSpec((1, 2, features, lanes), place),
                pl.BlockSpec((vocab, tokens), lambda i, w: (0, 0)),
            ],
            scratch_shapes=[pltpu.VMEM((tokens, vocab), bf16)],
        ),
        out_shape=[
            jax.ShapeDtypeStruct((pairs, 2, features, lanes), f32),
            jax.ShapeDtypeStruct((pairs, 2, features, lanes), bf16),
            jax.ShapeDtypeStruct((vocab, tokens), bf16),
        ],
        compiler_params=pltpu.CompilerParams(vmem_limit_bytes=32 << 20),
        cost_estimate=pl.CostEstimate(
            flops=2 * vocab * D * tokens,
            bytes_accessed=2 * vocab * D + 4 * D * tokens,
            transcendentals=vocab * tokens,
        ),
    )(where, ids, rows, logits, head)


def grad_head_kernel(left, features, *refs):
    out, zeros = refs[-2:]
    out[...] = lax.dot_general(
        left[...], features[...], (((1,), (1,)), ((), ())), preferred_element_type=f32
    ).astype(bf16)

    @pl.when((pl.program_id(0) == 0) & (pl.program_id(1) == 0))
    def _():
        zeros[...] = jnp.zeros_like(zeros)


def grad_head_rows(left, features, start, count, later_than, shape, before):
    vocab, tokens = left.shape
    rows, tile = 256, 1792
    given = (later_than,) if before is None else (later_than, before)
    return pl.pallas_call(
        grad_head_kernel,
        grid=(D // tile, count),
        in_specs=[
            pl.BlockSpec((rows, tokens), lambda i, j: (start + j, 0)),
            pl.BlockSpec((tile, tokens), lambda i, j: (i, 0)),
            *[pl.BlockSpec(memory_space=pl.ANY) for _ in given],
        ],
        out_specs=[
            pl.BlockSpec((rows, tile), lambda i, j: (start + j, i)),
            pl.BlockSpec(shape, lambda i, j: (0,) * len(shape)),
        ],
        out_shape=[
            jax.ShapeDtypeStruct((vocab, D), bf16),
            jax.ShapeDtypeStruct(shape, f32),
        ],
        input_output_aliases={3: 0} if before is not None else {},
        compiler_params=pltpu.CompilerParams(vmem_limit_bytes=20 << 20),
        cost_estimate=pl.CostEstimate(
            flops=2 * count * rows * D * tokens,
            bytes_accessed=2 * count * rows * D + 2 * D * tokens,
            transcendentals=0,
        ),
    )(left, features, *given)


def plain_logits(where, ids, scale, gain, pieces, head):
    blocks, _, lanes = pieces[0].shape
    features = D // blocks
    sides = []
    for i in range(0, len(pieces), 3):
        side = jnp.concatenate(pieces[i : i + 3], axis=1)[:, :features]
        sides.append(side[where[0] ^ jnp.arange(blocks)].reshape(D, lanes))
    all_features = jnp.concatenate(sides, axis=1).astype(f32)
    all_features = (all_features * scale * gain[:, None]).astype(bf16)
    logits = dot(head, all_features, 1, 0)
    top = jnp.max(logits, axis=0)
    expd = jnp.exp(logits - top)
    onehot = (jnp.arange(head.shape[0])[:, None] + where[1]) == ids
    stats = [
        top,
        jnp.sum(expd, axis=0),
        jnp.sum(expd * logits, axis=0),
        jnp.sum(jnp.where(onehot, logits, 0.0), axis=0),
    ]
    return logits, jnp.stack(stats), all_features


def plain_back(where, ids, rows, logits, head, blocks):
    top, share, coef = rows[0], rows[1], rows[2]
    lanes = logits.shape[1] // lax.axis_size("tp")
    onehot = (jnp.arange(head.shape[0])[:, None] + where[1]) == ids
    dlogits = coef * (jnp.exp(logits - top) * share - onehot.astype(f32))
    dlogits = dlogits.astype(bf16)
    product = dot(head, dlogits, 0, 0).reshape(blocks, D // blocks, -1)
    product = product[where[0] ^ jnp.arange(blocks)]
    return product[..., :lanes], product[..., lanes:].astype(bf16), dlogits


def shards(
    prev_hidden,
    token_embed,
    gain_hidden,
    gain_embed,
    gain_final,
    proj_hidden,
    proj_embed,
    head,
    target_ids,
    valid,
    rest_count,
):
    blocks, cores = lax.axis_size("seq"), lax.axis_size("tp")
    me = lax.axis_index("seq")
    rows, width = prev_hidden.shape
    features = proj_hidden.shape[1]
    tokens = rows * blocks
    lanes = tokens // cores

    prev_f = prev_hidden.astype(f32)
    embed_f = token_embed.astype(f32)
    sums = lax.psum(
        jnp.stack([jnp.sum(prev_f * prev_f, axis=-1), jnp.sum(embed_f * embed_f, axis=-1)]), "tp"
    )
    scales = lax.rsqrt(sums / D + epsilon)
    scale_prev, scale_embed = scales[0][:, None], scales[1][:, None]
    normed_prev = (prev_f * scale_prev * gain_hidden).astype(bf16)
    normed_embed = (embed_f * scale_embed * gain_embed).astype(bf16)
    main = round(0.75 * width / 128) * 128
    rest = width - main
    first, second, third, ids_here, valid_here, gain_here = lax.optimization_barrier(
        (
            normed_prev[:, :main],
            normed_embed[:, :main],
            jnp.concatenate([normed_prev[:, main:], normed_embed[:, main:]], axis=1),
            target_ids,
            valid,
            gain_final,
        )
    )
    facts = jnp.stack([ids_here // 256, ids_here % 256, valid_here]).astype(bf16)
    facts = dot(jnp.eye(rows, dtype=bf16), jnp.pad(facts, ((0, 5), (0, 0))), 1, 1).astype(bf16)
    gain_parts = jnp.stack(in_parts(gain_here)).astype(bf16).reshape(rows, -1)
    gain_columns = gain_parts.shape[1]
    facts = jnp.concatenate([facts, gain_parts], axis=1)
    facts = jnp.pad(facts, ((0, 0), (0, 128 - facts.shape[1])))

    high = list(reversed(range(2, bits_of("seq"))))
    first = gather_alone(jnp.concatenate([first, facts], axis=1), high + [1, 0])
    second = gather_alone(second, high + [0, 1])
    third = gather_alone(third, [0, 1] + high)
    first, second = first.reshape(tokens, main + 128), second.reshape(tokens, main)
    first, facts_all = first[:, :main], first[:, main:]
    third = third.reshape(tokens, 2 * rest)

    row = lax.broadcasted_iota(i32, (tokens, 1), 0)
    position = (me ^ (row // rows)) * rows + row % rows
    column = lax.broadcasted_iota(i32, (1, tokens), 1)
    order_prev = position == column
    order_embed = position - 1 == column

    from_prev = dot(proj_hidden[:main], first, 0, 1) + dot(proj_hidden[main:], third[:, :rest], 0, 1)
    from_embed = dot(proj_embed[:main], second, 0, 1) + dot(
        proj_embed[main:], third[:, rest : 2 * rest], 0, 1
    )
    facts_prev = dot(facts_all, order_prev.astype(bf16), 0, 0)
    partial_value = dot(
        jnp.concatenate([from_prev, from_embed], axis=1),
        jnp.concatenate([order_prev, order_embed], axis=0).astype(f32),
        1,
        0,
        lax.Precision.HIGHEST,
    )
    gain_all = facts_all[:, 8 : 8 + gain_columns].reshape(blocks, 3, features).astype(f32)
    gain_all = gain_all[:, 0] + gain_all[:, 1] + gain_all[:, 2]
    block = jnp.arange(blocks)
    gain_all = dot(
        ((me ^ block)[:, None] == block[None, :]).astype(f32), gain_all, 0, 0, lax.Precision.HIGHEST
    ).reshape(D)
    ids_all = (facts_prev[0:1] * 256 + facts_prev[1:2]).astype(i32)
    valid_all = facts_prev[2]
    core = lax.axis_index("tp")
    cut_of = lambda mask: lax.dynamic_slice_in_dim(partial_value, (core ^ mask) * lanes, lanes, 1)
    mixed_f = cut_of(0)
    for mask in tp_masks():
        mixed_f = mixed_f + from_partner(cut_of(mask), "tp", mask)
    mixed_f = mixed_f.astype(bf16).astype(f32)
    mixed = mixed_f.astype(bf16)
    square_parts = jnp.stack(in_parts(jnp.sum(mixed_f * mixed_f, axis=0))).astype(bf16)
    square_parts = jnp.pad(square_parts, ((0, 13), (0, 0)))
    one, two = cut_in_three(features, 16)
    pieces = gather(
        mixed[:one], mixed[one:two], jnp.concatenate([mixed[two:], square_parts], axis=0)
    )
    pieces = list(pieces)
    for mask in tp_masks():
        pieces = pieces + [from_partner(piece, "tp", mask) for piece in pieces[:3]]
    squares = [
        jnp.sum(piece[:, features - two :][:, :3].astype(f32), axis=(0, 1)) for piece in pieces[2::3]
    ]
    scale_own = lax.rsqrt(squares[0] / D + epsilon)
    scale_final = lax.rsqrt(jnp.concatenate(squares) / D + epsilon)

    vocab_rows = head.shape[0]
    where = jnp.stack([me, lax.axis_index(("seq", "tp")) * vocab_rows]).astype(i32)
    ids = lanes_by_index(ids_all)
    valid_lanes = lanes_by_index(valid_all)
    fits = cores == 2 and lanes % 128 == 0 and vocab_rows % 2048 == 0 and 2 * features % 128 == 0
    forward = head_logits if fits else plain_logits
    logits, stats, final_all = forward(where, ids, scale_final[None, :], gain_all, pieces, head)
    stats = stats[:4]
    for step in range(0, bits_of("seq"), 2):
        masks = [k << step for k in range(1, min(4, blocks >> step))]
        stats = merged([stats] + [from_partner(stats, "seq", mask) for mask in masks])
    stats = lanes_by_index(stats)
    stats = merged([stats] + [from_partner(stats, "tp", mask) for mask in tp_masks()])
    row_top, row_total, row_weighted, target_logit = lanes_by_index(stats)
    count = jnp.sum(valid_all) + rest_count[0].astype(f32)
    coef = loss_scale * valid_lanes / count
    row_values = jnp.stack([row_top, 1.0 / row_total, coef])
    row_values = jnp.pad(row_values, ((0, 5), (0, 0)))
    back = head_back if fits else plain_back
    kept, sent, dlogits = back(where, ids, row_values, logits, head, blocks)
    dfinal = kept.reshape(blocks, features, lanes)
    for mask in tp_masks():
        piece = sent[..., (mask - 1) * lanes : mask * lanes]
        from_core = from_partner(piece, "tp", mask)
        dfinal = dfinal + from_core.astype(f32).reshape(dfinal.shape)

    def grad_head_piece(start, count, tied):
        def work(last, shape, results):
            if not fits:
                return dot(dlogits, final_all, 1, 1).astype(bf16), None
            before = results[-1] if results else None
            shape = shape if tied else (8, 128)
            later_than = last if tied else from_core
            out, zeros = grad_head_rows(dlogits, final_all, start, count, later_than, shape, before)
            return out, (zeros if tied else None)

        return work

    quarter = vocab_rows // 1024
    early = [grad_head_piece(0, quarter, False)]
    if fits:
        early.append(grad_head_piece(quarter, quarter // 2, True))
    ahead = quarter + quarter // 2
    dfinal, results = scatter([dfinal[:, :one], dfinal[:, one:two], dfinal[:, two:]], early)
    dfinal = jnp.concatenate(dfinal, axis=0)

    total_dot = (coef * (row_weighted / row_total - target_logit))[:lanes] / scale_own
    dmixed = (
        scale_own * (dfinal * gain_final[:, None]) - mixed_f * (scale_own**3 * (total_dot / D))
    ).astype(bf16)
    dmixed = lanes_by_index(over_cores(dmixed))
    dmixed_prev = dot(dmixed, order_prev.astype(bf16), 1, 1).astype(bf16)
    dmixed_embed = dot(dmixed, order_embed.astype(bf16), 1, 1).astype(bf16)
    back_prev = dot(dmixed_prev, proj_hidden, 0, 1).reshape(blocks, rows, width)
    back_embed = dot(dmixed_embed, proj_embed, 0, 1).reshape(blocks, rows, width)

    def grad_head_end(start, count):
        def work(last, shape, before):
            grad_head = before[-1] if before else results[-1]
            if not fits:
                return grad_head, None
            return grad_head_rows(dlogits, final_all, start, count, last, shape, grad_head)

        return work

    def grad_proj(rows_in, rows_rest, back):
        rows_all = jnp.concatenate([rows_in, rows_rest], axis=1)
        return dot(rows_all, back, 0, 1).astype(bf16)

    (one, two, three), ends = scatter(
        [
            back_prev[..., :main],
            back_embed[..., :main],
            jnp.concatenate([back_prev[..., main:], back_embed[..., main:]], axis=-1),
        ],
        [
            grad_head_end(ahead, quarter),
            grad_head_end(ahead + quarter, quarter),
            grad_head_end(ahead + 2 * quarter, quarter // 2),
        ],
    )
    grad_head = ends[-1]
    grad_proj_hidden = grad_proj(first, third[:, :rest], dmixed_prev)
    grad_proj_embed = grad_proj(second, third[:, rest : 2 * rest], dmixed_embed)
    grad_prev = jnp.concatenate([one, three[:, :rest]], axis=1) * gain_hidden
    grad_embed = jnp.concatenate([two, three[:, rest:]], axis=1) * gain_embed
    dots = lax.psum(
        jnp.stack([jnp.sum(grad_prev * prev_f, axis=-1), jnp.sum(grad_embed * embed_f, axis=-1)]),
        "tp",
    )
    grad_prev_hidden = (
        scale_prev * grad_prev - prev_f * (scale_prev**3 * (dots[0] / D)[:, None])
    ).astype(bf16)
    grad_token_embed = (
        scale_embed * grad_embed - embed_f * (scale_embed**3 * (dots[1] / D)[:, None])
    ).astype(bf16)
    return (grad_prev_hidden, grad_token_embed, grad_proj_hidden, grad_proj_embed, grad_head)


def solution(mesh):
    return jax.shard_map(
        shards,
        mesh=mesh,
        in_specs=(
            P("seq", "tp"),
            P("seq", "tp"),
            P("tp"),
            P("tp"),
            P("seq"),
            P("tp", "seq"),
            P("tp", "seq"),
            P(("seq", "tp"), None),
            P("seq"),
            P("seq"),
            P(),
        ),
        out_specs=(
            P("seq", "tp"),
            P("seq", "tp"),
            P("tp", "seq"),
            P("tp", "seq"),
            P(("seq", "tp"), None),
        ),
        check_vma=False,
    )
```
